128 devices in a mesh: fsdp: 4 (over x), heads: 8 (over z, core), tensor: 4 (over y).
Axes of the slice: x: 4, y: 4, z: 4, core: 2. Of those that a mesh axis runs over, the one named last changes fastest.
Arguments:
- hidden_in: bfloat16 [8, 4, 512, 1024], P('fsdp', 'tensor', 'heads'), may hold values from -6 to 6
- cotangent: bfloat16 [8, 4, 512, 1024], P('fsdp', 'tensor', 'heads'), may hold values from -6 to 6
- block_order: int32 [4, 2], replicated, may hold values from 0 to 7, as said below
- query_weight: bfloat16 [1024, 8, 128], P(('fsdp', 'tensor'), 'heads'), may hold values from -0.1875 to 0.1875
- keyval_weight: bfloat16 [1024, 8, 128], P(('fsdp', 'tensor'), 'heads'), may hold values from -0.1875 to 0.1875
- output_weight: bfloat16 [1024, 8, 128], P(('fsdp', 'tensor'), 'heads'), may hold values from -1.5 to 1.5
- gate_weight: bfloat16 [1024, 4608], P(('fsdp', 'heads'), 'tensor'), may hold values from -0.1875 to 0.1875
- up_weight: bfloat16 [1024, 4608], P(('fsdp', 'heads'), 'tensor'), may hold values from -0.1875 to 0.1875
- down_weight: bfloat16 [1024, 4608], P(('fsdp', 'heads'), 'tensor'), may hold values from -0.09375 to 0.09375
- attn_gain: float32 [1024], replicated, may hold values from 0.1 to 1.9
- ffn_gain: float32 [1024], replicated, may hold values from 0.1 to 1.9
- query_gain: float32 [64], replicated, may hold values from 0.1 to 1.9
- key_gain: float32 [64], replicated, may hold values from 0.1 to 1.9
Outputs:
- block_out: bfloat16 [8, 4, 512, 1024], P('fsdp', 'tensor', 'heads')
- input_grad: float32 [8, 4, 512, 1024], P('fsdp', 'tensor', 'heads')
- query_grad: float32 [1024, 8, 128], P(('fsdp', 'tensor'), 'heads')
- keyval_grad: float32 [1024, 8, 128], P(('fsdp', 'tensor'), 'heads')
- output_grad: float32 [1024, 8, 128], P(('fsdp', 'tensor'), 'heads')
- gate_grad: float32 [1024, 4608], P(('fsdp', 'heads'), 'tensor')
- up_grad: float32 [1024, 4608], P(('fsdp', 'heads'), 'tensor')
- down_grad: float32 [1024, 4608], P(('fsdp', 'heads'), 'tensor')
- attn_gain_grad: float32 [1024], replicated
- ffn_gain_grad: float32 [1024], replicated
- query_gain_grad: float32 [64], replicated
- key_gain_grad: float32 [64], replicated
The draws below stay inside these ranges and needn't reach their ends.
Inputs may be any that keep to these rules, and one draw needn't show every extreme that they name: `block_order`: row r holds the two query blocks that tensor rank r keeps: a block c of 0 to 2 n - 1 (n the tensor axis's devices) and its mirror 2 n - 1 - c, in either order; every block appears exactly once.
All inputs are finite; a program needn't handle non-finite values.
Results may differ from the reference program's by a relative error of at most 0.019.
Values may be sent and summed in bfloat16 or wider, within the bound.
No kernel may reach another device: no remote copies, remote signals or barrier semaphores. Data moves between devices by JAX's collectives and lax.ppermute only.
A program may use at most 128 MiB of HBM per device.

```python
import jax
import jax.numpy as jnp
from jax import lax

D = 1024
HQ = 16
KVH = 8
HD = 64
FF = 4608
LEN = 2048
GROUP = 2
QW = 128
TOKS = 512
BLOCK = 256
SEQS = 8
N_TENSOR = 4


def draw_block_order(key, part):
    key = jax.random.fold_in(key, 7)
    first_key, second_key = jax.random.split(key)
    pairs = jax.random.permutation(first_key, N_TENSOR)
    flips = jax.random.randint(second_key, (N_TENSOR,), 0, 2)
    mirror = 2 * N_TENSOR - 1 - pairs
    leading = jnp.where(flips == 1, mirror, pairs)
    trailing = jnp.where(flips == 1, pairs, mirror)
    return jnp.stack([leading, trailing], axis=1).astype(jnp.int32)


def block_levels(stream_key, extent, shards, low, high):
    factor_of, own = 1.0, jax.random.fold_in(stream_key, 6)
    for axis_at, blocks in shards:
        heights = jnp.exp(jax.random.uniform(jax.random.fold_in(own, axis_at), (blocks,), jnp.float32, low / len(shards), high / len(shards)))
        factor_of = factor_of * jnp.repeat(heights, extent[axis_at] // blocks).reshape([-1 if axis == axis_at else 1 for axis in range(len(extent))])
    return factor_of


def centred(own_key, dims, deviation, bound, cuts=(), held_as=jnp.bfloat16):
    level = block_levels(own_key, dims, cuts, -0.22, 0.18) if cuts else 1.0
    entries = jax.random.normal(own_key, dims, jnp.float32) * deviation * level
    return jnp.minimum(jnp.maximum(entries, -bound), bound).astype(held_as)


def setup_inputs(seed: int = 0) -> dict:
    keys = jax.random.split(jax.random.key(seed), 14)
    hidden_in = centred(keys[0], (SEQS, N_TENSOR, TOKS, D), 1.0, 6.0, ((0, 4), (1, 4), (2, 8)))
    cotangent = centred(keys[1], (SEQS, N_TENSOR, TOKS, D), 1.0, 6.0, ((0, 4), (1, 4), (2, 8)))
    block_order = draw_block_order(jax.random.fold_in(keys[13], 71), 0)
    query_weight = centred(keys[3], (D, KVH, QW), D ** -0.5, 0.1875, ((0, 16), (1, 8)))
    keyval_weight = centred(keys[4], (D, KVH, 2 * HD), D ** -0.5, 0.1875, ((0, 16), (1, 8)))
    output_weight = centred(keys[5], (D, KVH, QW), (HQ * HD // 64) ** -0.5, 1.5, ((0, 16), (1, 8)))
    gate_weight = centred(keys[6], (D, FF), D ** -0.5, 0.1875, ((0, 32), (1, 4)))
    up_weight = centred(keys[7], (D, FF), D ** -0.5, 0.1875, ((0, 32), (1, 4)))
    down_weight = centred(keys[8], (D, FF), FF ** -0.5, 0.09375, ((0, 32), (1, 4)))
    attn_gain = jnp.clip(1.0 + 0.18 * jax.random.normal(keys[9], (D,), jnp.float32), 0.1, 1.9)
    ffn_gain = jnp.clip(1.0 + 0.18 * jax.random.normal(keys[10], (D,), jnp.float32), 0.1, 1.9)
    query_gain = jnp.clip(1.0 + 0.18 * jax.random.normal(keys[11], (HD,), jnp.float32), 0.1, 1.9)
    key_gain = jnp.clip(1.0 + 0.18 * jax.random.normal(keys[12], (HD,), jnp.float32), 0.1, 1.9)
    return dict(hidden_in=hidden_in, cotangent=cotangent, block_order=block_order, query_weight=query_weight, keyval_weight=keyval_weight, output_weight=output_weight, gate_weight=gate_weight, up_weight=up_weight, down_weight=down_weight, attn_gain=attn_gain, ffn_gain=ffn_gain, query_gain=query_gain, key_gain=key_gain)


eps_norm = 1e-05
rope_base = 1000000.0

@jax.custom_vjp
def low(v):
    return lax.optimization_barrier(v.astype(jnp.bfloat16)).astype(jnp.float32)

@jax.custom_vjp
def low_back(v):
    return v

def low_keep(v):
    return (low(v), None)

def low_pass(kept, grad):
    return (grad,)

def back_keep(v):
    return (v, None)

def back_low(kept, grad):
    return (low(grad),)
low.defvjp(low_keep, low_pass)
low_back.defvjp(back_keep, back_low)

def rms_scale(values):
    return lax.rsqrt(lax.optimization_barrier(jnp.mean(values * values, axis=-1, keepdims=True)) + eps_norm)

def rope_tables(positions, head_width):
    half = head_width // 2
    freq = rope_base ** (-(jnp.arange(half, dtype=jnp.float32) * 2.0 / head_width))
    angles = positions.astype(jnp.float32)[:, None] * freq[None, :]
    return (jnp.cos(angles), jnp.sin(angles))

def rotate(values, cosine, sine):
    half = values.shape[-1] // 2
    first = values[..., :half]
    second = values[..., half:]
    return jnp.concatenate([first * cosine - second * sine, second * cosine + first * sine], axis=-1)

def product(left, right):
    return jnp.dot(left, right, precision=lax.Precision.HIGHEST, preferred_element_type=jnp.float32)

def layer(sequence, weights, positions):
    query_w, keyval_w, output_w, gate_w, up_w, down_w, gain_one, gain_two, gain_query, gain_key = weights
    scale = HD ** (-0.5)
    normed_one = low(sequence * rms_scale(sequence) * gain_one)
    query_raw = low_back(product(normed_one, query_w.reshape(D, KVH * QW))).reshape(LEN, KVH, GROUP, HD)
    keyval_raw = low_back(product(normed_one, keyval_w.reshape(D, KVH * 2 * HD))).reshape(LEN, KVH, 2, HD)
    cosine, sine = rope_tables(positions, HD)
    query_rot = low(rotate(query_raw * rms_scale(query_raw) * gain_query, cosine[:, None, None, :], sine[:, None, None, :]))
    key_raw = keyval_raw[:, :, 0, :]
    value_raw = keyval_raw[:, :, 1, :]
    key_rot = low(rotate(key_raw * rms_scale(key_raw) * gain_key, cosine[:, None, :], sine[:, None, :]))
    value_low = low(value_raw)
    blocks = max(LEN // 512, 1)
    query_blocks = query_rot.reshape(blocks, LEN // blocks, KVH, GROUP, HD)
    position_blocks = positions.reshape(blocks, LEN // blocks)

    def one_block(operands):
        query_part, position_part = operands
        scores = low_back(jnp.einsum('ckgd,lkd->kgcl', query_part, key_rot, precision=lax.Precision.HIGHEST) * scale)
        allowed = position_part[:, None] >= positions[None, :]
        scores = jnp.where(allowed[None, None], scores, -1e+30)
        shares = low(jax.nn.softmax(scores, axis=-1))
        return jnp.einsum('kgcl,lkd->ckgd', shares, value_low, precision=lax.Precision.HIGHEST)
    context = lax.map(jax.checkpoint(one_block), (query_blocks, position_blocks))
    context = low_back(low(context.reshape(LEN, KVH * QW)))
    branch = low_back(product(context, output_w.reshape(D, KVH * QW).T))
    middle = sequence + branch
    normed_two = low(middle * rms_scale(middle) * gain_two)
    gate_value = low_back(product(normed_two, gate_w))
    upper_value = low_back(product(normed_two, up_w))
    hidden = low(jax.nn.silu(gate_value) * upper_value)
    feed = low_back(product(hidden, down_w.T))
    return middle + feed

def reference(hidden_in, cotangent, block_order, query_weight, keyval_weight, output_weight, gate_weight, up_weight, down_weight, attn_gain, ffn_gain, query_gain, key_gain):
    offsets = jnp.arange(BLOCK, dtype=jnp.int32)
    positions = (block_order[:, :, None] * BLOCK + offsets[None, None, :]).reshape(LEN).astype(jnp.int32)
    inputs = hidden_in.astype(jnp.float32).reshape(SEQS, LEN, D)
    weights = [weight.astype(jnp.float32) for weight in (query_weight, keyval_weight, output_weight, gate_weight, up_weight, down_weight, attn_gain, ffn_gain, query_gain, key_gain)]

    def whole(sequences, query_w, keyval_w, output_w, gate_w, up_w, down_w, gain_one, gain_two, gain_query, gain_key):
        packed = (query_w, keyval_w, output_w, gate_w, up_w, down_w, gain_one, gain_two, gain_query, gain_key)

        def one_sequence(sequence):
            return layer(sequence, packed, positions)
        return lax.map(jax.checkpoint(one_sequence), sequences)
    outputs, pullback = jax.vjp(whole, inputs, weights[0], weights[1], weights[2], weights[3], weights[4], weights[5], weights[6], weights[7], weights[8], weights[9])
    grads = pullback(cotangent.astype(jnp.float32).reshape(SEQS, LEN, D))
    block_out = outputs.reshape(SEQS, N_TENSOR, TOKS, D).astype(jnp.bfloat16)
    input_grad = grads[0].reshape(SEQS, N_TENSOR, TOKS, D)
    return (block_out, input_grad, grads[1], grads[2], grads[3], grads[4], grads[5], grads[6], grads[7], grads[8], grads[9], grads[10])
```

```python
import jax
import jax.numpy as jnp
from jax import lax
from jax.sharding import PartitionSpec as P

eps_norm = 1e-05
rope_base = 1000000.0
masked_value = -1e30


def rms_scale(values):
    return lax.rsqrt(jnp.mean(values * values, axis=-1, keepdims=True) + eps_norm)


def rope_tables(positions, head_width):
    half = head_width // 2
    freq = rope_base ** (-(jnp.arange(half, dtype=jnp.float32) * 2.0 / head_width))
    angles = positions.astype(jnp.float32)[:, None] * freq[None, :]
    return (jnp.cos(angles), jnp.sin(angles))


def rotate(values, cosine, sine):
    half = values.shape[-1] // 2
    first = values[..., :half]
    second = values[..., half:]
    return jnp.concatenate(
        [first * cosine - second * sine, second * cosine + first * sine], axis=-1
    )


def rotate_back(grads, cosine, sine):
    half = grads.shape[-1] // 2
    first = grads[..., :half]
    second = grads[..., half:]
    return jnp.concatenate(
        [first * cosine + second * sine, second * cosine - first * sine], axis=-1
    )


def norm_back(values, scale, gain, grads):
    scaled = grads * gain
    inner = jnp.mean(scaled * values, axis=-1, keepdims=True)
    return (scale * (scaled - values * scale * scale * inner), grads * values * scale)


def matmul(left, right):
    return jnp.dot(left, right, preferred_element_type=jnp.float32)


def contract_rows(left, right):
    return lax.dot_general(
        left, right, (((0,), (0,)), ((), ())), preferred_element_type=jnp.float32
    )


def contract_cols(left, right):
    return lax.dot_general(
        left, right, (((1,), (1,)), ((), ())), preferred_element_type=jnp.float32
    )


def sum_four(parts):
    return (parts[0] + parts[2]) + (parts[1] + parts[3])


def shift_chips(values, axis, step):
    size = lax.axis_size(axis)
    return lax.ppermute(values, axis, [(i, (i + step) % size) for i in range(size)])


def shift_z(values, step):
    size = lax.axis_size("heads")
    return lax.ppermute(values, "heads", [(i, (i + 2 * step) % size) for i in range(size)])


def swap_core(values):
    size = lax.axis_size("heads")
    return lax.ppermute(values, "heads", [(i, i ^ 1) for i in range(size)])


def gather_ring(values, axis):
    shift = shift_z if axis == "z" else lambda v, s: shift_chips(v, axis, s)
    return [values] + [shift(values, s) for s in (1, 2, 3)]


def scatter_ring(parts, axis):
    shift = shift_z if axis == "z" else lambda v, s: shift_chips(v, axis, s)
    return [parts[0]] + [shift(parts[s], -s) for s in (1, 2, 3)]


def gather_heads(values):
    own = jnp.stack(gather_ring(values, "z"))
    return jnp.stack([own, swap_core(own)])


def scatter_heads(parts):
    own = parts[0].astype(jnp.float32) + swap_core(parts[1]).astype(jnp.float32)
    own_low = own.astype(jnp.bfloat16)
    moved = scatter_ring([own[0], own_low[1], own_low[2], own_low[3]], "z")
    return sum_four([part.astype(jnp.float32) for part in moved])


def scatter_tensor(parts, first):
    moved = scatter_ring([first, parts[1], parts[2], parts[3]], "tensor")
    return sum_four([part.astype(jnp.float32) for part in moved])


def reduce_all(values):
    values = values + swap_core(values)
    for axis in ("z", "tensor", "fsdp"):
        values = sum_four(gather_ring(values, axis))
    return values


def scatter_rows(grads, axis):
    size = lax.axis_size(axis)
    rank = lax.axis_index(axis)
    rows = grads.shape[0] // size
    pieces = [
        lax.dynamic_slice_in_dim(grads, lax.rem(rank - s + size, size) * rows, rows, 0)
        for s in range(size)
    ]
    moved = scatter_ring([pieces[0]] + [p.astype(jnp.bfloat16) for p in pieces[1:]], axis)
    return sum_four([part.astype(jnp.float32) for part in moved])


def masked_scores(queries, keys, query_pos, key_pos, scale):
    scores = jnp.einsum("cgd,ld->gcl", queries, keys, preferred_element_type=jnp.float32) * scale
    allowed = query_pos[:, None] >= key_pos[None, :]
    return jnp.where(allowed[None], scores, masked_value)


def attend(queries, keys, values, query_pos, key_pos, scale):
    scores = masked_scores(queries, keys, query_pos, key_pos, scale)
    row_max = jnp.max(scores, axis=-1, keepdims=True)
    raised = jnp.exp(scores - row_max)
    total = jnp.sum(raised, axis=-1, keepdims=True)
    shares = (raised / total).astype(jnp.bfloat16)
    context = jnp.einsum("gcl,ld->cgd", shares, values, preferred_element_type=jnp.float32)
    return (context.astype(jnp.bfloat16), (row_max + jnp.log(total))[..., 0])


def attend_back(queries, keys, values, logsum, context_grad, query_pos, key_pos, scale):
    scores = masked_scores(queries, keys, query_pos, key_pos, scale)
    shares = jnp.exp(scores - logsum[..., None])
    share_grad = jnp.einsum("cgd,ld->gcl", context_grad, values, preferred_element_type=jnp.float32)
    share_dot = jnp.sum(shares * share_grad, axis=-1, keepdims=True)
    score_low = (shares * (share_grad - share_dot)).astype(jnp.bfloat16)
    query_part = (
        jnp.einsum("gcl,ld->cgd", score_low, keys, preferred_element_type=jnp.float32) * scale
    )
    key_part = (
        jnp.einsum("gcl,cgd->ld", score_low, queries, preferred_element_type=jnp.float32) * scale
    )
    value_part = jnp.einsum(
        "gcl,cgd->ld",
        shares.astype(jnp.bfloat16),
        context_grad,
        preferred_element_type=jnp.float32,
    )
    return (query_part, key_part, value_part)


def body(
    hidden_in,
    cotangent,
    block_order,
    query_weight,
    keyval_weight,
    output_weight,
    gate_weight,
    up_weight,
    down_weight,
    attn_gain,
    ffn_gain,
    query_gain,
    key_gain,
):
    sequences, _, own_rows, width = hidden_in.shape
    tensor_size = lax.axis_size("tensor")
    heads_size = lax.axis_size("heads")
    chips = heads_size // 2
    shard_rows = own_rows * heads_size
    block_len = shard_rows // 2
    seq_len = shard_rows * tensor_size
    head_dim = query_gain.shape[0]
    units = gate_weight.shape[1]
    query_width = query_weight.shape[2]
    group_size = query_width // head_dim
    scale = head_dim ** (-0.5)
    rank = lax.axis_index("tensor")
    head_rank = lax.axis_index("heads")
    hidden_own = hidden_in[:, 0]
    cot_own = cotangent[:, 0]

    chip_at = lax.rem(head_rank // 2 - jnp.arange(chips, dtype=jnp.int32) + chips, chips)
    core_at = lax.rem(head_rank + jnp.arange(2, dtype=jnp.int32), 2)
    head_at = (chip_at[:, None] * 2 + core_at[None, :]).reshape(heads_size)
    row_at = (head_at[:, None] * own_rows + jnp.arange(own_rows, dtype=jnp.int32)[None, :]).reshape(
        shard_rows
    )
    rank_at = lax.rem(rank - jnp.arange(tensor_size, dtype=jnp.int32) + tensor_size, tensor_size)
    order_at = block_order[rank_at]
    second = row_at >= block_len
    key_pos = (
        jnp.where(second[None, :], order_at[:, 1:2], order_at[:, 0:1]) * block_len
        + lax.rem(row_at, block_len)[None, :]
    )
    query_pos = key_pos[0]
    key_pos = key_pos.reshape(seq_len)
    cosine, sine = rope_tables(query_pos, head_dim)
    cos_query = cosine[None, :, None, :]
    sin_query = sine[None, :, None, :]
    cos_key = cosine[None]
    sin_key = sine[None]

    attn_own = jnp.concatenate(
        [query_weight[:, 0], keyval_weight[:, 0], output_weight[:, 0]], axis=1
    )
    attn_all = lax.all_gather(attn_own, ("fsdp", "tensor"), axis=0, tiled=True)
    feed_own = jnp.concatenate([gate_weight, up_weight, down_weight], axis=1)
    feed_all = lax.all_gather(feed_own, ("fsdp", "heads"), axis=0, tiled=True)
    qkv_all = attn_all[:, : 2 * query_width]
    output_all = attn_all[:, 2 * query_width :]
    gate_up_all = feed_all[:, : 2 * units]
    down_all = feed_all[:, 2 * units :]

    def to_sequence(values):
        values = values.reshape(2, chips, sequences, own_rows, values.shape[-1])
        return values.transpose(2, 1, 0, 3, 4).reshape(sequences, shard_rows, values.shape[-1])

    def from_sequence(values):
        values = values.reshape(sequences, chips, 2, own_rows, values.shape[-1])
        return values.transpose(2, 1, 0, 3, 4).reshape(sequences * shard_rows, values.shape[-1])

    inputs = hidden_own.astype(jnp.float32)
    scale_one = rms_scale(inputs)
    normed_one = (inputs * scale_one * attn_gain).astype(jnp.bfloat16)
    rows_flat = gather_heads(normed_one).reshape(sequences * shard_rows, width)
    cot_flat = jnp.stack(gather_ring(cot_own, "tensor")).reshape(-1, width)
    qkv_raw = to_sequence(matmul(rows_flat, qkv_all))
    query_raw = qkv_raw[..., :query_width].reshape(sequences, shard_rows, group_size, head_dim)
    key_raw = qkv_raw[..., query_width : query_width + head_dim]
    value_raw = qkv_raw[..., query_width + head_dim :]
    query_scale = rms_scale(query_raw)
    key_scale = rms_scale(key_raw)
    query_rot = rotate(query_raw * query_scale * query_gain, cos_query, sin_query).astype(
        jnp.bfloat16
    )
    key_rot = rotate(key_raw * key_scale * key_gain, cos_key, sin_key).astype(jnp.bfloat16)
    sending = jnp.concatenate([key_rot, value_raw.astype(jnp.bfloat16)], axis=-1)
    gathered = jnp.stack(gather_ring(sending, "tensor"), axis=1)
    gathered = gathered.reshape(sequences, seq_len, 2 * head_dim)
    keys_all = gathered[..., :head_dim]
    values_all = gathered[..., head_dim:]

    halves = [slice(0, block_len), slice(block_len, shard_rows)]
    contexts = []
    logsums = []
    for seq in range(sequences):
        pieces = [
            attend(
                query_rot[seq, half], keys_all[seq], values_all[seq], query_pos[half], key_pos, scale
            )
            for half in halves
        ]
        contexts.append(jnp.concatenate([piece[0] for piece in pieces]))
        logsums.append([piece[1] for piece in pieces])
    context_flat = from_sequence(
        jnp.stack(contexts).reshape(sequences, shard_rows, query_width)
    )
    branch_part = contract_cols(context_flat, output_all).astype(jnp.bfloat16)
    branch = scatter_heads(branch_part.reshape(2, chips, sequences, own_rows, width))
    middle = inputs + branch
    scale_two = rms_scale(middle)
    normed_two = (middle * scale_two * ffn_gain).astype(jnp.bfloat16)
    two_flat = jnp.stack(gather_ring(normed_two, "tensor")).reshape(-1, width)
    gate_up = matmul(two_flat, gate_up_all)
    gate_value = gate_up[:, :units]
    upper_value = gate_up[:, units:]
    sigmoid_gate = jax.nn.sigmoid(gate_value)
    activated = gate_value * sigmoid_gate
    hidden = (activated * upper_value).astype(jnp.bfloat16)
    hidden_grad = matmul(cot_flat, down_all)
    gate_low = (
        hidden_grad * upper_value * sigmoid_gate * (1.0 + gate_value * (1.0 - sigmoid_gate))
    ).astype(jnp.bfloat16)
    upper_low = (hidden_grad * activated).astype(jnp.bfloat16)
    both_low = jnp.concatenate([gate_low, upper_low], axis=1)
    normed_two_part = contract_cols(both_low, gate_up_all).reshape(
        tensor_size, sequences, own_rows, width
    )
    normed_two_grad = scatter_tensor(normed_two_part.astype(jnp.bfloat16), normed_two_part[0])
    middle_norm_grad, ffn_terms = norm_back(middle, scale_two, ffn_gain, normed_two_grad)
    middle_grad = cot_own.astype(jnp.float32) + middle_norm_grad
    branch_low = middle_grad.astype(jnp.bfloat16)
    feed_part = contract_cols(hidden, down_all).reshape(tensor_size, sequences, own_rows, width)
    feed = scatter_tensor(feed_part.astype(jnp.bfloat16), feed_part[0])
    block_out = (middle + feed).astype(jnp.bfloat16)
    feed_grad = jnp.concatenate(
        [
            contract_rows(two_flat, both_low).astype(jnp.bfloat16),
            contract_rows(cot_flat, hidden).astype(jnp.bfloat16),
        ],
        axis=1,
    )
    feed_grad = lax.psum_scatter(
        feed_grad, ("fsdp", "heads"), scatter_dimension=0, tiled=True
    ).astype(jnp.float32)

    branch_flat = gather_heads(branch_low).reshape(sequences * shard_rows, width)
    context_grad = to_sequence(matmul(branch_flat, output_all).astype(jnp.bfloat16))
    context_grad = context_grad.reshape(sequences, shard_rows, group_size, head_dim)
    output_grad = contract_rows(branch_flat, context_flat)

    query_parts = []
    key_totals = []
    for seq in range(sequences):
        pieces = [
            attend_back(
                query_rot[seq, half],
                keys_all[seq],
                values_all[seq],
                logsums[seq][at],
                context_grad[seq, half],
                query_pos[half],
                key_pos,
                scale,
            )
            for at, half in enumerate(halves)
        ]
        query_parts.append(jnp.concatenate([piece[0] for piece in pieces]))
        key_totals.append(
            jnp.concatenate(
                [pieces[0][1] + pieces[1][1], pieces[0][2] + pieces[1][2]], axis=-1
            ).reshape(tensor_size, shard_rows, 2 * head_dim)
        )
    kv_terms = jnp.stack(key_totals, axis=1)
    kv_own = scatter_tensor(kv_terms.astype(jnp.bfloat16), kv_terms[0])
    key_rot_grad = kv_own[..., :head_dim]
    value_grad = kv_own[..., head_dim:]
    query_rot_grad = jnp.stack(query_parts)
    query_norm_grad = rotate_back(query_rot_grad, cos_query, sin_query)
    query_raw_grad, query_terms = norm_back(query_raw, query_scale, query_gain, query_norm_grad)
    key_norm_grad = rotate_back(key_rot_grad, cos_key, sin_key)
    key_raw_grad, key_terms = norm_back(key_raw, key_scale, key_gain, key_norm_grad)
    qkv_low = from_sequence(
        jnp.concatenate(
            [
                query_raw_grad.reshape(sequences, shard_rows, query_width),
                key_raw_grad,
                value_grad,
            ],
            axis=-1,
        ).astype(jnp.bfloat16)
    )
    normed_one_part = contract_cols(qkv_low, qkv_all).astype(jnp.bfloat16)
    normed_one_grad = scatter_heads(
        normed_one_part.reshape(2, chips, sequences, own_rows, width)
    )
    qkv_grad = contract_rows(rows_flat, qkv_low)
    attn_grad = jnp.concatenate([qkv_grad, output_grad], axis=1)
    attn_grad = scatter_rows(scatter_rows(attn_grad, "fsdp"), "tensor")
    attn_gain_part = jnp.sum(qkv_grad * qkv_all.astype(jnp.float32), axis=1) / attn_gain
    gains = reduce_all(
        jnp.concatenate(
            [
                attn_gain_part,
                jnp.sum(ffn_terms, axis=(0, 1)),
                jnp.sum(query_terms, axis=(0, 1, 2)),
                jnp.sum(key_terms, axis=(0, 1)),
            ]
        )
    )
    input_norm_grad, _ = norm_back(inputs, scale_one, attn_gain, normed_one_grad)
    input_grad = middle_grad + input_norm_grad
    return (
        block_out[:, None],
        input_grad[:, None],
        attn_grad[:, None, :query_width],
        attn_grad[:, None, query_width : 2 * query_width],
        attn_grad[:, None, 2 * query_width :],
        feed_grad[:, :units],
        feed_grad[:, units : 2 * units],
        feed_grad[:, 2 * units :],
        gains[:width],
        gains[width : 2 * width],
        gains[2 * width : 2 * width + head_dim],
        gains[2 * width + head_dim :],
    )


def solution(mesh):
    placed = (
        P("fsdp", "tensor", "heads", None),
        P("fsdp", "tensor", "heads", None),
        P(),
        P(("fsdp", "tensor"), "heads", None),
        P(("fsdp", "tensor"), "heads", None),
        P(("fsdp", "tensor"), "heads", None),
        P(("fsdp", "heads"), "tensor"),
        P(("fsdp", "heads"), "tensor"),
        P(("fsdp", "heads"), "tensor"),
        P(),
        P(),
        P(),
        P(),
    )
    return jax.shard_map(
        body,
        mesh=mesh,
        in_specs=placed,
        out_specs=(
            P("fsdp", "tensor", "heads", None),
            P("fsdp", "tensor", "heads", None),
            P(("fsdp", "tensor"), "heads", None),
            P(("fsdp", "tensor"), "heads", None),
            P(("fsdp", "tensor"), "heads", None),
            P(("fsdp", "heads"), "tensor"),
            P(("fsdp", "heads"), "tensor"),
            P(("fsdp", "heads"), "tensor"),
            P(),
            P(),
            P(),
            P(),
        ),
        check_vma=False,
    )
```

```python
import functools

import jax
import jax.numpy as jnp
from jax import lax
from jax.experimental import pallas as pl
from jax.experimental.pallas import tpu as pltpu
from jax.sharding import PartitionSpec as P

eps_norm = 1e-05
rope_base = 1000000.0
log2_e = 1.4426950408889634
block = 256
piece = 64
head_dim = 64
lanes = 128


def rms_scale(values):
    return lax.rsqrt(jnp.mean(values * values, axis=-1, keepdims=True) + eps_norm)


def norm_back(values, scale, gain, grads):
    scaled = grads * gain
    inner = jnp.mean(scaled * values, axis=-1, keepdims=True)
    return (scale * (scaled - values * scale * scale * inner), grads * values * scale)


def matmul(left, right):
    return jnp.dot(left, right, preferred_element_type=jnp.float32)


def contract_rows(left, right):
    return lax.dot_general(
        left, right, (((0,), (0,)), ((), ())), preferred_element_type=jnp.float32
    )


def contract_cols(left, right):
    return lax.dot_general(
        left, right, (((1,), (1,)), ((), ())), preferred_element_type=jnp.float32
    )


def sum_four(parts):
    return (parts[0] + parts[2]) + (parts[1] + parts[3])


def shift_chips(values, axis, step):
    size = lax.axis_size(axis)
    return lax.ppermute(values, axis, [(i, (i + step) % size) for i in range(size)])


def shift_z(values, step):
    size = lax.axis_size("heads")
    return lax.ppermute(values, "heads", [(i, (i + 2 * step) % size) for i in range(size)])


def swap_core(values):
    size = lax.axis_size("heads")
    return lax.ppermute(values, "heads", [(i, i ^ 1) for i in range(size)])


def gather_ring(values, axis):
    shift = shift_z if axis == "z" else lambda v, s: shift_chips(v, axis, s)
    return [values] + [shift(values, s) for s in (1, 2, 3)]


def scatter_ring(parts, axis):
    shift = shift_z if axis == "z" else lambda v, s: shift_chips(v, axis, s)
    return [parts[0]] + [shift(parts[s], -s) for s in (1, 2, 3)]


def gather_heads(values):
    own = jnp.stack(gather_ring(values, "z"))
    return jnp.stack([own, swap_core(own)])


def scatter_heads(parts):
    own = parts[0].astype(jnp.float32) + swap_core(parts[1]).astype(jnp.float32)
    own_low = own.astype(jnp.bfloat16)
    moved = scatter_ring([own[0], own_low[1], own_low[2], own_low[3]], "z")
    return sum_four([part.astype(jnp.float32) for part in moved])


def scatter_tensor(parts, first):
    moved = scatter_ring([first, parts[1], parts[2], parts[3]], "tensor")
    return sum_four([part.astype(jnp.float32) for part in moved])


def split_low(values):
    high = values.astype(jnp.bfloat16)
    rest = (values - high.astype(jnp.float32)).astype(jnp.bfloat16)
    return jnp.stack([high, rest])


def scatter_rows(grads, gains, axis):
    size = lax.axis_size(axis)
    rank = lax.axis_index(axis)
    rows = grads.shape[0] // size
    columns = grads.shape[1]
    count = gains.shape[0]
    extra = -(-2 * count // (16 * columns)) * 16
    tail = split_low(gains).reshape(-1)
    tail = jnp.pad(tail, (0, extra * columns - 2 * count)).reshape(extra, columns)
    pieces = [
        lax.dynamic_slice_in_dim(grads, lax.rem(rank - s + size, size) * rows, rows, 0)
        for s in range(size)
    ]
    sent = [jnp.concatenate([p.astype(jnp.bfloat16), tail]) for p in pieces[1:]]
    moved = scatter_ring([pieces[0]] + sent, axis)
    total = sum_four([part[:rows].astype(jnp.float32) for part in moved])
    tails = [tail] + [part[rows:] for part in moved[1:]]
    tails = [t.reshape(-1)[: 2 * count].reshape(2, count).astype(jnp.float32) for t in tails]
    return total, sum_four([t[0] + t[1] for t in tails])


def place_ring(parts, axis):
    size = lax.axis_size(axis)
    rank = lax.axis_index(axis)
    placed = jnp.zeros((size,) + parts[0].shape, parts[0].dtype)
    for s, part in enumerate(parts):
        placed = lax.dynamic_update_index_in_dim(placed, part, lax.rem(rank - s + size, size), 0)
    return placed


def dot_nn(left, right):
    return lax.dot_general(
        left, right, (((1,), (0,)), ((), ())), preferred_element_type=jnp.float32
    )


def dot_nt(left, right):
    return lax.dot_general(
        left, right, (((1,), (1,)), ((), ())), preferred_element_type=jnp.float32
    )


def lane_index(shape):
    return lax.broadcasted_iota(jnp.int32, shape, 1)


def half_sums(values):
    rows = lax.broadcasted_iota(jnp.int32, (lanes, lanes), 0) // head_dim
    columns = lax.broadcasted_iota(jnp.int32, (lanes, lanes), 1) // head_dim
    ones = jnp.where(rows == columns, 1.0, 0.0).astype(jnp.float32)
    return lax.dot_general(
        values,
        ones,
        (((1,), (0,)), ((), ())),
        precision=lax.Precision.HIGHEST,
        preferred_element_type=jnp.float32,
    )


def turn_lanes(values):
    lane = lane_index(values.shape)
    up = pltpu.roll(values, lanes - head_dim // 2, 1)
    down = pltpu.roll(values, head_dim // 2, 1)
    return jnp.where(lax.rem(lane, head_dim) < head_dim // 2, up, down)


def rows_of(ref):
    return ref[...].reshape(ref.shape[0] * ref.shape[1] * ref.shape[3], ref.shape[4])


def prepare_kernel(raw_ref, gain_ref, cos_ref, sin_ref, query_ref, keyval_ref):
    raw = rows_of(raw_ref)
    cosine = cos_ref[...]
    sine = sin_ref[...]
    shape = query_ref.shape
    first = lane_index(cosine.shape) < head_dim
    for part, out_ref in ((0, query_ref), (1, keyval_ref)):
        values = raw[:, part * lanes : (part + 1) * lanes]
        scale = lax.rsqrt(half_sums(values * values) * (1.0 / head_dim) + eps_norm)
        normed = values * scale * gain_ref[:, part * lanes : (part + 1) * lanes]
        turned = normed * cosine + turn_lanes(normed) * sine
        if part == 1:
            turned = jnp.where(first, turned, values)
        out_ref[...] = turned.astype(jnp.bfloat16).reshape(shape)


def finish_kernel(
    raw_ref, gain_ref, cos_ref, sin_ref, query_ref, own_ref, one_ref, two_ref, three_ref,
    low_ref, terms_ref,
):
    raw = rows_of(raw_ref)
    cosine = cos_ref[...]
    sine = sin_ref[...]
    first = lane_index(cosine.shape) < head_dim
    keyval = (rows_of(own_ref) + rows_of(two_ref).astype(jnp.float32)) + (
        rows_of(one_ref).astype(jnp.float32) + rows_of(three_ref).astype(jnp.float32)
    )

    @pl.when(pl.program_id(0) == 0)
    def _():
        terms_ref[...] = jnp.zeros(terms_ref.shape, jnp.float32)

    for part, grads in ((0, rows_of(query_ref)), (1, keyval)):
        at = slice(part * lanes, (part + 1) * lanes)
        values = raw[:, at]
        scale = lax.rsqrt(half_sums(values * values) * (1.0 / head_dim) + eps_norm)
        turned = grads * cosine - turn_lanes(grads) * sine
        scaled = turned * gain_ref[:, at]
        inner = half_sums(scaled * values) * (1.0 / head_dim)
        back = scale * (scaled - values * scale * scale * inner)
        terms = turned * values * scale
        if part == 1:
            back = jnp.where(first, back, grads)
        terms_ref[:, at] += jnp.sum(terms.reshape(-1, 8, lanes), axis=0)
        low_ref[..., at] = back.astype(jnp.bfloat16).reshape(low_ref.shape[:-1] + (lanes,))


def row_places(meta_ref):
    chip = meta_ref[8]
    core = meta_ref[9]
    places = []
    for s in range(4):
        chip_at = lax.rem(chip - s + 4, 4)
        for cr in range(2):
            core_at = lax.rem(core + cr, 2)
            slot = lax.div(chip_at, 2)
            row = lax.rem(chip_at, 2) * (2 * piece) + core_at * piece
            places.append((s, cr, slot, row))
    return places


def at_row(start, count=piece):
    return pl.ds(pl.multiple_of(start, piece), count)


def load_keys(places, meta_ref, keyval_refs, key_s, value_s, ones):
    lane = lane_index((piece, lanes))
    first = lane < head_dim
    none = jnp.zeros((piece, lanes), jnp.bfloat16)
    one = jnp.ones((piece, lanes), jnp.bfloat16)
    for u, keyval_ref in enumerate(keyval_refs):
        for s, cr, slot, row in places:
            values = keyval_ref[cr, s, 0]
            other = jnp.concatenate([values[:, head_dim:], values[:, :head_dim]], axis=1)
            start = meta_ref[2 * u + slot] * (2 * block) + row
            lower = at_row(start)
            upper = at_row(start + block)
            key_s[lower, :] = jnp.where(first, values, none)
            key_s[upper, :] = jnp.where(first, none, other)
            value_s[lower, :lanes] = jnp.where(first, other, none)
            value_s[upper, :lanes] = jnp.where(first, none, values)
            if ones:
                value_s[lower, lanes:] = jnp.where(first, one, none)
                value_s[upper, lanes:] = jnp.where(first, none, one)


def block_steps(meta_ref, blocks):
    first = meta_ref[0]
    steps = []
    for i in range(blocks - 1):
        early = i < first
        steps.append((jnp.where(early, 0, 1), jnp.where(early, i, i - first), False))
    steps.append((0, first, True))
    steps.append((1, meta_ref[1], True))
    return steps


def attend_kernel(
    factor, meta_ref, query_ref, own_ref, one_ref, two_ref, three_ref,
    context_ref, low_ref, total_ref, query_s, key_s, value_s, sum_s,
):
    places = row_places(meta_ref)
    load_keys(places, meta_ref, (own_ref, one_ref, two_ref, three_ref), key_s, value_s, True)
    for s, cr, slot, row in places:
        query_s[at_row(slot * block + row), :] = query_ref[cr, s, 0]
    sum_s[...] = jnp.zeros(sum_s.shape, jnp.float32)
    query_at = lax.broadcasted_iota(jnp.int32, (block, 2 * block), 0)
    key_at = lax.rem(lane_index((block, 2 * block)), block)
    for b, j, diagonal in block_steps(meta_ref, key_s.shape[0] // (2 * block)):
        rows = pl.ds(pl.multiple_of(b * block, block), block)
        keys = pl.ds(pl.multiple_of(j * (2 * block), 2 * block), 2 * block)
        raised = jnp.exp2(dot_nt(query_s[rows, :], key_s[keys, :]) * factor)
        if diagonal:
            raised = jnp.where(query_at >= key_at, raised, 0.0)
        sum_s[rows, :] += dot_nn(raised.astype(jnp.bfloat16), value_s[keys, :])
    for s, cr, slot, row in places:
        found = sum_s[at_row(slot * block + row), :]
        total = found[:, lanes:]
        context = found[:, :lanes] / total
        context_ref[cr, s, 0] = context
        low_ref[cr, s, 0] = context.astype(jnp.bfloat16)
        total_ref[cr, s, 0] = total


def attend_back_kernel(
    factor, scale, meta_ref, query_ref, own_ref, one_ref, two_ref, three_ref,
    context_ref, total_ref, grad_ref,
    query_out, own_out, one_out, two_out, three_out,
    query_s, grad_s, context_s, total_s, stack_s, key_s, value_s, turned_s, rows_s, query_sum,
    keyval_sum,
):
    places = row_places(meta_ref)
    load_keys(places, meta_ref, (own_ref, one_ref, two_ref, three_ref), key_s, value_s, False)
    blocks = key_s.shape[0] // (2 * block)
    for j in range(blocks):
        turned_s[j] = key_s[j * 2 * block : (j + 1) * 2 * block, :].T
    for s, cr, slot, row in places:
        at = at_row(slot * block + row)
        query_s[at, :] = query_ref[cr, s, 0]
        grad_s[at, :] = grad_ref[cr, s, 0]
        context_s[at, :] = context_ref[cr, s, 0]
        total_s[at, :] = total_ref[cr, s, 0]
    first = lane_index((block, lanes)) < head_dim
    none = jnp.zeros((block, lanes), jnp.bfloat16)
    pick = lax.broadcasted_iota(jnp.int32, (8, lanes), 0)
    pick = jnp.where(pick == lane_index((8, lanes)) // head_dim, 1.0, 0.0).astype(jnp.float32)
    for b in range(2):
        at = slice(b * block, (b + 1) * block)
        query = query_s[at, :]
        grads = grad_s[at, :]
        other_query = jnp.concatenate([query[:, head_dim:], query[:, :head_dim]], axis=1)
        other_grads = jnp.concatenate([grads[:, head_dim:], grads[:, :head_dim]], axis=1)
        base = 4 * b * block
        stack_s[base : base + block, :] = jnp.where(first, query, none)
        stack_s[base + block : base + 2 * block, :] = jnp.where(first, other_query, none)
        stack_s[base + 2 * block : base + 3 * block, :] = jnp.where(first, none, other_grads)
        stack_s[base + 3 * block : base + 4 * block, :] = jnp.where(first, none, grads)
        inner = lax.dot_general(
            pick,
            grads.astype(jnp.float32) * context_s[at, :],
            (((1,), (1,)), ((), ())),
            precision=lax.Precision.HIGHEST,
            preferred_element_type=jnp.float32,
        )
        logs = jnp.log2(total_s[at, :]).T
        rows_s[b, 0:1, :] = logs[0:1, :]
        rows_s[b, 1:2, :] = logs[head_dim : head_dim + 1, :]
        rows_s[b, 2:4, :] = inner[0:2, :]
    query_sum[...] = jnp.zeros(query_sum.shape, jnp.float32)
    keyval_sum[...] = jnp.zeros(keyval_sum.shape, jnp.float32)
    key_at = lax.broadcasted_iota(jnp.int32, (block, block), 0)
    query_at = lane_index((block, block))
    for b, j, diagonal in block_steps(meta_ref, blocks):
        rows = pl.ds(pl.multiple_of(b * block, block), block)
        keys = pl.ds(pl.multiple_of(j * (2 * block), 2 * block), 2 * block)
        key_rows = pl.ds(pl.multiple_of(j * block, block), block)
        stack_rows = pl.ds(pl.multiple_of(b * (4 * block), 4 * block), 4 * block)
        scores = dot_nt(key_s[keys, :], query_s[rows, :])
        share_grad = dot_nt(value_s[keys, :], grad_s[rows, :])
        shares_low = []
        score_low = []
        for g in range(2):
            at = slice(g * block, (g + 1) * block)
            shares = jnp.exp2(scores[at, :] * factor - rows_s[b, g : g + 1, :])
            if diagonal:
                shares = jnp.where(query_at >= key_at, shares, 0.0)
            shares_low.append(shares.astype(jnp.bfloat16))
            score_low.append(
                (shares * (share_grad[at, :] - rows_s[b, 2 + g : 3 + g, :])).astype(jnp.bfloat16)
            )
        keyval_sum[key_rows, :] += dot_nn(
            jnp.concatenate(score_low + shares_low, axis=1), stack_s[stack_rows, :]
        )
        query_sum[b] += dot_nn(turned_s[j], jnp.concatenate(score_low, axis=0))
    for b in range(2):
        context_s[b * block : (b + 1) * block, :] = query_sum[b].T * scale
    for s, cr, slot, row in places:
        query_out[cr, s, 0] = context_s[at_row(slot * block + row), :]
    weights = jnp.where(lane_index((piece, lanes)) < head_dim, scale, 1.0)
    for u, out_ref in enumerate((own_out, one_out, two_out, three_out)):
        for s, cr, slot, row in places:
            found = keyval_sum[at_row(meta_ref[2 * u + slot] * block + row), :] * weights
            out_ref[cr, s, 0] = found.astype(out_ref.dtype)


def by_sequence(width):
    return pl.BlockSpec((2, 4, 1, piece, width), lambda s: (0, 0, s, 0, 0))


def whole(shape):
    return pl.BlockSpec(shape, lambda s: (0,) * len(shape))


in_scalars = pl.BlockSpec(memory_space=pltpu.SMEM)


def five(width, dtype, sequences):
    return jax.ShapeDtypeStruct((2, 4, sequences, piece, width), dtype)


def prepare(raw, gain, cosine, sine):
    sequences = raw.shape[2]
    rows = cosine.shape[0]
    return pl.pallas_call(
        prepare_kernel,
        grid=(sequences,),
        in_specs=[
            by_sequence(2 * lanes), whole((1, 2 * lanes)), whole((rows, lanes)), whole((rows, lanes)),
        ],
        out_specs=[by_sequence(lanes), by_sequence(lanes)],
        out_shape=[five(lanes, jnp.bfloat16, sequences)] * 2,
        compiler_params=pltpu.CompilerParams(vmem_limit_bytes=24 * 2**20),
        cost_estimate=pl.CostEstimate(flops=10**8, bytes_accessed=2 * 10**6, transcendentals=0),
        name="prepare",
    )(raw, gain, cosine, sine)


def finish(raw, gain, cosine, sine, query_grad, keyval_parts):
    sequences = raw.shape[2]
    rows = cosine.shape[0]
    return pl.pallas_call(
        finish_kernel,
        grid=(sequences,),
        in_specs=[
            by_sequence(2 * lanes), whole((1, 2 * lanes)), whole((rows, lanes)), whole((rows, lanes)),
        ] + [by_sequence(lanes)] * 5,
        out_specs=[by_sequence(2 * lanes), whole((8, 2 * lanes))],
        out_shape=[
            five(2 * lanes, jnp.bfloat16, sequences),
            jax.ShapeDtypeStruct((8, 2 * lanes), jnp.float32),
        ],
        compiler_params=pltpu.CompilerParams(vmem_limit_bytes=24 * 2**20),
        cost_estimate=pl.CostEstimate(flops=10**8, bytes_accessed=4 * 10**6, transcendentals=0),
        name="finish",
    )(raw, gain, cosine, sine, query_grad, *keyval_parts)


def attend(meta, query, keyval_parts, scale):
    sequences = query.shape[2]
    keys = 4 * 8 * piece
    return pl.pallas_call(
        functools.partial(attend_kernel, scale * log2_e),
        grid=(sequences,),
        in_specs=[in_scalars] + [by_sequence(lanes)] * 5,
        out_specs=[by_sequence(lanes)] * 3,
        out_shape=[
            five(lanes, jnp.float32, sequences),
            five(lanes, jnp.bfloat16, sequences),
            five(lanes, jnp.float32, sequences),
        ],
        scratch_shapes=[
            pltpu.VMEM((2 * block, lanes), jnp.bfloat16),
            pltpu.VMEM((2 * keys, lanes), jnp.bfloat16),
            pltpu.VMEM((2 * keys, 2 * lanes), jnp.bfloat16),
            pltpu.VMEM((2 * block, 2 * lanes), jnp.float32),
        ],
        compiler_params=pltpu.CompilerParams(vmem_limit_bytes=24 * 2**20),
        cost_estimate=pl.CostEstimate(
            flops=2 * 10**9, bytes_accessed=4 * 10**6, transcendentals=2 * 10**6
        ),
        name="attend",
    )(meta, query, *keyval_parts)


def attend_back(meta, query, keyval_parts, context, total, grads, scale):
    sequences = query.shape[2]
    keys = 4 * 8 * piece
    blocks = keys // block
    return pl.pallas_call(
        functools.partial(attend_back_kernel, scale * log2_e, scale),
        grid=(sequences,),
        in_specs=[in_scalars] + [by_sequence(lanes)] * 8,
        out_specs=[by_sequence(lanes)] * 5,
        out_shape=[five(lanes, jnp.float32, sequences)] * 2
        + [five(lanes, jnp.bfloat16, sequences)] * 3,
        scratch_shapes=[
            pltpu.VMEM((2 * block, lanes), jnp.bfloat16),
            pltpu.VMEM((2 * block, lanes), jnp.bfloat16),
            pltpu.VMEM((2 * block, lanes), jnp.float32),
            pltpu.VMEM((2 * block, lanes), jnp.float32),
            pltpu.VMEM((8 * block, lanes), jnp.bfloat16),
            pltpu.VMEM((2 * keys, lanes), jnp.bfloat16),
            pltpu.VMEM((2 * keys, lanes), jnp.bfloat16),
            pltpu.VMEM((blocks, lanes, 2 * block), jnp.bfloat16),
            pltpu.VMEM((2, 8, block), jnp.float32),
            pltpu.VMEM((2, lanes, block), jnp.float32),
            pltpu.VMEM((keys, lanes), jnp.float32),
        ],
        compiler_params=pltpu.CompilerParams(vmem_limit_bytes=32 * 2**20),
        cost_estimate=pl.CostEstimate(
            flops=5 * 10**9, bytes_accessed=8 * 10**6, transcendentals=2 * 10**6
        ),
        name="attend_back",
    )(meta, query, *keyval_parts, context, total, grads)


def body(
    hidden_in,
    cotangent,
    block_order,
    query_weight,
    keyval_weight,
    output_weight,
    gate_weight,
    up_weight,
    down_weight,
    attn_gain,
    ffn_gain,
    query_gain,
    key_gain,
):
    sequences, _, own_rows, width = hidden_in.shape
    tensor_size = lax.axis_size("tensor")
    heads_size = lax.axis_size("heads")
    chips = heads_size // 2
    shard_rows = own_rows * heads_size
    all_rows = sequences * shard_rows
    units = gate_weight.shape[1]
    query_width = query_weight.shape[2]
    scale = head_dim ** (-0.5)
    rank = lax.axis_index("tensor")
    head_rank = lax.axis_index("heads")
    chip = head_rank // 2
    core = lax.rem(head_rank, 2)
    hidden_own = hidden_in[:, 0]
    cot_own = cotangent[:, 0]
    folded = (2, chips, sequences, own_rows)

    chip_at = lax.rem(chip - jnp.arange(chips, dtype=jnp.int32) + chips, chips)
    core_at = lax.rem(core + jnp.arange(2, dtype=jnp.int32), 2)
    head_at = chip_at[None, :] * 2 + core_at[:, None]
    row_at = (head_at[:, :, None] * own_rows + jnp.arange(own_rows, dtype=jnp.int32)).reshape(
        shard_rows
    )
    rank_at = lax.rem(rank - jnp.arange(tensor_size, dtype=jnp.int32) + tensor_size, tensor_size)
    order_at = block_order[rank_at]
    meta = jnp.concatenate([order_at.reshape(-1), chip[None], core[None]]).astype(jnp.int32)
    positions = (
        jnp.where(row_at >= block, order_at[0, 1], order_at[0, 0]) * block + lax.rem(row_at, block)
    )
    lane = jnp.arange(lanes, dtype=jnp.int32)
    freq = rope_base ** (
        -(lax.rem(lane, head_dim // 2).astype(jnp.float32) * 2.0 / head_dim)
    )
    angles = positions.astype(jnp.float32)[:, None] * freq[None, :]
    cosine = jnp.cos(angles)
    sine = jnp.sin(angles) * jnp.where(lax.rem(lane, head_dim) < head_dim // 2, -1.0, 1.0)[None, :]
    head_gain = jnp.concatenate(
        [query_gain, query_gain, key_gain, jnp.ones((head_dim,), jnp.float32)]
    )[None, :]

    feed_own = jnp.concatenate([gate_weight, up_weight, down_weight], axis=1)
    feed_all = lax.all_gather(feed_own, ("fsdp", "heads"), axis=0, tiled=True)
    gate_up_all = feed_all[:, : 2 * units]
    down_all = feed_all[:, 2 * units :]

    inputs = hidden_own.astype(jnp.float32)
    scale_one = rms_scale(inputs)
    normed_one = (inputs * scale_one * attn_gain).astype(jnp.bfloat16)
    rows_flat = gather_heads(normed_one).reshape(all_rows, width)
    attn_own = jnp.concatenate(
        [query_weight[:, 0], keyval_weight[:, 0], output_weight[:, 0]], axis=1
    )
    attn_all = place_ring(gather_ring(attn_own, "tensor"), "tensor")
    attn_all = place_ring(gather_ring(attn_all, "fsdp"), "fsdp").reshape(width, 3 * query_width)
    qkv_all = attn_all[:, : 2 * query_width]
    output_all = attn_all[:, 2 * query_width :]
    cot_flat = jnp.stack(gather_ring(cot_own, "tensor")).reshape(-1, width)

    qkv_raw = matmul(rows_flat, qkv_all).reshape(folded + (2 * query_width,))
    query_rot, keyval_rot = prepare(qkv_raw, head_gain, cosine, sine)
    keyval_rot, cot_flat = lax.optimization_barrier((keyval_rot, cot_flat))
    keyval_parts = gather_ring(keyval_rot, "tensor")
    context, context_low, total = attend(meta, query_rot, keyval_parts, scale)
    context_flat = context_low.reshape(all_rows, query_width)
    branch_part = contract_cols(context_flat, output_all).astype(jnp.bfloat16)
    branch = scatter_heads(branch_part.reshape(folded + (width,)))
    middle = inputs + branch
    scale_two = rms_scale(middle)
    normed_two = (middle * scale_two * ffn_gain).astype(jnp.bfloat16)
    two_flat = jnp.stack(gather_ring(normed_two, "tensor")).reshape(-1, width)
    gate_up = matmul(two_flat, gate_up_all)
    gate_value = gate_up[:, :units]
    upper_value = gate_up[:, units:]
    sigmoid_gate = jax.nn.sigmoid(gate_value)
    activated = gate_value * sigmoid_gate
    hidden = (activated * upper_value).astype(jnp.bfloat16)
    hidden_grad = matmul(cot_flat, down_all)
    gate_low = (
        hidden_grad * upper_value * sigmoid_gate * (1.0 + gate_value * (1.0 - sigmoid_gate))
    ).astype(jnp.bfloat16)
    upper_low = (hidden_grad * activated).astype(jnp.bfloat16)
    both_low = jnp.concatenate([gate_low, upper_low], axis=1)
    normed_two_part = contract_cols(both_low, gate_up_all).reshape(
        tensor_size, sequences, own_rows, width
    )
    normed_two_grad = scatter_tensor(normed_two_part.astype(jnp.bfloat16), normed_two_part[0])
    middle_norm_grad, ffn_terms = norm_back(middle, scale_two, ffn_gain, normed_two_grad)
    middle_grad = cot_own.astype(jnp.float32) + middle_norm_grad
    branch_low = middle_grad.astype(jnp.bfloat16)
    feed_part = contract_cols(hidden, down_all).reshape(tensor_size, sequences, own_rows, width)
    feed = scatter_tensor(feed_part.astype(jnp.bfloat16), feed_part[0])
    block_out = (middle + feed).astype(jnp.bfloat16)
    feed_grad = jnp.concatenate(
        [
            contract_rows(two_flat, both_low).astype(jnp.bfloat16),
            contract_rows(cot_flat, hidden).astype(jnp.bfloat16),
        ],
        axis=1,
    )
    feed_grad = lax.psum_scatter(
        feed_grad, ("fsdp", "heads"), scatter_dimension=0, tiled=True
    ).astype(jnp.float32)

    branch_flat = gather_heads(branch_low).reshape(all_rows, width)
    context_grad = matmul(branch_flat, output_all).astype(jnp.bfloat16)
    output_grad = contract_rows(branch_flat, context_flat)
    query_grad, own, one, two, three = attend_back(
        meta,
        query_rot,
        keyval_parts,
        context,
        total,
        context_grad.reshape(folded + (query_width,)),
        scale,
    )
    kv_moved = scatter_ring([own, one, two, three], "tensor")
    qkv_low, head_terms = finish(qkv_raw, head_gain, cosine, sine, query_grad, kv_moved)
    qkv_low = qkv_low.reshape(all_rows, 2 * query_width)
    normed_one_part = contract_cols(qkv_low, qkv_all).astype(jnp.bfloat16)
    normed_one_grad = scatter_heads(normed_one_part.reshape(folded + (width,)))
    qkv_grad = contract_rows(rows_flat, qkv_low)
    attn_gain_part = jnp.sum(qkv_grad * qkv_all.astype(jnp.float32), axis=1) / attn_gain
    head_terms = jnp.sum(head_terms, axis=0)
    gains = jnp.concatenate(
        [
            attn_gain_part,
            jnp.sum(ffn_terms, axis=(0, 1)),
            head_terms[:head_dim] + head_terms[head_dim : 2 * head_dim],
            head_terms[2 * head_dim : 3 * head_dim],
        ]
    )
    attn_grad = jnp.concatenate([qkv_grad, output_grad], axis=1)
    attn_grad, gains = scatter_rows(attn_grad, gains, "fsdp")
    attn_grad, gains = scatter_rows(attn_grad, gains, "tensor")
    gains = sum_four(gather_ring(gains, "z"))
    gains = gains + swap_core(gains)
    input_norm_grad, _ = norm_back(inputs, scale_one, attn_gain, normed_one_grad)
    input_grad = middle_grad + input_norm_grad
    return (
        block_out[:, None],
        input_grad[:, None],
        attn_grad[:, None, :query_width],
        attn_grad[:, None, query_width : 2 * query_width],
        attn_grad[:, None, 2 * query_width :],
        feed_grad[:, :units],
        feed_grad[:, units : 2 * units],
        feed_grad[:, 2 * units :],
        gains[:width],
        gains[width : 2 * width],
        gains[2 * width : 2 * width + head_dim],
        gains[2 * width + head_dim :],
    )


def solution(mesh):
    placed = (
        P("fsdp", "tensor", "heads", None),
        P("fsdp", "tensor", "heads", None),
        P(),
        P(("fsdp", "tensor"), "heads", None),
        P(("fsdp", "tensor"), "heads", None),
        P(("fsdp", "tensor"), "heads", None),
        P(("fsdp", "heads"), "tensor"),
        P(("fsdp", "heads"), "tensor"),
        P(("fsdp", "heads"), "tensor"),
        P(),
        P(),
        P(),
        P(),
    )
    return jax.shard_map(
        body,
        mesh=mesh,
        in_specs=placed,
        out_specs=(
            P("fsdp", "tensor", "heads", None),
            P("fsdp", "tensor", "heads", None),
            P(("fsdp", "tensor"), "heads", None),
            P(("fsdp", "tensor"), "heads", None),
            P(("fsdp", "tensor"), "heads", None),
            P(("fsdp", "heads"), "tensor"),
            P(("fsdp", "heads"), "tensor"),
            P(("fsdp", "heads"), "tensor"),
            P(),
            P(),
            P(),
            P(),
        ),
        check_vma=False,
    )
```

```python
import functools

import jax
import jax.numpy as jnp
from jax import lax
from jax.experimental import pallas as pl
from jax.experimental.pallas import tpu as pltpu
from jax.sharding import PartitionSpec as P

eps_norm = 1e-05
rope_base = 1000000.0
log2_e = 1.4426950408889634
block = 256
piece = 64
head_dim = 64
lanes = 128


def rms_scale(values):
    return lax.rsqrt(jnp.mean(values * values, axis=-1, keepdims=True) + eps_norm)


def norm_back(values, scale, gain, grads):
    scaled = grads * gain
    inner = jnp.mean(scaled * values, axis=-1, keepdims=True)
    return (scale * (scaled - values * scale * scale * inner), grads * values * scale)


def matmul(left, right):
    return jnp.dot(left, right, preferred_element_type=jnp.float32)


def contract_rows(left, right):
    return lax.dot_general(
        left, right, (((0,), (0,)), ((), ())), preferred_element_type=jnp.float32
    )


def contract_cols(left, right):
    return lax.dot_general(
        left, right, (((1,), (1,)), ((), ())), preferred_element_type=jnp.float32
    )


def sum_four(parts):
    return (parts[0] + parts[2]) + (parts[1] + parts[3])


def exchange(values, axis, mask):
    name = "heads" if axis in ("z", "core") else axis
    shift = 2 if axis == "z" else 1
    size = lax.axis_size(name)
    return lax.ppermute(values, name, [(i, i ^ (mask * shift)) for i in range(size)])


def swap_core(values):
    return exchange(values, "core", 1)


def gather_ring(values, axis):
    return [values] + [exchange(values, axis, m) for m in (1, 2, 3)]


def scatter_ring(parts, axis):
    return [parts[0]] + [exchange(parts[m], axis, m) for m in (1, 2, 3)]


def place_ring(parts, axis):
    size = lax.axis_size(axis)
    rank = lax.axis_index(axis)
    placed = jnp.zeros((size,) + parts[0].shape, parts[0].dtype)
    for s, part in enumerate(parts):
        placed = lax.dynamic_update_index_in_dim(placed, part, lax.bitwise_xor(rank, s), 0)
    return placed


def dot_nn(left, right):
    return lax.dot_general(
        left, right, (((1,), (0,)), ((), ())), preferred_element_type=jnp.float32
    )


def dot_nt(left, right):
    return lax.dot_general(
        left, right, (((1,), (1,)), ((), ())), preferred_element_type=jnp.float32
    )


def lane_index(shape):
    return lax.broadcasted_iota(jnp.int32, shape, 1)


def half_sums(values):
    rows = lax.broadcasted_iota(jnp.int32, (lanes, lanes), 0) // head_dim
    columns = lax.broadcasted_iota(jnp.int32, (lanes, lanes), 1) // head_dim
    ones = jnp.where(rows == columns, 1.0, 0.0).astype(jnp.float32)
    return lax.dot_general(
        values,
        ones,
        (((1,), (0,)), ((), ())),
        precision=lax.Precision.HIGHEST,
        preferred_element_type=jnp.float32,
    )


def turn_lanes(values):
    lane = lane_index(values.shape)
    up = pltpu.roll(values, lanes - head_dim // 2, 1)
    down = pltpu.roll(values, head_dim // 2, 1)
    return jnp.where(lax.rem(lane, head_dim) < head_dim // 2, up, down)


def rows_of(ref):
    return ref[...].reshape(ref.shape[0] * ref.shape[1] * ref.shape[3], ref.shape[4])


def prepare_kernel(raw_ref, gain_ref, cos_ref, sin_ref, query_ref, keyval_ref):
    raw = rows_of(raw_ref)
    cosine = cos_ref[...]
    sine = sin_ref[...]
    shape = query_ref.shape
    first = lane_index(cosine.shape) < head_dim
    for part, out_ref in ((0, query_ref), (1, keyval_ref)):
        values = raw[:, part * lanes : (part + 1) * lanes]
        scale = lax.rsqrt(half_sums(values * values) * (1.0 / head_dim) + eps_norm)
        normed = values * scale * gain_ref[:, part * lanes : (part + 1) * lanes]
        turned = normed * cosine + turn_lanes(normed) * sine
        if part == 1:
            turned = jnp.where(first, turned, values)
        out_ref[...] = turned.astype(jnp.bfloat16).reshape(shape)


def finish_kernel(
    raw_ref, gain_ref, cos_ref, sin_ref, query_ref, own_ref, one_ref, two_ref, three_ref,
    low_ref, terms_ref,
):
    raw = rows_of(raw_ref)
    cosine = cos_ref[...]
    sine = sin_ref[...]
    first = lane_index(cosine.shape) < head_dim
    keyval = (rows_of(own_ref) + rows_of(two_ref).astype(jnp.float32)) + (
        rows_of(one_ref).astype(jnp.float32) + rows_of(three_ref).astype(jnp.float32)
    )

    @pl.when(pl.program_id(0) == 0)
    def _():
        terms_ref[...] = jnp.zeros(terms_ref.shape, jnp.float32)

    for part, grads in ((0, rows_of(query_ref)), (1, keyval)):
        at = slice(part * lanes, (part + 1) * lanes)
        values = raw[:, at]
        scale = lax.rsqrt(half_sums(values * values) * (1.0 / head_dim) + eps_norm)
        turned = grads * cosine - turn_lanes(grads) * sine
        scaled = turned * gain_ref[:, at]
        inner = half_sums(scaled * values) * (1.0 / head_dim)
        back = scale * (scaled - values * scale * scale * inner)
        terms = turned * values * scale
        if part == 1:
            back = jnp.where(first, back, grads)
        terms_ref[:, at] += jnp.sum(terms.reshape(-1, 8, lanes), axis=0)
        low_ref[..., at] = back.astype(jnp.bfloat16).reshape(low_ref.shape[:-1] + (lanes,))


def row_places(meta_ref):
    chip = meta_ref[8]
    core = meta_ref[9]
    places = []
    for s in range(4):
        chip_at = lax.bitwise_xor(chip, s)
        for cr in range(2):
            core_at = lax.rem(core + cr, 2)
            slot = lax.div(chip_at, 2)
            row = lax.rem(chip_at, 2) * (2 * piece) + core_at * piece
            places.append((s, cr, slot, row))
    return places


def at_row(start, count=piece):
    return pl.ds(pl.multiple_of(start, piece), count)


def load_keys(places, meta_ref, keyval_refs, key_s, value_s, ones):
    lane = lane_index((piece, lanes))
    first = lane < head_dim
    none = jnp.zeros((piece, lanes), jnp.bfloat16)
    one = jnp.ones((piece, lanes), jnp.bfloat16)
    for u, keyval_ref in enumerate(keyval_refs):
        for s, cr, slot, row in places:
            values = keyval_ref[cr, s, 0]
            other = jnp.concatenate([values[:, head_dim:], values[:, :head_dim]], axis=1)
            start = meta_ref[2 * u + slot] * (2 * block) + row
            lower = at_row(start)
            upper = at_row(start + block)
            key_s[lower, :] = jnp.where(first, values, none)
            key_s[upper, :] = jnp.where(first, none, other)
            value_s[lower, :lanes] = jnp.where(first, other, none)
            value_s[upper, :lanes] = jnp.where(first, none, values)
            if ones:
                value_s[lower, lanes:] = jnp.where(first, one, none)
                value_s[upper, lanes:] = jnp.where(first, none, one)


def block_steps(meta_ref, blocks):
    first = meta_ref[0]
    steps = []
    for i in range(blocks - 1):
        early = i < first
        steps.append((jnp.where(early, 0, 1), jnp.where(early, i, i - first), False))
    steps.append((0, first, True))
    steps.append((1, meta_ref[1], True))
    return steps


def attend_kernel(
    factor, meta_ref, query_ref, own_ref, one_ref, two_ref, three_ref,
    context_ref, low_ref, total_ref, placed_ref, query_s, key_s, value_s, sum_s,
):
    places = row_places(meta_ref)
    load_keys(places, meta_ref, (own_ref, one_ref, two_ref, three_ref), key_s, value_s, True)
    for s, cr, slot, row in places:
        query_s[at_row(slot * block + row), :] = query_ref[cr, s, 0]
    sum_s[...] = jnp.zeros(sum_s.shape, jnp.float32)
    query_at = lax.broadcasted_iota(jnp.int32, (block, 2 * block), 0)
    key_at = lax.rem(lane_index((block, 2 * block)), block)
    for b, j, diagonal in block_steps(meta_ref, key_s.shape[0] // (2 * block)):
        rows = pl.ds(pl.multiple_of(b * block, block), block)
        keys = pl.ds(pl.multiple_of(j * (2 * block), 2 * block), 2 * block)
        raised = jnp.exp2(dot_nt(query_s[rows, :], key_s[keys, :]) * factor)
        if diagonal:
            raised = jnp.where(query_at >= key_at, raised, 0.0)
        sum_s[rows, :] += dot_nn(raised.astype(jnp.bfloat16), value_s[keys, :])
    for s, cr, slot, row in places:
        found = sum_s[at_row(slot * block + row), :]
        total = found[:, lanes:]
        context = found[:, :lanes] / total
        context_ref[cr, s, 0] = context
        low = context.astype(jnp.bfloat16)
        low_ref[cr, s, 0] = low
        head = lax.bitwise_xor(meta_ref[8], s) * 2 + lax.rem(meta_ref[9] + cr, 2)
        placed_ref[head, 0] = low
        total_ref[cr, s, 0] = total


def attend_back_kernel(
    factor, scale, meta_ref, query_ref, own_ref, one_ref, two_ref, three_ref,
    context_ref, total_ref, grad_ref,
    query_out, own_out, one_out, two_out, three_out,
    query_s, grad_s, context_s, total_s, stack_s, key_s, value_s, turned_s, rows_s, query_sum,
    keyval_sum,
):
    places = row_places(meta_ref)
    load_keys(places, meta_ref, (own_ref, one_ref, two_ref, three_ref), key_s, value_s, False)
    blocks = key_s.shape[0] // (2 * block)
    for j in range(blocks):
        turned_s[j] = key_s[j * 2 * block : (j + 1) * 2 * block, :].T
    for s, cr, slot, row in places:
        at = at_row(slot * block + row)
        query_s[at, :] = query_ref[cr, s, 0]
        grad_s[at, :] = grad_ref[cr, s, 0]
        context_s[at, :] = context_ref[cr, s, 0]
        total_s[at, :] = total_ref[cr, s, 0]
    first = lane_index((block, lanes)) < head_dim
    none = jnp.zeros((block, lanes), jnp.bfloat16)
    pick = lax.broadcasted_iota(jnp.int32, (8, lanes), 0)
    pick = jnp.where(pick == lane_index((8, lanes)) // head_dim, 1.0, 0.0).astype(jnp.float32)
    for b in range(2):
        at = slice(b * block, (b + 1) * block)
        query = query_s[at, :]
        grads = grad_s[at, :]
        other_query = jnp.concatenate([query[:, head_dim:], query[:, :head_dim]], axis=1)
        other_grads = jnp.concatenate([grads[:, head_dim:], grads[:, :head_dim]], axis=1)
        base = 4 * b * block
        stack_s[base : base + block, :] = jnp.where(first, query, none)
        stack_s[base + block : base + 2 * block, :] = jnp.where(first, other_query, none)
        stack_s[base + 2 * block : base + 3 * block, :] = jnp.where(first, none, other_grads)
        stack_s[base + 3 * block : base + 4 * block, :] = jnp.where(first, none, grads)
        inner = lax.dot_general(
            pick,
            grads.astype(jnp.float32) * context_s[at, :],
            (((1,), (1,)), ((), ())),
            precision=lax.Precision.HIGHEST,
            preferred_element_type=jnp.float32,
        )
        logs = jnp.log2(total_s[at, :]).T
        rows_s[b, 0:1, :] = logs[0:1, :]
        rows_s[b, 1:2, :] = logs[head_dim : head_dim + 1, :]
        rows_s[b, 2:4, :] = inner[0:2, :]
    query_sum[...] = jnp.zeros(query_sum.shape, jnp.float32)
    keyval_sum[...] = jnp.zeros(keyval_sum.shape, jnp.float32)
    key_at = lax.broadcasted_iota(jnp.int32, (block, block), 0)
    query_at = lane_index((block, block))
    for b, j, diagonal in block_steps(meta_ref, blocks):
        rows = pl.ds(pl.multiple_of(b * block, block), block)
        keys = pl.ds(pl.multiple_of(j * (2 * block), 2 * block), 2 * block)
        key_rows = pl.ds(pl.multiple_of(j * block, block), block)
        stack_rows = pl.ds(pl.multiple_of(b * (4 * block), 4 * block), 4 * block)
        scores = dot_nt(key_s[keys, :], query_s[rows, :])
        share_grad = dot_nt(value_s[keys, :], grad_s[rows, :])
        shares_low = []
        score_low = []
        for g in range(2):
            at = slice(g * block, (g + 1) * block)
            shares = jnp.exp2(scores[at, :] * factor - rows_s[b, g : g + 1, :])
            if diagonal:
                shares = jnp.where(query_at >= key_at, shares, 0.0)
            shares_low.append(shares.astype(jnp.bfloat16))
            score_low.append(
                (shares * (share_grad[at, :] - rows_s[b, 2 + g : 3 + g, :])).astype(jnp.bfloat16)
            )
        keyval_sum[key_rows, :] += dot_nn(
            jnp.concatenate(score_low + shares_low, axis=1), stack_s[stack_rows, :]
        )
        query_sum[b] += dot_nn(turned_s[j], jnp.concatenate(score_low, axis=0))
    for b in range(2):
        context_s[b * block : (b + 1) * block, :] = query_sum[b].T * scale
    for s, cr, slot, row in places:
        query_out[cr, s, 0] = context_s[at_row(slot * block + row), :]
    weights = jnp.where(lane_index((piece, lanes)) < head_dim, scale, 1.0)
    for u, out_ref in enumerate((own_out, one_out, two_out, three_out)):
        for s, cr, slot, row in places:
            found = keyval_sum[at_row(meta_ref[2 * u + slot] * block + row), :] * weights
            out_ref[cr, s, 0] = found.astype(out_ref.dtype)


near_x = ((0, 3, 1, 2), (0, 1, 3, 2))
near_z = ((0, 3), (1, 2))
part_rows = 32
chunk = 384


def feed_back_kernel(
    rank_ref, two_ref, cot_ref, low_ref, hidden_ref, weight_ref, other_ref, mine_ref, part_ref,
    turned_s, left_s, sum_s,
):
    step = pl.program_id(0)
    last = pl.num_programs(0) - 1
    first_down = pl.num_programs(0) * 2 // 3
    half = mine_ref.shape[0]

    @pl.when(step == 0)
    def _():
        for k, ref in enumerate((two_ref, cot_ref)):
            turned_s[...] = ref[...].T
            place = 0
            for c in range(2):
                for h in range(2):
                    for x in near_x[h]:
                        for z in near_z[h]:
                            found = (
                                lax.bitwise_xor(rank_ref[0], x) * 4
                                + lax.bitwise_xor(rank_ref[1], z)
                            ) * 2 + lax.bitwise_xor(rank_ref[2], c)
                            start = pl.multiple_of(found * part_rows, part_rows)
                            left_s[k, place : place + part_rows, :] = turned_s[
                                pl.ds(start, part_rows), :
                            ]
                            place += part_rows
        sum_s[...] = jnp.zeros(sum_s.shape, jnp.float32)

    def product(k, values):
        mine_ref[...] = dot_nn(left_s[k, :half, :], values).astype(jnp.bfloat16)
        other_ref[...] = dot_nn(left_s[k, half:, :], values).astype(jnp.bfloat16)

    @pl.when(step < first_down)
    def _():
        product(0, low_ref[...])

    @pl.when(step >= first_down)
    def _():
        hidden = hidden_ref[...]
        product(1, hidden)
        sum_s[...] += dot_nt(hidden, weight_ref[...])

    @pl.when(step == last)
    def _():
        rows = part_ref.shape[1]
        for s in range(4):
            part_ref[lax.bitwise_xor(rank_ref[3], s)] = sum_s[
                s * rows : (s + 1) * rows, :
            ].astype(jnp.bfloat16)


def feed_back_step(ranks, two, cotangent, low, hidden, weights):
    tokens, width = two.shape
    columns = weights.shape[1]
    steps = columns // chunk
    first_down = steps * 2 // 3
    half = width // 2

    def down_at(j):
        return jnp.maximum(j - first_down, 0)

    return pl.pallas_call(
        feed_back_kernel,
        grid=(steps,),
        in_specs=[
            in_scalars,
            whole((tokens, width)),
            whole((tokens, width)),
            pl.BlockSpec((tokens, chunk), lambda j: (0, jnp.minimum(j, first_down - 1))),
            pl.BlockSpec((tokens, chunk), lambda j: (0, down_at(j))),
            pl.BlockSpec((width, chunk), lambda j: (0, first_down + down_at(j))),
        ],
        out_specs=[
            pl.BlockSpec((half, chunk), lambda j: (0, j)),
            pl.BlockSpec((half, chunk), lambda j: (0, j)),
            whole((4, tokens // 4, width)),
        ],
        out_shape=[
            jax.ShapeDtypeStruct((half, columns), jnp.bfloat16),
            jax.ShapeDtypeStruct((half, columns), jnp.bfloat16),
            jax.ShapeDtypeStruct((4, tokens // 4, width), jnp.bfloat16),
        ],
        scratch_shapes=[
            pltpu.VMEM((width, tokens), jnp.bfloat16),
            pltpu.VMEM((2, width, tokens), jnp.bfloat16),
            pltpu.VMEM((tokens, width), jnp.float32),
        ],
        compiler_params=pltpu.CompilerParams(vmem_limit_bytes=56 * 2**20),
        cost_estimate=pl.CostEstimate(flops=10**8, bytes_accessed=10**5, transcendentals=0),
        name="feed_back_step",
    )(ranks, two, cotangent, low, hidden, weights)


def head_weight(refs, s, hr):
    return refs[s][...] if hr == 0 else refs[4][s]


def branch_kernel(
    hidden_ref, gain_ref, own_ref, one_ref, two_ref, three_ref, w_own, w_one, w_two,
    w_three, w_swap, middle_ref, normed_ref,
):
    weights = (w_own, w_one, w_two, w_three, w_swap)
    middle = hidden_ref[...].astype(jnp.float32)
    for s, context_ref in enumerate((own_ref, one_ref, two_ref, three_ref)):
        for hr in range(2):
            context = context_ref[:, hr * lanes : (hr + 1) * lanes]
            middle = middle + dot_nt(context, head_weight(weights, s, hr))
    middle_ref[...] = middle
    scale = lax.rsqrt(jnp.mean(middle * middle, axis=-1, keepdims=True) + eps_norm)
    normed_ref[...] = (middle * scale * gain_ref[...]).astype(jnp.bfloat16)


def branch_back_kernel(
    in_own, in_one, in_two, in_three, middle_ref, cot_ref, gain_ref, w_own, w_one, w_two,
    w_three, w_swap, grad_ref, low_ref, terms_ref, own_ref, one_ref, two_ref, three_ref,
):
    weights = (w_own, w_one, w_two, w_three, w_swap)
    parts = [ref[...].astype(jnp.float32) for ref in (in_own, in_one, in_two, in_three)]
    grads = (parts[0] + parts[2]) + (parts[1] + parts[3])
    middle = middle_ref[...]
    scale = lax.rsqrt(jnp.mean(middle * middle, axis=-1, keepdims=True) + eps_norm)
    back, terms = norm_back(middle, scale, gain_ref[...], grads)
    back = cot_ref[...].astype(jnp.float32) + back
    low = back.astype(jnp.bfloat16)
    grad_ref[...] = back
    low_ref[...] = low
    terms_ref[...] = jnp.sum(terms, axis=0, keepdims=True)
    for s, out_ref in enumerate((own_ref, one_ref, two_ref, three_ref)):
        for hr in range(2):
            out_ref[:, hr * lanes : (hr + 1) * lanes] = dot_nn(
                low, head_weight(weights, s, hr)
            ).astype(jnp.bfloat16)


gain_rows = 32


def send_pieces(rank, rows, pick, gains, out_refs):
    high = gains.astype(jnp.bfloat16)
    rest = (gains - high.astype(jnp.float32)).astype(jnp.bfloat16)
    for s, out_ref in enumerate(out_refs):
        start = pl.multiple_of(lax.bitwise_xor(rank, s) * rows, rows)
        for k in range(3):
            out_ref[k * rows : (k + 1) * rows, :] = pick(k, start).astype(out_ref.dtype)
        out_ref[3 * rows : 3 * rows + gain_rows, :] = high.astype(out_ref.dtype)
        out_ref[3 * rows + gain_rows :, :] = rest.astype(out_ref.dtype)


def sum_refs(refs, rows):
    parts = [ref[rows, :].astype(jnp.float32) for ref in refs]
    return (parts[0] + parts[2]) + (parts[1] + parts[3])


def first_stage_kernel(
    rank_ref, qkv_ref, output_ref, weight_ref, gain_ref, ffn_ref, head_ref,
    own_ref, one_ref, two_ref, three_ref, gain_s,
):
    products = qkv_ref[...] * weight_ref[...].astype(jnp.float32)
    ones = jnp.ones((8, products.shape[1]), jnp.float32)
    attn = lax.dot_general(
        ones,
        products,
        (((1,), (1,)), ((), ())),
        precision=lax.Precision.HIGHEST,
        preferred_element_type=jnp.float32,
    )[0:1, :] / gain_ref[...]
    ffn = ffn_ref[...]
    head = jnp.sum(head_ref[...], axis=0, keepdims=True)
    gain_s[...] = jnp.zeros(gain_s.shape, jnp.float32)
    count = attn.shape[1] // lanes
    for i in range(count):
        gain_s[i : i + 1, :] = attn[:, i * lanes : (i + 1) * lanes]
        gain_s[count + i : count + i + 1, :] = ffn[:, i * lanes : (i + 1) * lanes]
    gain_s[2 * count : 2 * count + 1, :] = head[:, :lanes]
    gain_s[2 * count + 1 : 2 * count + 2, :] = head[:, lanes:]
    rows = qkv_ref.shape[0] // 4

    def pick(k, start):
        if k == 2:
            return output_ref[pl.ds(start, rows), :]
        return qkv_ref[pl.ds(start, rows), k * lanes : (k + 1) * lanes]

    send_pieces(rank_ref[0], rows, pick, gain_s[...], (own_ref, one_ref, two_ref, three_ref))


def second_stage_kernel(
    rank_ref, in_own, in_one, in_two, in_three, own_ref, one_ref, two_ref, three_ref, sum_s,
):
    refs = (in_own, in_one, in_two, in_three)
    count = sum_s.shape[0]
    sum_s[...] = sum_refs(refs, slice(0, count))
    gains = sum_refs(refs, slice(count, count + gain_rows)) + sum_refs(
        refs, slice(count + gain_rows, count + 2 * gain_rows)
    )
    rows = count // 12

    def pick(k, start):
        return sum_s[pl.ds(pl.multiple_of(k * (4 * rows) + start, rows), rows), :]

    send_pieces(rank_ref[0], rows, pick, gains, (own_ref, one_ref, two_ref, three_ref))


def third_stage_kernel(
    in_own, in_one, in_two, in_three, query_ref, keyval_ref, output_ref, gain_ref,
):
    refs = (in_own, in_one, in_two, in_three)
    rows = query_ref.shape[0]
    for k, out_ref in enumerate((query_ref, keyval_ref, output_ref)):
        out_ref[...] = sum_refs(refs, slice(k * rows, (k + 1) * rows))
    gain_ref[...] = sum_refs(refs, slice(3 * rows, 3 * rows + gain_rows)) + sum_refs(
        refs, slice(3 * rows + gain_rows, 3 * rows + 2 * gain_rows)
    )


def blocks_of(arrays):
    return [whole(array.shape) for array in arrays]


def piece_shapes(rows):
    shape = (3 * rows + 2 * gain_rows, lanes)
    return [jax.ShapeDtypeStruct(shape, jnp.float32)] + [
        jax.ShapeDtypeStruct(shape, jnp.bfloat16)
    ] * 3


def branch_step(hidden, gain, contexts, weights):
    rows, width = hidden.shape
    operands = (hidden, gain, *contexts, *weights)
    shapes = [
        jax.ShapeDtypeStruct((rows, width), jnp.float32),
        jax.ShapeDtypeStruct((rows, width), jnp.bfloat16),
    ]
    return pl.pallas_call(
        branch_kernel,
        grid=(1,),
        in_specs=blocks_of(operands),
        out_specs=blocks_of(shapes),
        out_shape=shapes,
        compiler_params=pltpu.CompilerParams(vmem_limit_bytes=24 * 2**20),
        cost_estimate=pl.CostEstimate(
            flops=3 * 10**8, bytes_accessed=4 * 10**6, transcendentals=0
        ),
        name="branch_step",
    )(*operands)


def branch_back_step(parts, middle, cotangent, gain, weights):
    rows, width = middle.shape
    operands = (*parts, middle, cotangent, gain, *weights)
    shapes = [
        jax.ShapeDtypeStruct((rows, width), jnp.float32),
        jax.ShapeDtypeStruct((rows, width), jnp.bfloat16),
        jax.ShapeDtypeStruct((1, width), jnp.float32),
    ] + [jax.ShapeDtypeStruct((rows, 2 * lanes), jnp.bfloat16)] * 4
    return pl.pallas_call(
        branch_back_kernel,
        grid=(1,),
        in_specs=blocks_of(operands),
        out_specs=blocks_of(shapes),
        out_shape=shapes,
        compiler_params=pltpu.CompilerParams(vmem_limit_bytes=56 * 2**20),
        cost_estimate=pl.CostEstimate(
            flops=3 * 10**8, bytes_accessed=5 * 10**6, transcendentals=0
        ),
        name="branch_back_step",
    )(*operands)


def first_stage(rank, qkv_grad, output_grad, weight, gain, ffn, head):
    operands = (qkv_grad, output_grad, weight, gain, ffn, head)
    shapes = piece_shapes(qkv_grad.shape[0] // 4)
    return pl.pallas_call(
        first_stage_kernel,
        grid=(1,),
        in_specs=[in_scalars] + blocks_of(operands),
        out_specs=blocks_of(shapes),
        out_shape=shapes,
        scratch_shapes=[pltpu.VMEM((gain_rows, lanes), jnp.float32)],
        compiler_params=pltpu.CompilerParams(vmem_limit_bytes=24 * 2**20),
        cost_estimate=pl.CostEstimate(flops=10**7, bytes_accessed=3 * 10**6, transcendentals=0),
        name="first_stage",
    )(rank[None].astype(jnp.int32), *operands)


def second_stage(rank, parts):
    count = parts[0].shape[0] - 2 * gain_rows
    operands = tuple(parts)
    shapes = piece_shapes(count // 12)
    return pl.pallas_call(
        second_stage_kernel,
        grid=(1,),
        in_specs=[in_scalars] + blocks_of(operands),
        out_specs=blocks_of(shapes),
        out_shape=shapes,
        scratch_shapes=[pltpu.VMEM((count, lanes), jnp.float32)],
        compiler_params=pltpu.CompilerParams(vmem_limit_bytes=24 * 2**20),
        cost_estimate=pl.CostEstimate(flops=10**6, bytes_accessed=10**6, transcendentals=0),
        name="second_stage",
    )(rank[None].astype(jnp.int32), *operands)


def third_stage(parts):
    rows = (parts[0].shape[0] - 2 * gain_rows) // 3
    operands = tuple(parts)
    shapes = [jax.ShapeDtypeStruct((rows, lanes), jnp.float32)] * 3 + [
        jax.ShapeDtypeStruct((gain_rows, lanes), jnp.float32)
    ]
    return pl.pallas_call(
        third_stage_kernel,
        grid=(1,),
        in_specs=blocks_of(operands),
        out_specs=blocks_of(shapes),
        out_shape=shapes,
        compiler_params=pltpu.CompilerParams(vmem_limit_bytes=24 * 2**20),
        cost_estimate=pl.CostEstimate(flops=10**6, bytes_accessed=10**6, transcendentals=0),
        name="third_stage",
    )(*operands)


def by_sequence(width):
    return pl.BlockSpec((2, 4, 1, piece, width), lambda s: (0, 0, s, 0, 0))


def whole(shape):
    return pl.BlockSpec(shape, lambda s: (0,) * len(shape))


in_scalars = pl.BlockSpec(memory_space=pltpu.SMEM)


def five(width, dtype, sequences):
    return jax.ShapeDtypeStruct((2, 4, sequences, piece, width), dtype)


def prepare(raw, gain, cosine, sine):
    sequences = raw.shape[2]
    rows = cosine.shape[0]
    return pl.pallas_call(
        prepare_kernel,
        grid=(sequences,),
        in_specs=[
            by_sequence(2 * lanes), whole((1, 2 * lanes)), whole((rows, lanes)), whole((rows, lanes)),
        ],
        out_specs=[by_sequence(lanes), by_sequence(lanes)],
        out_shape=[five(lanes, jnp.bfloat16, sequences)] * 2,
        compiler_params=pltpu.CompilerParams(vmem_limit_bytes=24 * 2**20),
        cost_estimate=pl.CostEstimate(flops=10**8, bytes_accessed=2 * 10**6, transcendentals=0),
        name="prepare",
    )(raw, gain, cosine, sine)


def finish(raw, gain, cosine, sine, query_grad, keyval_parts):
    sequences = raw.shape[2]
    rows = cosine.shape[0]
    return pl.pallas_call(
        finish_kernel,
        grid=(sequences,),
        in_specs=[
            by_sequence(2 * lanes), whole((1, 2 * lanes)), whole((rows, lanes)), whole((rows, lanes)),
        ] + [by_sequence(lanes)] * 5,
        out_specs=[by_sequence(2 * lanes), whole((8, 2 * lanes))],
        out_shape=[
            five(2 * lanes, jnp.bfloat16, sequences),
            jax.ShapeDtypeStruct((8, 2 * lanes), jnp.float32),
        ],
        compiler_params=pltpu.CompilerParams(vmem_limit_bytes=24 * 2**20),
        cost_estimate=pl.CostEstimate(flops=10**8, bytes_accessed=4 * 10**6, transcendentals=0),
        name="finish",
    )(raw, gain, cosine, sine, query_grad, *keyval_parts)


def attend(meta, query, keyval_parts, scale):
    sequences = query.shape[2]
    keys = 4 * 8 * piece
    return pl.pallas_call(
        functools.partial(attend_kernel, scale * log2_e),
        grid=(sequences,),
        in_specs=[in_scalars] + [by_sequence(lanes)] * 5,
        out_specs=[by_sequence(lanes)] * 3
        + [pl.BlockSpec((8, 1, piece, lanes), lambda s: (0, s, 0, 0))],
        out_shape=[
            five(lanes, jnp.float32, sequences),
            five(lanes, jnp.bfloat16, sequences),
            five(lanes, jnp.float32, sequences),
            jax.ShapeDtypeStruct((8, sequences, piece, lanes), jnp.bfloat16),
        ],
        scratch_shapes=[
            pltpu.VMEM((2 * block, lanes), jnp.bfloat16),
            pltpu.VMEM((2 * keys, lanes), jnp.bfloat16),
            pltpu.VMEM((2 * keys, 2 * lanes), jnp.bfloat16),
            pltpu.VMEM((2 * block, 2 * lanes), jnp.float32),
        ],
        compiler_params=pltpu.CompilerParams(vmem_limit_bytes=24 * 2**20),
        cost_estimate=pl.CostEstimate(
            flops=2 * 10**9, bytes_accessed=4 * 10**6, transcendentals=2 * 10**6
        ),
        name="attend",
    )(meta, query, *keyval_parts)


def attend_back(meta, query, keyval_parts, context, total, grads, scale):
    sequences = query.shape[2]
    keys = 4 * 8 * piece
    blocks = keys // block
    return pl.pallas_call(
        functools.partial(attend_back_kernel, scale * log2_e, scale),
        grid=(sequences,),
        in_specs=[in_scalars] + [by_sequence(lanes)] * 8,
        out_specs=[by_sequence(lanes)] * 5,
        out_shape=[five(lanes, jnp.float32, sequences)] * 2
        + [five(lanes, jnp.bfloat16, sequences)] * 3,
        scratch_shapes=[
            pltpu.VMEM((2 * block, lanes), jnp.bfloat16),
            pltpu.VMEM((2 * block, lanes), jnp.bfloat16),
            pltpu.VMEM((2 * block, lanes), jnp.float32),
            pltpu.VMEM((2 * block, lanes), jnp.float32),
            pltpu.VMEM((8 * block, lanes), jnp.bfloat16),
            pltpu.VMEM((2 * keys, lanes), jnp.bfloat16),
            pltpu.VMEM((2 * keys, lanes), jnp.bfloat16),
            pltpu.VMEM((blocks, lanes, 2 * block), jnp.bfloat16),
            pltpu.VMEM((2, 8, block), jnp.float32),
            pltpu.VMEM((2, lanes, block), jnp.float32),
            pltpu.VMEM((keys, lanes), jnp.float32),
        ],
        compiler_params=pltpu.CompilerParams(vmem_limit_bytes=56 * 2**20),
        cost_estimate=pl.CostEstimate(
            flops=5 * 10**9, bytes_accessed=8 * 10**6, transcendentals=2 * 10**6
        ),
        name="attend_back",
    )(meta, query, *keyval_parts, context, total, grads)


def body(
    hidden_in,
    cotangent,
    block_order,
    query_weight,
    keyval_weight,
    output_weight,
    gate_weight,
    up_weight,
    down_weight,
    attn_gain,
    ffn_gain,
    query_gain,
    key_gain,
):
    sequences, _, own_rows, width = hidden_in.shape
    tensor_size = lax.axis_size("tensor")
    heads_size = lax.axis_size("heads")
    chips = heads_size // 2
    shard_rows = own_rows * heads_size
    all_rows = sequences * shard_rows
    units = gate_weight.shape[1]
    query_width = query_weight.shape[2]
    scale = head_dim ** (-0.5)
    rank = lax.axis_index("tensor")
    head_rank = lax.axis_index("heads")
    chip = head_rank // 2
    core = lax.rem(head_rank, 2)
    hidden_own = hidden_in[:, 0]
    cot_own = cotangent[:, 0]
    folded = (2, chips, sequences, own_rows)

    barrier = lax.optimization_barrier
    own_tokens = sequences * own_rows

    attn_own = jnp.concatenate(
        [query_weight[:, 0], keyval_weight[:, 0], output_weight[:, 0]], axis=1
    )
    attn_ring = gather_ring(attn_own, "tensor")
    inputs = hidden_own.astype(jnp.float32)
    scale_one = rms_scale(inputs)
    normed_one = (inputs * scale_one * attn_gain).astype(jnp.bfloat16)
    attn_ring[1], normed_one = barrier((attn_ring[1], normed_one))
    attn_y = place_ring(attn_ring, "tensor")
    attn_y, cot_own, block_order = barrier((attn_y, cot_own, block_order))
    attn_ring = gather_ring(attn_y, "fsdp")

    chip_at = chip ^ jnp.arange(chips, dtype=jnp.int32)
    core_at = lax.rem(core + jnp.arange(2, dtype=jnp.int32), 2)
    head_at = chip_at[None, :] * 2 + core_at[:, None]
    row_at = (head_at[:, :, None] * own_rows + jnp.arange(own_rows, dtype=jnp.int32)).reshape(
        shard_rows
    )
    rank_at = rank ^ jnp.arange(tensor_size, dtype=jnp.int32)
    order_at = block_order[rank_at]
    meta = jnp.concatenate([order_at.reshape(-1), chip[None], core[None]]).astype(jnp.int32)
    positions = (
        jnp.where(row_at >= block, order_at[0, 1], order_at[0, 0]) * block + lax.rem(row_at, block)
    )
    lane = jnp.arange(lanes, dtype=jnp.int32)
    freq = rope_base ** (
        -(lax.rem(lane, head_dim // 2).astype(jnp.float32) * 2.0 / head_dim)
    )
    angles = positions.astype(jnp.float32)[:, None] * freq[None, :]
    cosine = jnp.cos(angles)
    sine = jnp.sin(angles) * jnp.where(lax.rem(lane, head_dim) < head_dim // 2, -1.0, 1.0)[None, :]
    head_gain = jnp.concatenate(
        [query_gain, query_gain, key_gain, jnp.ones((head_dim,), jnp.float32)]
    )[None, :]
    rows_ring, attn_ring, meta, cosine, sine, head_gain = barrier(
        (gather_ring(normed_one, "z"), attn_ring, meta, cosine, sine, head_gain)
    )
    attn_all = place_ring(attn_ring, "fsdp").reshape(width, 3 * query_width)
    qkv_all = attn_all[:, : 2 * query_width]
    output_all = attn_all[:, 2 * query_width :]
    rows_own = jnp.stack(rows_ring)
    rows_halves = [rows_own.reshape(-1, width), swap_core(rows_own).reshape(-1, width)]
    rows_flat = jnp.concatenate(rows_halves)

    feed_own = jnp.concatenate([gate_weight, up_weight, down_weight], axis=1)
    feed_all = lax.all_gather(feed_own, ("fsdp", "heads"), axis=0, tiled=True)
    gate_up_all = feed_all[:, : 2 * units]
    down_all = feed_all[:, 2 * units :]

    qkv_raw = matmul(rows_flat, qkv_all).reshape(folded + (2 * query_width,))
    query_rot, keyval_rot = prepare(qkv_raw, head_gain, cosine, sine)
    output_ring = gather_ring(output_all, "z")
    cot_one = exchange(cot_own, "tensor", 1)
    keyval_rot, cot_one = barrier((keyval_rot, cot_one))
    keyval_parts = gather_ring(keyval_rot, "tensor")

    cot_two = jnp.stack([cot_own, cot_one])
    keyval_parts, cot_two, output_ring = barrier((keyval_parts, cot_two, output_ring))
    cot_three = exchange(cot_two, "tensor", 3)

    context, context_low, total, context_placed = attend(meta, query_rot, keyval_parts, scale)
    core_rows = (chips, own_tokens, query_width)
    context_swap = swap_core(context_low[1].reshape(core_rows))
    context_pairs = jnp.concatenate([context_low[0].reshape(core_rows), context_swap], axis=2)
    contexts = scatter_ring([context_pairs[s] for s in range(chips)], "z")
    weights = (*output_ring, swap_core(jnp.stack(output_ring)))
    middle, normed_two = branch_step(
        hidden_own.reshape(own_tokens, width), ffn_gain[None, :], contexts, weights
    )
    normed_two, cot_three = barrier((normed_two, cot_three))
    two_ring = gather_ring(normed_two, "tensor")
    cot_flat = jnp.stack([cot_two[0], cot_two[1], cot_three[1], cot_three[0]]).reshape(-1, width)
    hidden_grad = matmul(cot_flat, down_all)
    two_ring, hidden_grad = barrier((two_ring, hidden_grad))
    two_flat = jnp.stack(two_ring).reshape(-1, width)
    gate_up = matmul(two_flat, gate_up_all)
    gate_value = gate_up[:, :units]
    upper_value = gate_up[:, units:]
    sigmoid_gate = jax.nn.sigmoid(gate_value)
    activated = gate_value * sigmoid_gate
    hidden = (activated * upper_value).astype(jnp.bfloat16)
    gate_low = (
        hidden_grad * upper_value * sigmoid_gate * (1.0 + gate_value * (1.0 - sigmoid_gate))
    ).astype(jnp.bfloat16)
    upper_low = (hidden_grad * activated).astype(jnp.bfloat16)
    both_low = jnp.concatenate([gate_low, upper_low], axis=1)
    two_part = contract_cols(both_low, gate_up_all).astype(jnp.bfloat16)
    two_moved = scatter_ring(
        [two_part[s * own_tokens : (s + 1) * own_tokens] for s in range(tensor_size)], "tensor"
    )

    x_rank = lax.axis_index("fsdp")
    quarter = width // 4
    eighth = width // 8
    ranks = jnp.stack([x_rank, chip, core, rank]).astype(jnp.int32)
    feed_other, feed_mine, feed_part = feed_back_step(
        ranks, two_flat, cot_flat, both_low, hidden, feed_all
    )
    two_moved, feed_other, feed_mine, feed_part = barrier(
        (two_moved, feed_other, feed_mine, feed_part)
    )
    feed_sum = swap_core(feed_other) + feed_mine
    feed = lax.psum_scatter(feed_part, "tensor", scatter_dimension=0, tiled=True)

    middle_grad, branch_low, ffn_row, *grad_pairs = branch_back_step(
        two_moved,
        middle,
        cot_own.reshape(own_tokens, width),
        ffn_gain[None, :],
        weights,
    )
    branch_all = lax.all_gather(branch_low.reshape(sequences, own_rows, width), "heads")
    grad_moved = scatter_ring(grad_pairs, "z")
    grad_moved, feed_sum = barrier((grad_moved, feed_sum))
    sent_a = exchange(feed_sum[eighth:quarter], "fsdp", 1)
    sent_b = exchange(feed_sum[quarter + eighth :], "fsdp", 3)
    grad_moved = jnp.stack(grad_moved)
    context_grad = jnp.stack(
        [grad_moved[..., :query_width], swap_core(grad_moved[..., query_width:])]
    ).reshape(folded + (query_width,))
    context_grad, feed = barrier((context_grad, feed))
    query_grad, own, one, two, three = attend_back(
        meta, query_rot, keyval_parts, context, total, context_grad, scale
    )
    block_out = (middle + feed[0].astype(jnp.float32)).astype(jnp.bfloat16)
    kv_moved = scatter_ring([own, one, two, three], "tensor")
    kv_moved[1], sent_a, sent_b = barrier((kv_moved[1], sent_a, sent_b))
    sum_a = feed_sum[:eighth].astype(jnp.float32) + sent_a.astype(jnp.float32)
    sum_b = feed_sum[quarter : quarter + eighth].astype(jnp.float32) + sent_b.astype(jnp.float32)
    row_half = eighth // 2
    last_a = exchange(sum_a[row_half:].astype(jnp.bfloat16), "fsdp", 3)
    last_b = exchange(sum_b[row_half:].astype(jnp.bfloat16), "fsdp", 1)
    output_grad = contract_rows(
        branch_all.reshape(all_rows, width), context_placed.reshape(all_rows, query_width)
    )

    qkv_low, head_terms = finish(qkv_raw, head_gain, cosine, sine, query_grad, kv_moved)
    qkv_low, output_grad = barrier((qkv_low, output_grad))
    qkv_low = qkv_low.reshape(all_rows, 2 * query_width)
    one_part = contract_cols(qkv_low, qkv_all).astype(jnp.bfloat16)
    one_part, qkv_low = barrier((one_part.reshape(folded + (width,)), qkv_low))
    one_swap = swap_core(one_part[1])
    half_rows = all_rows // 2
    qkv_grad = contract_rows(rows_halves[0], qkv_low[:half_rows]) + contract_rows(
        rows_halves[1], qkv_low[half_rows:]
    )
    attn_pieces = first_stage(
        x_rank, qkv_grad, output_grad, qkv_all, attn_gain[None, :], ffn_row, head_terms
    )
    one_sum = one_part[0].astype(jnp.float32) + one_swap.astype(jnp.float32)
    attn_pieces, one_sum = barrier((attn_pieces, one_sum))
    one_sent = exchange(jnp.stack([one_sum[1], one_sum[2]]).astype(jnp.bfloat16), "z", 1)
    attn_moved = scatter_ring(attn_pieces, "fsdp")
    attn_moved, last_a, last_b = barrier((attn_moved, last_a, last_b))
    z_sent = (sum_b[:row_half] + last_b.astype(jnp.float32)).astype(jnp.bfloat16)
    z_sent = exchange(z_sent, "z", 1)
    attn_pieces = second_stage(rank, attn_moved)
    attn_moved = scatter_ring(attn_pieces, "tensor")
    attn_moved, one_sent = barrier((attn_moved, one_sent))
    query_out, keyval_out, output_out, gains = third_stage(attn_moved)
    gains = gains + swap_core(gains)
    one_far = (one_sum[3] + one_sent[1].astype(jnp.float32)).astype(jnp.bfloat16)
    one_far = exchange(one_far, "z", 3)
    gains, z_sent = barrier((gains, z_sent))
    z_sum = (
        sum_a[:row_half] + last_a.astype(jnp.float32) + z_sent.astype(jnp.float32)
    )
    z_last = exchange(z_sum[part_rows:].astype(jnp.bfloat16), "z", 3)
    gains = gains + exchange(gains, "z", 1)
    gains, one_far = barrier((gains, one_far))
    gains = gains + exchange(gains, "z", 3)
    gains, z_last = barrier((gains, z_last))
    feed_grad = z_sum[:part_rows] + z_last.astype(jnp.float32)
    normed_one_grad = one_sum[0] + one_sent[0].astype(jnp.float32) + one_far.astype(jnp.float32)
    input_norm_grad, _ = norm_back(inputs, scale_one, attn_gain, normed_one_grad)
    input_grad = middle_grad.reshape(inputs.shape) + input_norm_grad
    gain_at = width // lanes
    return (
        block_out.reshape(hidden_in.shape),
        input_grad[:, None],
        query_out[:, None],
        keyval_out[:, None],
        output_out[:, None],
        feed_grad[:, :units],
        feed_grad[:, units : 2 * units],
        feed_grad[:, 2 * units :],
        gains[:gain_at].reshape(width),
        gains[gain_at : 2 * gain_at].reshape(width),
        gains[2 * gain_at, :head_dim] + gains[2 * gain_at, head_dim:],
        gains[2 * gain_at + 1, :head_dim],
    )


def solution(mesh):
    placed = (
        P("fsdp", "tensor", "heads", None),
        P("fsdp", "tensor", "heads", None),
        P(),
        P(("fsdp", "tensor"), "heads", None),
        P(("fsdp", "tensor"), "heads", None),
        P(("fsdp", "tensor"), "heads", None),
        P(("fsdp", "heads"), "tensor"),
        P(("fsdp", "heads"), "tensor"),
        P(("fsdp", "heads"), "tensor"),
        P(),
        P(),
        P(),
        P(),
    )
    return jax.shard_map(
        body,
        mesh=mesh,
        in_specs=placed,
        out_specs=(
            P("fsdp", "tensor", "heads", None),
            P("fsdp", "tensor", "heads", None),
            P(("fsdp", "tensor"), "heads", None),
            P(("fsdp", "tensor"), "heads", None),
            P(("fsdp", "tensor"), "heads", None),
            P(("fsdp", "heads"), "tensor"),
            P(("fsdp", "heads"), "tensor"),
            P(("fsdp", "heads"), "tensor"),
            P(),
            P(),
            P(),
            P(),
        ),
        check_vma=False,
    )
```

```python
import functools

import jax
import jax.numpy as jnp
from jax import lax
from jax.experimental import pallas as pl
from jax.experimental.pallas import tpu as pltpu
from jax.sharding import PartitionSpec as P

eps_norm = 1e-05
rope_base = 1000000.0
log2_e = 1.4426950408889634
block = 256
piece = 64
head_dim = 64
lanes = 128


def rms_scale(values):
    return lax.rsqrt(jnp.mean(values * values, axis=-1, keepdims=True) + eps_norm)


def norm_back(values, scale, gain, grads):
    scaled = grads * gain
    inner = jnp.mean(scaled * values, axis=-1, keepdims=True)
    return (scale * (scaled - values * scale * scale * inner), grads * values * scale)


def matmul(left, right):
    return jnp.dot(left, right, preferred_element_type=jnp.float32)


def contract_rows(left, right):
    return lax.dot_general(
        left, right, (((0,), (0,)), ((), ())), preferred_element_type=jnp.float32
    )


def contract_cols(left, right):
    return lax.dot_general(
        left, right, (((1,), (1,)), ((), ())), preferred_element_type=jnp.float32
    )


def sum_four(parts):
    return (parts[0] + parts[2]) + (parts[1] + parts[3])


def exchange(values, axis, mask):
    name = "heads" if axis in ("z", "core") else axis
    shift = 2 if axis == "z" else 1
    size = lax.axis_size(name)
    return lax.ppermute(values, name, [(i, i ^ (mask * shift)) for i in range(size)])


def swap_core(values):
    return exchange(values, "core", 1)


def gather_ring(values, axis):
    return [values] + [exchange(values, axis, m) for m in (1, 2, 3)]


def scatter_ring(parts, axis):
    return [parts[0]] + [exchange(parts[m], axis, m) for m in (1, 2, 3)]


def place_ring(parts, axis):
    size = lax.axis_size(axis)
    rank = lax.axis_index(axis)
    placed = jnp.zeros((size,) + parts[0].shape, parts[0].dtype)
    for s, part in enumerate(parts):
        placed = lax.dynamic_update_index_in_dim(placed, part, lax.bitwise_xor(rank, s), 0)
    return placed


def dot_nn(left, right):
    return lax.dot_general(
        left, right, (((1,), (0,)), ((), ())), preferred_element_type=jnp.float32
    )


def dot_nt(left, right):
    return lax.dot_general(
        left, right, (((1,), (1,)), ((), ())), preferred_element_type=jnp.float32
    )


def lane_index(shape):
    return lax.broadcasted_iota(jnp.int32, shape, 1)


def half_sums(values):
    rows = lax.broadcasted_iota(jnp.int32, (lanes, lanes), 0) // head_dim
    columns = lax.broadcasted_iota(jnp.int32, (lanes, lanes), 1) // head_dim
    ones = jnp.where(rows == columns, 1.0, 0.0).astype(jnp.float32)
    return lax.dot_general(
        values,
        ones,
        (((1,), (0,)), ((), ())),
        precision=lax.Precision.HIGHEST,
        preferred_element_type=jnp.float32,
    )


def turn_lanes(values):
    lane = lane_index(values.shape)
    up = pltpu.roll(values, lanes - head_dim // 2, 1)
    down = pltpu.roll(values, head_dim // 2, 1)
    return jnp.where(lax.rem(lane, head_dim) < head_dim // 2, up, down)


def rows_of(ref):
    return ref[...].reshape(ref.shape[0] * ref.shape[1] * ref.shape[3], ref.shape[4])


def project_kernel(
    rank_ref, own_ref, swap_ref, w_own, w_one, w_two, w_three, gain_ref, cos_ref, sin_ref,
    raw_ref, query_ref, keyval_ref,
):
    halves = []
    for rows_ref in (own_ref, swap_ref):
        total = None
        for s, w_ref in enumerate((w_own, w_one, w_two, w_three)):
            depth = w_ref.shape[0] * w_ref.shape[1]
            start = pl.multiple_of(lax.bitwise_xor(rank_ref[0], s) * depth, depth)
            rows = rows_ref[:, 0, :, pl.ds(start, depth)].reshape(-1, depth)
            weight = w_ref[...].reshape(depth, w_ref.shape[2])[:, : 2 * lanes]
            part = dot_nn(rows, weight)
            total = part if total is None else total + part
        halves.append(total)
    raw = jnp.concatenate(halves)
    raw_ref[...] = raw.reshape(raw_ref.shape)
    cosine = cos_ref[...]
    sine = sin_ref[...]
    shape = query_ref.shape
    first = lane_index(cosine.shape) < head_dim
    for part, out_ref in ((0, query_ref), (1, keyval_ref)):
        values = raw[:, part * lanes : (part + 1) * lanes]
        scale = lax.rsqrt(half_sums(values * values) * (1.0 / head_dim) + eps_norm)
        normed = values * scale * gain_ref[:, part * lanes : (part + 1) * lanes]
        turned = normed * cosine + turn_lanes(normed) * sine
        if part == 1:
            turned = jnp.where(first, turned, values)
        out_ref[...] = turned.astype(jnp.bfloat16).reshape(shape)


def finish_kernel(
    raw_ref, gain_ref, cos_ref, sin_ref, query_ref, own_ref, one_ref, two_ref, three_ref,
    low_ref, terms_ref,
):
    raw = rows_of(raw_ref)
    cosine = cos_ref[...]
    sine = sin_ref[...]
    first = lane_index(cosine.shape) < head_dim
    keyval = (rows_of(own_ref) + rows_of(two_ref).astype(jnp.float32)) + (
        rows_of(one_ref).astype(jnp.float32) + rows_of(three_ref).astype(jnp.float32)
    )

    @pl.when(pl.program_id(0) == 0)
    def _():
        terms_ref[...] = jnp.zeros(terms_ref.shape, jnp.float32)

    for part, grads in ((0, rows_of(query_ref)), (1, keyval)):
        at = slice(part * lanes, (part + 1) * lanes)
        values = raw[:, at]
        scale = lax.rsqrt(half_sums(values * values) * (1.0 / head_dim) + eps_norm)
        turned = grads * cosine - turn_lanes(grads) * sine
        scaled = turned * gain_ref[:, at]
        inner = half_sums(scaled * values) * (1.0 / head_dim)
        back = scale * (scaled - values * scale * scale * inner)
        terms = turned * values * scale
        if part == 1:
            back = jnp.where(first, back, grads)
        terms_ref[:, at] += jnp.sum(terms.reshape(-1, 8, lanes), axis=0)
        low_ref[..., at] = back.astype(jnp.bfloat16).reshape(low_ref.shape[:-1] + (lanes,))


def row_places(meta_ref):
    chip = meta_ref[8]
    core = meta_ref[9]
    places = []
    for s in range(4):
        chip_at = lax.bitwise_xor(chip, s)
        for cr in range(2):
            core_at = lax.rem(core + cr, 2)
            slot = lax.div(chip_at, 2)
            row = lax.rem(chip_at, 2) * (2 * piece) + core_at * piece
            places.append((s, cr, slot, row))
    return places


def at_row(start, count=piece):
    return pl.ds(pl.multiple_of(start, piece), count)


def load_keys(places, meta_ref, keyval_refs, key_s, value_s, ones):
    lane = lane_index((piece, lanes))
    first = lane < head_dim
    none = jnp.zeros((piece, lanes), jnp.bfloat16)
    one = jnp.ones((piece, lanes), jnp.bfloat16)
    for u, keyval_ref in enumerate(keyval_refs):
        for s, cr, slot, row in places:
            values = keyval_ref[cr, s, 0]
            other = jnp.concatenate([values[:, head_dim:], values[:, :head_dim]], axis=1)
            start = meta_ref[2 * u + slot] * (2 * block) + row
            lower = at_row(start)
            upper = at_row(start + block)
            key_s[lower, :] = jnp.where(first, values, none)
            key_s[upper, :] = jnp.where(first, none, other)
            value_s[lower, :lanes] = jnp.where(first, other, none)
            value_s[upper, :lanes] = jnp.where(first, none, values)
            if ones:
                value_s[lower, lanes:] = jnp.where(first, one, none)
                value_s[upper, lanes:] = jnp.where(first, none, one)


def block_steps(meta_ref, blocks):
    first = meta_ref[0]
    steps = []
    for i in range(blocks - 1):
        early = i < first
        steps.append((jnp.where(early, 0, 1), jnp.where(early, i, i - first), False))
    steps.append((0, first, True))
    steps.append((1, meta_ref[1], True))
    return steps


def attend_kernel(
    factor, meta_ref, query_ref, own_ref, one_ref, two_ref, three_ref,
    context_ref, low_ref, total_ref, placed_ref, query_s, key_s, value_s, sum_s,
):
    places = row_places(meta_ref)
    load_keys(places, meta_ref, (own_ref, one_ref, two_ref, three_ref), key_s, value_s, True)
    for s, cr, slot, row in places:
        query_s[at_row(slot * block + row), :] = query_ref[cr, s, 0]
    sum_s[...] = jnp.zeros(sum_s.shape, jnp.float32)
    query_at = lax.broadcasted_iota(jnp.int32, (block, 2 * block), 0)
    key_at = lax.rem(lane_index((block, 2 * block)), block)
    for b, j, diagonal in block_steps(meta_ref, key_s.shape[0] // (2 * block)):
        rows = pl.ds(pl.multiple_of(b * block, block), block)
        keys = pl.ds(pl.multiple_of(j * (2 * block), 2 * block), 2 * block)
        raised = jnp.exp2(dot_nt(query_s[rows, :], key_s[keys, :]) * factor)
        if diagonal:
            raised = jnp.where(query_at >= key_at, raised, 0.0)
        sum_s[rows, :] += dot_nn(raised.astype(jnp.bfloat16), value_s[keys, :])
    for s, cr, slot, row in places:
        found = sum_s[at_row(slot * block + row), :]
        total = found[:, lanes:]
        context = found[:, :lanes] / total
        context_ref[cr, s, 0] = context
        low = context.astype(jnp.bfloat16)
        low_ref[cr, s, 0] = low
        head = lax.bitwise_xor(meta_ref[8], s) * 2 + lax.rem(meta_ref[9] + cr, 2)
        placed_ref[head, 0] = low
        total_ref[cr, s, 0] = total


def attend_back_kernel(
    factor, scale, meta_ref, query_ref, own_ref, one_ref, two_ref, three_ref,
    context_ref, total_ref, grad_ref,
    query_out, own_out, one_out, two_out, three_out,
    query_s, grad_s, context_s, total_s, stack_s, key_s, value_s, turned_s, rows_s, query_sum,
    keyval_sum,
):
    places = row_places(meta_ref)
    load_keys(places, meta_ref, (own_ref, one_ref, two_ref, three_ref), key_s, value_s, False)
    blocks = key_s.shape[0] // (2 * block)
    for j in range(blocks):
        turned_s[j] = key_s[j * 2 * block : (j + 1) * 2 * block, :].T
    for s, cr, slot, row in places:
        at = at_row(slot * block + row)
        query_s[at, :] = query_ref[cr, s, 0]
        grad_s[at, :] = grad_ref[cr, s, 0]
        context_s[at, :] = context_ref[cr, s, 0]
        total_s[at, :] = total_ref[cr, s, 0]
    first = lane_index((block, lanes)) < head_dim
    none = jnp.zeros((block, lanes), jnp.bfloat16)
    pick = lax.broadcasted_iota(jnp.int32, (8, lanes), 0)
    pick = jnp.where(pick == lane_index((8, lanes)) // head_dim, 1.0, 0.0).astype(jnp.float32)
    for b in range(2):
        at = slice(b * block, (b + 1) * block)
        query = query_s[at, :]
        grads = grad_s[at, :]
        other_query = jnp.concatenate([query[:, head_dim:], query[:, :head_dim]], axis=1)
        other_grads = jnp.concatenate([grads[:, head_dim:], grads[:, :head_dim]], axis=1)
        base = 4 * b * block
        stack_s[base : base + block, :] = jnp.where(first, query, none)
        stack_s[base + block : base + 2 * block, :] = jnp.where(first, other_query, none)
        stack_s[base + 2 * block : base + 3 * block, :] = jnp.where(first, none, other_grads)
        stack_s[base + 3 * block : base + 4 * block, :] = jnp.where(first, none, grads)
        inner = lax.dot_general(
            pick,
            grads.astype(jnp.float32) * context_s[at, :],
            (((1,), (1,)), ((), ())),
            precision=lax.Precision.HIGHEST,
            preferred_element_type=jnp.float32,
        )
        logs = jnp.log2(total_s[at, :]).T
        rows_s[b, 0:1, :] = logs[0:1, :]
        rows_s[b, 1:2, :] = logs[head_dim : head_dim + 1, :]
        rows_s[b, 2:4, :] = inner[0:2, :]
    query_sum[...] = jnp.zeros(query_sum.shape, jnp.float32)
    keyval_sum[...] = jnp.zeros(keyval_sum.shape, jnp.float32)
    key_at = lax.broadcasted_iota(jnp.int32, (block, block), 0)
    query_at = lane_index((block, block))
    for b, j, diagonal in block_steps(meta_ref, blocks):
        rows = pl.ds(pl.multiple_of(b * block, block), block)
        keys = pl.ds(pl.multiple_of(j * (2 * block), 2 * block), 2 * block)
        key_rows = pl.ds(pl.multiple_of(j * block, block), block)
        stack_rows = pl.ds(pl.multiple_of(b * (4 * block), 4 * block), 4 * block)
        scores = dot_nt(key_s[keys, :], query_s[rows, :])
        share_grad = dot_nt(value_s[keys, :], grad_s[rows, :])
        shares_low = []
        score_low = []
        for g in range(2):
            at = slice(g * block, (g + 1) * block)
            shares = jnp.exp2(scores[at, :] * factor - rows_s[b, g : g + 1, :])
            if diagonal:
                shares = jnp.where(query_at >= key_at, shares, 0.0)
            shares_low.append(shares.astype(jnp.bfloat16))
            score_low.append(
                (shares * (share_grad[at, :] - rows_s[b, 2 + g : 3 + g, :])).astype(jnp.bfloat16)
            )
        keyval_sum[key_rows, :] += dot_nn(
            jnp.concatenate(score_low + shares_low, axis=1), stack_s[stack_rows, :]
        )
        query_sum[b] += dot_nn(turned_s[j], jnp.concatenate(score_low, axis=0))
    for b in range(2):
        context_s[b * block : (b + 1) * block, :] = query_sum[b].T * scale
    for s, cr, slot, row in places:
        query_out[cr, s, 0] = context_s[at_row(slot * block + row), :]
    weights = jnp.where(lane_index((piece, lanes)) < head_dim, scale, 1.0)
    for u, out_ref in enumerate((own_out, one_out, two_out, three_out)):
        for s, cr, slot, row in places:
            found = keyval_sum[at_row(meta_ref[2 * u + slot] * block + row), :] * weights
            out_ref[cr, s, 0] = found.astype(out_ref.dtype)


near_x = ((0, 3, 1, 2), (0, 1, 3, 2))
near_z = ((0, 3), (1, 2))
part_rows = 32
chunk = 384


def feed_back_kernel(
    rank_ref, two_ref, cot_ref, gate_ref, upper_ref, hidden_ref, weight_ref, other_ref, mine_ref, part_ref,
    turned_s, left_s, sum_s,
):
    step = pl.program_id(0)
    last = pl.num_programs(0) - 1
    first_down = pl.num_programs(0) * 2 // 3
    half = mine_ref.shape[0]

    @pl.when(step == 0)
    def _():
        for k, ref in enumerate((two_ref, cot_ref)):
            turned_s[...] = ref[...].T
            place = 0
            for c in range(2):
                for h in range(2):
                    for x in near_x[h]:
                        for z in near_z[h]:
                            found = (
                                lax.bitwise_xor(rank_ref[0], x) * 4
                                + lax.bitwise_xor(rank_ref[1], z)
                            ) * 2 + lax.bitwise_xor(rank_ref[2], c)
                            start = pl.multiple_of(found * part_rows, part_rows)
                            left_s[k, place : place + part_rows, :] = turned_s[
                                pl.ds(start, part_rows), :
                            ]
                            place += part_rows
        sum_s[...] = jnp.zeros(sum_s.shape, jnp.float32)

    def product(k, values):
        mine_ref[...] = dot_nn(left_s[k, :half, :], values).astype(jnp.bfloat16)
        other_ref[...] = dot_nn(left_s[k, half:, :], values).astype(jnp.bfloat16)

    @pl.when(step < first_down // 2)
    def _():
        product(0, gate_ref[...])

    @pl.when((step >= first_down // 2) & (step < first_down))
    def _():
        product(0, upper_ref[...])

    @pl.when(step >= first_down)
    def _():
        hidden = hidden_ref[...]
        product(1, hidden)
        sum_s[...] += dot_nt(hidden, weight_ref[...])

    @pl.when(step == last)
    def _():
        rows = part_ref.shape[1]
        for s in range(4):
            part_ref[lax.bitwise_xor(rank_ref[3], s)] = sum_s[
                s * rows : (s + 1) * rows, :
            ].astype(jnp.bfloat16)


def feed_back_step(ranks, two, cotangent, gate, upper, hidden, weights):
    tokens, width = two.shape
    columns = weights.shape[1]
    steps = columns // chunk
    first_down = steps * 2 // 3
    third = first_down // 2
    half = width // 2

    def down_at(j):
        return jnp.maximum(j - first_down, 0)

    return pl.pallas_call(
        feed_back_kernel,
        grid=(steps,),
        in_specs=[
            in_scalars,
            whole((tokens, width)),
            whole((tokens, width)),
            pl.BlockSpec((tokens, chunk), lambda j: (0, jnp.minimum(j, third - 1))),
            pl.BlockSpec((tokens, chunk), lambda j: (0, jnp.clip(j - third, 0, third - 1))),
            pl.BlockSpec((tokens, chunk), lambda j: (0, down_at(j))),
            pl.BlockSpec((width, chunk), lambda j: (0, first_down + down_at(j))),
        ],
        out_specs=[
            pl.BlockSpec((half, chunk), lambda j: (0, j)),
            pl.BlockSpec((half, chunk), lambda j: (0, j)),
            whole((4, tokens // 4, width)),
        ],
        out_shape=[
            jax.ShapeDtypeStruct((half, columns), jnp.bfloat16),
            jax.ShapeDtypeStruct((half, columns), jnp.bfloat16),
            jax.ShapeDtypeStruct((4, tokens // 4, width), jnp.bfloat16),
        ],
        scratch_shapes=[
            pltpu.VMEM((width, tokens), jnp.bfloat16),
            pltpu.VMEM((2, width, tokens), jnp.bfloat16),
            pltpu.VMEM((tokens, width), jnp.float32),
        ],
        compiler_params=pltpu.CompilerParams(vmem_limit_bytes=56 * 2**20),
        cost_estimate=pl.CostEstimate(flops=10**8, bytes_accessed=10**5, transcendentals=0),
        name="feed_back_step",
    )(ranks, two, cotangent, gate, upper, hidden, weights)


def head_weight(refs, s, hr):
    return refs[s][...] if hr == 0 else refs[4][s]


def feature_block(rank, s, width):
    start = lax.bitwise_xor(rank, s) * (width // 4)
    return pl.ds(pl.multiple_of(start, width // 4), width // 4)


def branch_kernel(
    rank_ref, hidden_ref, gain_ref, own_ref, one_ref, two_ref, three_ref, w_own, w_one, w_two,
    w_three, w_swap, middle_ref, normed_ref,
):
    weights = (w_own, w_one, w_two, w_three, w_swap)
    width = hidden_ref.shape[1]
    branch = None
    for s, context_ref in enumerate((own_ref, one_ref, two_ref, three_ref)):
        for hr in range(2):
            context = context_ref[:, hr * lanes : (hr + 1) * lanes]
            part = dot_nt(context, head_weight(weights, s, hr))
            branch = part if branch is None else branch + part
    for s in range(4):
        at = feature_block(rank_ref[0], s, width)
        middle_ref[:, at] = (
            hidden_ref[:, at].astype(jnp.float32)
            + branch[:, s * (width // 4) : (s + 1) * (width // 4)]
        )
    middle = middle_ref[...]
    scale = lax.rsqrt(jnp.mean(middle * middle, axis=-1, keepdims=True) + eps_norm)
    normed_ref[...] = (middle * scale * gain_ref[...]).astype(jnp.bfloat16)


def branch_back_kernel(
    rank_ref, in_own, in_one, in_two, in_three, middle_ref, cot_ref, gain_ref, w_own, w_one, w_two,
    w_three, w_swap, grad_ref, low_ref, terms_ref, own_ref, one_ref, two_ref, three_ref,
):
    weights = (w_own, w_one, w_two, w_three, w_swap)
    parts = [ref[...].astype(jnp.float32) for ref in (in_own, in_one, in_two, in_three)]
    grads = (parts[0] + parts[2]) + (parts[1] + parts[3])
    middle = middle_ref[...]
    scale = lax.rsqrt(jnp.mean(middle * middle, axis=-1, keepdims=True) + eps_norm)
    back, terms = norm_back(middle, scale, gain_ref[...], grads)
    back = cot_ref[...].astype(jnp.float32) + back
    low = back.astype(jnp.bfloat16)
    grad_ref[...] = back
    low_ref[...] = low
    terms_ref[...] = jnp.sum(terms, axis=0, keepdims=True)
    width = low_ref.shape[1]
    low = jnp.concatenate(
        [low_ref[:, feature_block(rank_ref[0], s, width)] for s in range(4)], axis=1
    )
    for s, out_ref in enumerate((own_ref, one_ref, two_ref, three_ref)):
        for hr in range(2):
            out_ref[:, hr * lanes : (hr + 1) * lanes] = dot_nn(
                low, head_weight(weights, s, hr)
            ).astype(jnp.bfloat16)


gain_rows = 32


def send_pieces(rank, rows, pick, gains, out_refs):
    high = gains.astype(jnp.bfloat16)
    rest = (gains - high.astype(jnp.float32)).astype(jnp.bfloat16)
    for s, out_ref in enumerate(out_refs):
        start = pl.multiple_of(lax.bitwise_xor(rank, s) * rows, rows)
        for k in range(3):
            out_ref[k * rows : (k + 1) * rows, :] = pick(k, start).astype(out_ref.dtype)
        out_ref[3 * rows : 3 * rows + gain_rows, :] = high.astype(out_ref.dtype)
        out_ref[3 * rows + gain_rows :, :] = rest.astype(out_ref.dtype)


def sum_refs(refs, rows):
    parts = [ref[rows, :].astype(jnp.float32) for ref in refs]
    return (parts[0] + parts[2]) + (parts[1] + parts[3])


def first_stage_kernel(
    rank_ref, qkv_ref, output_ref, weight_ref, gain_ref, ffn_ref, head_ref,
    own_ref, one_ref, two_ref, three_ref, gain_s,
):
    products = qkv_ref[...] * weight_ref[...].astype(jnp.float32)
    ones = jnp.ones((8, products.shape[1]), jnp.float32)
    attn = lax.dot_general(
        ones,
        products,
        (((1,), (1,)), ((), ())),
        precision=lax.Precision.HIGHEST,
        preferred_element_type=jnp.float32,
    )[0:1, :] / gain_ref[...]
    ffn = ffn_ref[...]
    head = jnp.sum(head_ref[...], axis=0, keepdims=True)
    gain_s[...] = jnp.zeros(gain_s.shape, jnp.float32)
    count = attn.shape[1] // lanes
    for i in range(count):
        gain_s[i : i + 1, :] = attn[:, i * lanes : (i + 1) * lanes]
        gain_s[count + i : count + i + 1, :] = ffn[:, i * lanes : (i + 1) * lanes]
    gain_s[2 * count : 2 * count + 1, :] = head[:, :lanes]
    gain_s[2 * count + 1 : 2 * count + 2, :] = head[:, lanes:]
    rows = qkv_ref.shape[0] // 4

    def pick(k, start):
        if k == 2:
            return output_ref[pl.ds(start, rows), :]
        return qkv_ref[pl.ds(start, rows), k * lanes : (k + 1) * lanes]

    send_pieces(rank_ref[0], rows, pick, gain_s[...], (own_ref, one_ref, two_ref, three_ref))


def second_stage_kernel(
    rank_ref, in_own, in_one, in_two, in_three, own_ref, one_ref, two_ref, three_ref, sum_s,
):
    refs = (in_own, in_one, in_two, in_three)
    count = sum_s.shape[0]
    sum_s[...] = sum_refs(refs, slice(0, count))
    gains = sum_refs(refs, slice(count, count + gain_rows)) + sum_refs(
        refs, slice(count + gain_rows, count + 2 * gain_rows)
    )
    rows = count // 12

    def pick(k, start):
        return sum_s[pl.ds(pl.multiple_of(k * (4 * rows) + start, rows), rows), :]

    send_pieces(rank_ref[0], rows, pick, gains, (own_ref, one_ref, two_ref, three_ref))


def third_stage_kernel(
    in_own, in_one, in_two, in_three, query_ref, keyval_ref, output_ref, gain_ref,
):
    refs = (in_own, in_one, in_two, in_three)
    rows = query_ref.shape[0]
    for k, out_ref in enumerate((query_ref, keyval_ref, output_ref)):
        out_ref[...] = sum_refs(refs, slice(k * rows, (k + 1) * rows))
    gain_ref[...] = sum_refs(refs, slice(3 * rows, 3 * rows + gain_rows)) + sum_refs(
        refs, slice(3 * rows + gain_rows, 3 * rows + 2 * gain_rows)
    )


def blocks_of(arrays):
    return [whole(array.shape) for array in arrays]


def piece_shapes(rows):
    shape = (3 * rows + 2 * gain_rows, lanes)
    return [jax.ShapeDtypeStruct(shape, jnp.float32)] + [
        jax.ShapeDtypeStruct(shape, jnp.bfloat16)
    ] * 3


def branch_step(rank, hidden, gain, contexts, weights):
    rows, width = hidden.shape
    operands = (hidden, gain, *contexts, *weights)
    shapes = [
        jax.ShapeDtypeStruct((rows, width), jnp.float32),
        jax.ShapeDtypeStruct((rows, width), jnp.bfloat16),
    ]
    return pl.pallas_call(
        branch_kernel,
        grid=(1,),
        in_specs=[in_scalars] + blocks_of(operands),
        out_specs=blocks_of(shapes),
        out_shape=shapes,
        compiler_params=pltpu.CompilerParams(vmem_limit_bytes=24 * 2**20),
        cost_estimate=pl.CostEstimate(
            flops=3 * 10**8, bytes_accessed=4 * 10**6, transcendentals=0
        ),
        name="branch_step",
    )(rank[None].astype(jnp.int32), *operands)


def branch_back_step(rank, parts, middle, cotangent, gain, weights):
    rows, width = middle.shape
    operands = (*parts, middle, cotangent, gain, *weights)
    shapes = [
        jax.ShapeDtypeStruct((rows, width), jnp.float32),
        jax.ShapeDtypeStruct((rows, width), jnp.bfloat16),
        jax.ShapeDtypeStruct((1, width), jnp.float32),
    ] + [jax.ShapeDtypeStruct((rows, 2 * lanes), jnp.bfloat16)] * 4
    return pl.pallas_call(
        branch_back_kernel,
        grid=(1,),
        in_specs=[in_scalars] + blocks_of(operands),
        out_specs=blocks_of(shapes),
        out_shape=shapes,
        compiler_params=pltpu.CompilerParams(vmem_limit_bytes=56 * 2**20),
        cost_estimate=pl.CostEstimate(
            flops=3 * 10**8, bytes_accessed=5 * 10**6, transcendentals=0
        ),
        name="branch_back_step",
    )(rank[None].astype(jnp.int32), *operands)


def first_stage(rank, qkv_grad, output_grad, weight, gain, ffn, head):
    operands = (qkv_grad, output_grad, weight, gain, ffn, head)
    shapes = piece_shapes(qkv_grad.shape[0] // 4)
    return pl.pallas_call(
        first_stage_kernel,
        grid=(1,),
        in_specs=[in_scalars] + blocks_of(operands),
        out_specs=blocks_of(shapes),
        out_shape=shapes,
        scratch_shapes=[pltpu.VMEM((gain_rows, lanes), jnp.float32)],
        compiler_params=pltpu.CompilerParams(vmem_limit_bytes=24 * 2**20),
        cost_estimate=pl.CostEstimate(flops=10**7, bytes_accessed=3 * 10**6, transcendentals=0),
        name="first_stage",
    )(rank[None].astype(jnp.int32), *operands)


def second_stage(rank, parts):
    count = parts[0].shape[0] - 2 * gain_rows
    operands = tuple(parts)
    shapes = piece_shapes(count // 12)
    return pl.pallas_call(
        second_stage_kernel,
        grid=(1,),
        in_specs=[in_scalars] + blocks_of(operands),
        out_specs=blocks_of(shapes),
        out_shape=shapes,
        scratch_shapes=[pltpu.VMEM((count, lanes), jnp.float32)],
        compiler_params=pltpu.CompilerParams(vmem_limit_bytes=24 * 2**20),
        cost_estimate=pl.CostEstimate(flops=10**6, bytes_accessed=10**6, transcendentals=0),
        name="second_stage",
    )(rank[None].astype(jnp.int32), *operands)


def third_stage(parts):
    rows = (parts[0].shape[0] - 2 * gain_rows) // 3
    operands = tuple(parts)
    shapes = [jax.ShapeDtypeStruct((rows, lanes), jnp.float32)] * 3 + [
        jax.ShapeDtypeStruct((gain_rows, lanes), jnp.float32)
    ]
    return pl.pallas_call(
        third_stage_kernel,
        grid=(1,),
        in_specs=blocks_of(operands),
        out_specs=blocks_of(shapes),
        out_shape=shapes,
        compiler_params=pltpu.CompilerParams(vmem_limit_bytes=24 * 2**20),
        cost_estimate=pl.CostEstimate(flops=10**6, bytes_accessed=10**6, transcendentals=0),
        name="third_stage",
    )(*operands)


def by_sequence(width):
    return pl.BlockSpec((2, 4, 1, piece, width), lambda s: (0, 0, s, 0, 0))


def whole(shape):
    return pl.BlockSpec(shape, lambda s: (0,) * len(shape))


in_scalars = pl.BlockSpec(memory_space=pltpu.SMEM)


def five(width, dtype, sequences):
    return jax.ShapeDtypeStruct((2, 4, sequences, piece, width), dtype)


def project(rank, own, swapped, weights, gain, cosine, sine):
    sequences, width = own.shape[1], own.shape[3]
    operands = (*weights, gain, cosine, sine)
    rows_spec = pl.BlockSpec((4, 1, piece, width), lambda s: (0, s, 0, 0))
    return pl.pallas_call(
        project_kernel,
        grid=(sequences,),
        in_specs=[in_scalars, rows_spec, rows_spec] + blocks_of(operands),
        out_specs=[by_sequence(2 * lanes), by_sequence(lanes), by_sequence(lanes)],
        out_shape=[five(2 * lanes, jnp.float32, sequences)]
        + [five(lanes, jnp.bfloat16, sequences)] * 2,
        compiler_params=pltpu.CompilerParams(vmem_limit_bytes=56 * 2**20),
        cost_estimate=pl.CostEstimate(flops=10**8, bytes_accessed=2 * 10**6, transcendentals=0),
        name="project",
    )(rank[None].astype(jnp.int32), own, swapped, *operands)


def finish(raw, gain, cosine, sine, query_grad, keyval_parts):
    sequences = raw.shape[2]
    rows = cosine.shape[0]
    return pl.pallas_call(
        finish_kernel,
        grid=(sequences,),
        in_specs=[
            by_sequence(2 * lanes), whole((1, 2 * lanes)), whole((rows, lanes)), whole((rows, lanes)),
        ] + [by_sequence(lanes)] * 5,
        out_specs=[by_sequence(2 * lanes), whole((8, 2 * lanes))],
        out_shape=[
            five(2 * lanes, jnp.bfloat16, sequences),
            jax.ShapeDtypeStruct((8, 2 * lanes), jnp.float32),
        ],
        compiler_params=pltpu.CompilerParams(vmem_limit_bytes=24 * 2**20),
        cost_estimate=pl.CostEstimate(flops=10**8, bytes_accessed=4 * 10**6, transcendentals=0),
        name="finish",
    )(raw, gain, cosine, sine, query_grad, *keyval_parts)


def attend(meta, query, keyval_parts, scale):
    sequences = query.shape[2]
    keys = 4 * 8 * piece
    return pl.pallas_call(
        functools.partial(attend_kernel, scale * log2_e),
        grid=(sequences,),
        in_specs=[in_scalars] + [by_sequence(lanes)] * 5,
        out_specs=[by_sequence(lanes)] * 3
        + [pl.BlockSpec((8, 1, piece, lanes), lambda s: (0, s, 0, 0))],
        out_shape=[
            five(lanes, jnp.float32, sequences),
            five(lanes, jnp.bfloat16, sequences),
            five(lanes, jnp.float32, sequences),
            jax.ShapeDtypeStruct((8, sequences, piece, lanes), jnp.bfloat16),
        ],
        scratch_shapes=[
            pltpu.VMEM((2 * block, lanes), jnp.bfloat16),
            pltpu.VMEM((2 * keys, lanes), jnp.bfloat16),
            pltpu.VMEM((2 * keys, 2 * lanes), jnp.bfloat16),
            pltpu.VMEM((2 * block, 2 * lanes), jnp.float32),
        ],
        compiler_params=pltpu.CompilerParams(vmem_limit_bytes=24 * 2**20),
        cost_estimate=pl.CostEstimate(
            flops=2 * 10**9, bytes_accessed=4 * 10**6, transcendentals=2 * 10**6
        ),
        name="attend",
    )(meta, query, *keyval_parts)


def attend_back(meta, query, keyval_parts, context, total, grads, scale):
    sequences = query.shape[2]
    keys = 4 * 8 * piece
    blocks = keys // block
    return pl.pallas_call(
        functools.partial(attend_back_kernel, scale * log2_e, scale),
        grid=(sequences,),
        in_specs=[in_scalars] + [by_sequence(lanes)] * 8,
        out_specs=[by_sequence(lanes)] * 5,
        out_shape=[five(lanes, jnp.float32, sequences)] * 2
        + [five(lanes, jnp.bfloat16, sequences)] * 3,
        scratch_shapes=[
            pltpu.VMEM((2 * block, lanes), jnp.bfloat16),
            pltpu.VMEM((2 * block, lanes), jnp.bfloat16),
            pltpu.VMEM((2 * block, lanes), jnp.float32),
            pltpu.VMEM((2 * block, lanes), jnp.float32),
            pltpu.VMEM((8 * block, lanes), jnp.bfloat16),
            pltpu.VMEM((2 * keys, lanes), jnp.bfloat16),
            pltpu.VMEM((2 * keys, lanes), jnp.bfloat16),
            pltpu.VMEM((blocks, lanes, 2 * block), jnp.bfloat16),
            pltpu.VMEM((2, 8, block), jnp.float32),
            pltpu.VMEM((2, lanes, block), jnp.float32),
            pltpu.VMEM((keys, lanes), jnp.float32),
        ],
        compiler_params=pltpu.CompilerParams(vmem_limit_bytes=56 * 2**20),
        cost_estimate=pl.CostEstimate(
            flops=5 * 10**9, bytes_accessed=8 * 10**6, transcendentals=2 * 10**6
        ),
        name="attend_back",
    )(meta, query, *keyval_parts, context, total, grads)


def body(
    hidden_in,
    cotangent,
    block_order,
    query_weight,
    keyval_weight,
    output_weight,
    gate_weight,
    up_weight,
    down_weight,
    attn_gain,
    ffn_gain,
    query_gain,
    key_gain,
):
    sequences, _, own_rows, width = hidden_in.shape
    tensor_size = lax.axis_size("tensor")
    heads_size = lax.axis_size("heads")
    chips = heads_size // 2
    shard_rows = own_rows * heads_size
    all_rows = sequences * shard_rows
    units = gate_weight.shape[1]
    query_width = query_weight.shape[2]
    scale = head_dim ** (-0.5)
    rank = lax.axis_index("tensor")
    head_rank = lax.axis_index("heads")
    chip = head_rank // 2
    core = lax.rem(head_rank, 2)
    hidden_own = hidden_in[:, 0]
    cot_own = cotangent[:, 0]
    folded = (2, chips, sequences, own_rows)

    barrier = lax.optimization_barrier
    own_tokens = sequences * own_rows

    attn_own = jnp.concatenate(
        [query_weight[:, 0], keyval_weight[:, 0], output_weight[:, 0]], axis=1
    )
    attn_ring = gather_ring(attn_own, "tensor")
    inputs = hidden_own.astype(jnp.float32)
    scale_one = rms_scale(inputs)
    normed_one = (inputs * scale_one * attn_gain).astype(jnp.bfloat16)
    attn_ring[1], normed_one = barrier((attn_ring[1], normed_one))
    attn_y = place_ring(attn_ring, "tensor")
    attn_y, cot_own, block_order = barrier((attn_y, cot_own, block_order))
    attn_ring = gather_ring(attn_y, "fsdp")

    chip_at = chip ^ jnp.arange(chips, dtype=jnp.int32)
    core_at = lax.rem(core + jnp.arange(2, dtype=jnp.int32), 2)
    head_at = chip_at[None, :] * 2 + core_at[:, None]
    row_at = (head_at[:, :, None] * own_rows + jnp.arange(own_rows, dtype=jnp.int32)).reshape(
        shard_rows
    )
    rank_at = rank ^ jnp.arange(tensor_size, dtype=jnp.int32)
    order_at = block_order[rank_at]
    meta = jnp.concatenate([order_at.reshape(-1), chip[None], core[None]]).astype(jnp.int32)
    positions = (
        jnp.where(row_at >= block, order_at[0, 1], order_at[0, 0]) * block + lax.rem(row_at, block)
    )
    lane = jnp.arange(lanes, dtype=jnp.int32)
    freq = rope_base ** (
        -(lax.rem(lane, head_dim // 2).astype(jnp.float32) * 2.0 / head_dim)
    )
    angles = positions.astype(jnp.float32)[:, None] * freq[None, :]
    cosine = jnp.cos(angles)
    sine = jnp.sin(angles) * jnp.where(lax.rem(lane, head_dim) < head_dim // 2, -1.0, 1.0)[None, :]
    head_gain = jnp.concatenate(
        [query_gain, query_gain, key_gain, jnp.ones((head_dim,), jnp.float32)]
    )[None, :]
    rows_ring, attn_ring, meta, cosine, sine, head_gain = barrier(
        (gather_ring(normed_one, "z"), attn_ring, meta, cosine, sine, head_gain)
    )
    output_all = jnp.stack([part[..., 2 * query_width :] for part in attn_ring])
    output_ring = gather_ring(output_all.reshape(width, query_width), "z")
    rows_own = jnp.stack(rows_ring)
    rows_swap = swap_core(rows_own)
    rows_halves = [rows_own.reshape(-1, width), rows_swap.reshape(-1, width)]

    feed_own = jnp.concatenate([gate_weight, up_weight, down_weight], axis=1)
    feed_all = lax.all_gather(feed_own, ("fsdp", "heads"), axis=0, tiled=True)
    gate_up_all = feed_all[:, : 2 * units]
    down_all = feed_all[:, 2 * units :]

    x_rank = lax.axis_index("fsdp")
    qkv_raw, query_rot, keyval_rot = project(
        x_rank, rows_own, rows_swap, attn_ring, head_gain, cosine, sine
    )
    attn_ring, keyval_rot = barrier((attn_ring, keyval_rot))
    attn_all = place_ring(attn_ring, "fsdp").reshape(width, 3 * query_width)
    qkv_all = attn_all[:, : 2 * query_width]
    cot_one = exchange(cot_own, "tensor", 1)
    keyval_parts = gather_ring(keyval_rot, "tensor")

    cot_two = jnp.stack([cot_own, cot_one])
    keyval_parts, cot_two, output_ring = barrier((keyval_parts, cot_two, output_ring))
    cot_three = exchange(cot_two, "tensor", 3)

    context, context_low, total, context_placed = attend(meta, query_rot, keyval_parts, scale)
    core_rows = (chips, own_tokens, query_width)
    context_swap = swap_core(context_low[1].reshape(core_rows))
    context_pairs = jnp.concatenate([context_low[0].reshape(core_rows), context_swap], axis=2)
    contexts = scatter_ring([context_pairs[s] for s in range(chips)], "z")
    weights = (*output_ring, swap_core(jnp.stack(output_ring)))
    middle, normed_two = branch_step(
        x_rank,
        hidden_own.reshape(own_tokens, width), ffn_gain[None, :], contexts, weights
    )
    normed_two, cot_three = barrier((normed_two, cot_three))
    two_ring = gather_ring(normed_two, "tensor")
    cot_flat = jnp.stack([cot_two[0], cot_two[1], cot_three[1], cot_three[0]]).reshape(-1, width)
    hidden_grad = matmul(cot_flat, down_all)
    two_ring, hidden_grad = barrier((two_ring, hidden_grad))
    two_flat = jnp.stack(two_ring).reshape(-1, width)
    gate_up = matmul(two_flat, gate_up_all)
    gate_value = gate_up[:, :units]
    upper_value = gate_up[:, units:]
    sigmoid_gate = jax.nn.sigmoid(gate_value)
    activated = gate_value * sigmoid_gate
    hidden = (activated * upper_value).astype(jnp.bfloat16)
    gate_low = (
        hidden_grad * upper_value * sigmoid_gate * (1.0 + gate_value * (1.0 - sigmoid_gate))
    ).astype(jnp.bfloat16)
    upper_low = (hidden_grad * activated).astype(jnp.bfloat16)
    both_low = jnp.concatenate([gate_low, upper_low], axis=1)
    two_part = contract_cols(both_low, gate_up_all).astype(jnp.bfloat16)
    two_moved = scatter_ring(
        [two_part[s * own_tokens : (s + 1) * own_tokens] for s in range(tensor_size)], "tensor"
    )

    quarter = width // 4
    eighth = width // 8
    ranks = jnp.stack([x_rank, chip, core, rank]).astype(jnp.int32)
    feed_other, feed_mine, feed_part = feed_back_step(
        ranks, two_flat, cot_flat, gate_low, upper_low, hidden, feed_all
    )
    two_moved, feed_other, feed_mine, feed_part = barrier(
        (two_moved, feed_other, feed_mine, feed_part)
    )
    feed_sum = swap_core(feed_other) + feed_mine

    middle_grad, branch_low, ffn_row, *grad_pairs = branch_back_step(
        x_rank,
        two_moved,
        middle,
        cot_own.reshape(own_tokens, width),
        ffn_gain[None, :],
        weights,
    )
    branch_all = lax.all_gather(branch_low.reshape(sequences, own_rows, width), "heads")
    grad_moved = scatter_ring(grad_pairs, "z")
    grad_moved, feed_sum = barrier((grad_moved, feed_sum))
    sent_a = exchange(feed_sum[eighth:quarter], "fsdp", 1)
    sent_b = exchange(feed_sum[quarter + eighth :], "fsdp", 3)
    grad_moved = jnp.stack(grad_moved)
    context_grad = jnp.stack(
        [grad_moved[..., :query_width], swap_core(grad_moved[..., query_width:])]
    ).reshape(folded + (query_width,))
    query_grad, own, one, two, three = attend_back(
        meta, query_rot, keyval_parts, context, total, context_grad, scale
    )
    kv_moved = scatter_ring([own, one, two, three], "tensor")
    kv_moved[1], sent_a, sent_b = barrier((kv_moved[1], sent_a, sent_b))
    sum_a = feed_sum[:eighth].astype(jnp.float32) + sent_a.astype(jnp.float32)
    sum_b = feed_sum[quarter : quarter + eighth].astype(jnp.float32) + sent_b.astype(jnp.float32)
    output_grad = contract_rows(
        branch_all.reshape(all_rows, width), context_placed.reshape(all_rows, query_width)
    )
    kv_moved, sum_a, sum_b, feed_part, output_grad = barrier(
        (kv_moved, sum_a, sum_b, feed_part, output_grad)
    )
    feed = lax.psum_scatter(feed_part, "tensor", scatter_dimension=0, tiled=True)
    block_out = (middle + feed[0].astype(jnp.float32)).astype(jnp.bfloat16)
    row_half = eighth // 2
    last_a = exchange(sum_a[row_half:].astype(jnp.bfloat16), "fsdp", 3)
    last_b = exchange(sum_b[row_half:].astype(jnp.bfloat16), "fsdp", 1)

    qkv_low, head_terms = finish(qkv_raw, head_gain, cosine, sine, query_grad, kv_moved)
    qkv_low = qkv_low.reshape(all_rows, 2 * query_width)
    one_part = contract_cols(qkv_low, qkv_all).astype(jnp.bfloat16)
    one_part, qkv_low = barrier((one_part.reshape(folded + (width,)), qkv_low))
    one_swap = swap_core(one_part[1])
    half_rows = all_rows // 2
    qkv_grad = contract_rows(rows_halves[0], qkv_low[:half_rows]) + contract_rows(
        rows_halves[1], qkv_low[half_rows:]
    )
    attn_pieces = first_stage(
        x_rank, qkv_grad, output_grad, qkv_all, attn_gain[None, :], ffn_row, head_terms
    )
    one_sum = one_part[0].astype(jnp.float32) + one_swap.astype(jnp.float32)
    attn_pieces, one_sum = barrier((attn_pieces, one_sum))
    one_sent = exchange(jnp.stack([one_sum[1], one_sum[2]]).astype(jnp.bfloat16), "z", 1)
    attn_moved = scatter_ring(attn_pieces, "fsdp")
    attn_pieces = second_stage(rank, attn_moved)
    attn_moved = scatter_ring(attn_pieces, "tensor")
    attn_moved, one_sent, last_a, last_b, block_out = barrier(
        (attn_moved, one_sent, last_a, last_b, block_out)
    )
    query_out, keyval_out, output_out, gains = third_stage(attn_moved)
    gains = gains + swap_core(gains)
    one_far = (one_sum[3] + one_sent[1].astype(jnp.float32)).astype(jnp.bfloat16)
    one_far = exchange(one_far, "z", 3)
    z_sent = (sum_b[:row_half] + last_b.astype(jnp.float32)).astype(jnp.bfloat16)
    z_sent = exchange(z_sent, "z", 1)
    gains = gains + exchange(gains, "z", 1)
    gains, one_far, z_sent = barrier((gains, one_far, z_sent))
    z_sum = (
        sum_a[:row_half] + last_a.astype(jnp.float32) + z_sent.astype(jnp.float32)
    )
    z_last = exchange(z_sum[part_rows:].astype(jnp.bfloat16), "z", 3)
    gains = gains + exchange(gains, "z", 3)
    feed_grad = z_sum[:part_rows] + z_last.astype(jnp.float32)
    normed_one_grad = one_sum[0] + one_sent[0].astype(jnp.float32) + one_far.astype(jnp.float32)
    input_norm_grad, _ = norm_back(inputs, scale_one, attn_gain, normed_one_grad)
    input_grad = middle_grad.reshape(inputs.shape) + input_norm_grad
    gain_at = width // lanes
    return (
        block_out.reshape(hidden_in.shape),
        input_grad[:, None],
        query_out[:, None],
        keyval_out[:, None],
        output_out[:, None],
        feed_grad[:, :units],
        feed_grad[:, units : 2 * units],
        feed_grad[:, 2 * units :],
        gains[:gain_at].reshape(width),
        gains[gain_at : 2 * gain_at].reshape(width),
        gains[2 * gain_at, :head_dim] + gains[2 * gain_at, head_dim:],
        gains[2 * gain_at + 1, :head_dim],
    )


def solution(mesh):
    placed = (
        P("fsdp", "tensor", "heads", None),
        P("fsdp", "tensor", "heads", None),
        P(),
        P(("fsdp", "tensor"), "heads", None),
        P(("fsdp", "tensor"), "heads", None),
        P(("fsdp", "tensor"), "heads", None),
        P(("fsdp", "heads"), "tensor"),
        P(("fsdp", "heads"), "tensor"),
        P(("fsdp", "heads"), "tensor"),
        P(),
        P(),
        P(),
        P(),
    )
    return jax.shard_map(
        body,
        mesh=mesh,
        in_specs=placed,
        out_specs=(
            P("fsdp", "tensor", "heads", None),
            P("fsdp", "tensor", "heads", None),
            P(("fsdp", "tensor"), "heads", None),
            P(("fsdp", "tensor"), "heads", None),
            P(("fsdp", "tensor"), "heads", None),
            P(("fsdp", "heads"), "tensor"),
            P(("fsdp", "heads"), "tensor"),
            P(("fsdp", "heads"), "tensor"),
            P(),
            P(),
            P(),
            P(),
        ),
        check_vma=False,
    )
```

```python
import functools

import jax
import jax.numpy as jnp
from jax import lax
from jax.experimental import pallas as pl
from jax.experimental.pallas import tpu as pltpu
from jax.sharding import PartitionSpec as P

eps_norm = 1e-05
rope_base = 1000000.0
log2_e = 1.4426950408889634
block = 256
piece = 64
head_dim = 64
lanes = 128


def rms_scale(values):
    return lax.rsqrt(jnp.mean(values * values, axis=-1, keepdims=True) + eps_norm)


def norm_back(values, scale, gain, grads):
    scaled = grads * gain
    inner = jnp.mean(scaled * values, axis=-1, keepdims=True)
    return (scale * (scaled - values * scale * scale * inner), grads * values * scale)


def matmul(left, right):
    return jnp.dot(left, right, preferred_element_type=jnp.float32)


def contract_rows(left, right):
    return lax.dot_general(
        left, right, (((0,), (0,)), ((), ())), preferred_element_type=jnp.float32
    )


def contract_cols(left, right):
    return lax.dot_general(
        left, right, (((1,), (1,)), ((), ())), preferred_element_type=jnp.float32
    )


def sum_four(parts):
    return (parts[0] + parts[2]) + (parts[1] + parts[3])


def exchange(values, axis, mask):
    name = "heads" if axis in ("z", "core") else axis
    shift = 2 if axis == "z" else 1
    size = lax.axis_size(name)
    return lax.ppermute(values, name, [(i, i ^ (mask * shift)) for i in range(size)])


def swap_core(values):
    return exchange(values, "core", 1)


def gather_ring(values, axis):
    return [values] + [exchange(values, axis, m) for m in (1, 2, 3)]


def scatter_ring(parts, axis):
    return [parts[0]] + [exchange(parts[m], axis, m) for m in (1, 2, 3)]


def place_ring(parts, axis):
    size = lax.axis_size(axis)
    rank = lax.axis_index(axis)
    placed = jnp.zeros((size,) + parts[0].shape, parts[0].dtype)
    for s, part in enumerate(parts):
        placed = lax.dynamic_update_index_in_dim(placed, part, lax.bitwise_xor(rank, s), 0)
    return placed


def dot_nn(left, right):
    return lax.dot_general(
        left, right, (((1,), (0,)), ((), ())), preferred_element_type=jnp.float32
    )


def dot_nt(left, right):
    return lax.dot_general(
        left, right, (((1,), (1,)), ((), ())), preferred_element_type=jnp.float32
    )


def lane_index(shape):
    return lax.broadcasted_iota(jnp.int32, shape, 1)


def half_sums(values):
    rows = lax.broadcasted_iota(jnp.int32, (lanes, lanes), 0) // head_dim
    columns = lax.broadcasted_iota(jnp.int32, (lanes, lanes), 1) // head_dim
    ones = jnp.where(rows == columns, 1.0, 0.0).astype(jnp.float32)
    return lax.dot_general(
        values,
        ones,
        (((1,), (0,)), ((), ())),
        precision=lax.Precision.HIGHEST,
        preferred_element_type=jnp.float32,
    )


def turn_lanes(values):
    lane = lane_index(values.shape)
    up = pltpu.roll(values, lanes - head_dim // 2, 1)
    down = pltpu.roll(values, head_dim // 2, 1)
    return jnp.where(lax.rem(lane, head_dim) < head_dim // 2, up, down)


def rows_of(ref):
    return ref[...].reshape(ref.shape[0] * ref.shape[1] * ref.shape[3], ref.shape[4])


def project_kernel(
    rank_ref, own_ref, swap_ref, w_own, w_one, w_two, w_three, gain_ref, cos_ref, sin_ref,
    raw_ref, query_ref, keyval_ref,
):
    halves = []
    for rows_ref in (own_ref, swap_ref):
        total = None
        for s, w_ref in enumerate((w_own, w_one, w_two, w_three)):
            depth = w_ref.shape[0] * w_ref.shape[1]
            start = pl.multiple_of(lax.bitwise_xor(rank_ref[0], s) * depth, depth)
            rows = rows_ref[:, 0, :, pl.ds(start, depth)].reshape(-1, depth)
            weight = w_ref[...].reshape(depth, w_ref.shape[2])[:, : 2 * lanes]
            part = dot_nn(rows, weight)
            total = part if total is None else total + part
        halves.append(total)
    raw = jnp.concatenate(halves)
    raw_ref[...] = raw.reshape(raw_ref.shape)
    cosine = cos_ref[...]
    sine = sin_ref[...]
    shape = query_ref.shape
    first = lane_index(cosine.shape) < head_dim
    for part, out_ref in ((0, query_ref), (1, keyval_ref)):
        values = raw[:, part * lanes : (part + 1) * lanes]
        scale = lax.rsqrt(half_sums(values * values) * (1.0 / head_dim) + eps_norm)
        normed = values * scale * gain_ref[:, part * lanes : (part + 1) * lanes]
        turned = normed * cosine + turn_lanes(normed) * sine
        if part == 1:
            turned = jnp.where(first, turned, values)
        out_ref[...] = turned.astype(jnp.bfloat16).reshape(shape)


def finish_kernel(
    raw_ref, gain_ref, cos_ref, sin_ref, query_ref, own_ref, one_ref, two_ref, three_ref,
    low_ref, terms_ref,
):
    raw = rows_of(raw_ref)
    cosine = cos_ref[...]
    sine = sin_ref[...]
    first = lane_index(cosine.shape) < head_dim
    keyval = (rows_of(own_ref) + rows_of(two_ref).astype(jnp.float32)) + (
        rows_of(one_ref).astype(jnp.float32) + rows_of(three_ref).astype(jnp.float32)
    )

    @pl.when(pl.program_id(0) == 0)
    def _():
        terms_ref[...] = jnp.zeros(terms_ref.shape, jnp.float32)

    for part, grads in ((0, rows_of(query_ref)), (1, keyval)):
        at = slice(part * lanes, (part + 1) * lanes)
        values = raw[:, at]
        scale = lax.rsqrt(half_sums(values * values) * (1.0 / head_dim) + eps_norm)
        turned = grads * cosine - turn_lanes(grads) * sine
        scaled = turned * gain_ref[:, at]
        inner = half_sums(scaled * values) * (1.0 / head_dim)
        back = scale * (scaled - values * scale * scale * inner)
        terms = turned * values * scale
        if part == 1:
            back = jnp.where(first, back, grads)
        terms_ref[:, at] += jnp.sum(terms.reshape(-1, 8, lanes), axis=0)
        low_ref[..., at] = back.astype(jnp.bfloat16).reshape(low_ref.shape[:-1] + (lanes,))


def row_places(meta_ref):
    chip = meta_ref[8]
    core = meta_ref[9]
    places = []
    for s in range(4):
        chip_at = lax.bitwise_xor(chip, s)
        for cr in range(2):
            core_at = lax.rem(core + cr, 2)
            slot = lax.div(chip_at, 2)
            row = lax.rem(chip_at, 2) * (2 * piece) + core_at * piece
            places.append((s, cr, slot, row))
    return places


def at_row(start, count=piece):
    return pl.ds(pl.multiple_of(start, piece), count)


def load_keys(places, meta_ref, keyval_refs, key_s, value_s, ones):
    lane = lane_index((piece, lanes))
    first = lane < head_dim
    none = jnp.zeros((piece, lanes), jnp.bfloat16)
    one = jnp.ones((piece, lanes), jnp.bfloat16)
    for u, keyval_ref in enumerate(keyval_refs):
        for s, cr, slot, row in places:
            values = keyval_ref[cr, s, 0]
            other = jnp.concatenate([values[:, head_dim:], values[:, :head_dim]], axis=1)
            start = meta_ref[2 * u + slot] * (2 * block) + row
            lower = at_row(start)
            upper = at_row(start + block)
            key_s[lower, :] = jnp.where(first, values, none)
            key_s[upper, :] = jnp.where(first, none, other)
            value_s[lower, :lanes] = jnp.where(first, other, none)
            value_s[upper, :lanes] = jnp.where(first, none, values)
            if ones:
                value_s[lower, lanes:] = jnp.where(first, one, none)
                value_s[upper, lanes:] = jnp.where(first, none, one)


def block_steps(meta_ref, blocks):
    first = meta_ref[0]
    steps = []
    for i in range(blocks - 1):
        early = i < first
        steps.append((jnp.where(early, 0, 1), jnp.where(early, i, i - first), False))
    steps.append((0, first, True))
    steps.append((1, meta_ref[1], True))
    return steps


def attend_kernel(
    factor, meta_ref, query_ref, own_ref, one_ref, two_ref, three_ref,
    context_ref, low_ref, total_ref, placed_ref, query_s, key_s, value_s, sum_s,
):
    places = row_places(meta_ref)
    load_keys(places, meta_ref, (own_ref, one_ref, two_ref, three_ref), key_s, value_s, True)
    for s, cr, slot, row in places:
        query_s[at_row(slot * block + row), :] = query_ref[cr, s, 0]
    sum_s[...] = jnp.zeros(sum_s.shape, jnp.float32)
    query_at = lax.broadcasted_iota(jnp.int32, (block, 2 * block), 0)
    key_at = lax.rem(lane_index((block, 2 * block)), block)
    for b, j, diagonal in block_steps(meta_ref, key_s.shape[0] // (2 * block)):
        rows = pl.ds(pl.multiple_of(b * block, block), block)
        keys = pl.ds(pl.multiple_of(j * (2 * block), 2 * block), 2 * block)
        raised = jnp.exp2(dot_nt(query_s[rows, :], key_s[keys, :]) * factor)
        if diagonal:
            raised = jnp.where(query_at >= key_at, raised, 0.0)
        sum_s[rows, :] += dot_nn(raised.astype(jnp.bfloat16), value_s[keys, :])
    for s, cr, slot, row in places:
        found = sum_s[at_row(slot * block + row), :]
        total = found[:, lanes:]
        context = found[:, :lanes] / total
        context_ref[cr, s, 0] = context
        low = context.astype(jnp.bfloat16)
        low_ref[cr, s, 0] = low
        head = lax.bitwise_xor(meta_ref[8], s) * 2 + lax.rem(meta_ref[9] + cr, 2)
        placed_ref[head, 0] = low
        total_ref[cr, s, 0] = total


def attend_back_kernel(
    factor, scale, meta_ref, query_ref, own_ref, one_ref, two_ref, three_ref,
    context_ref, total_ref, grad_ref,
    query_out, own_out, one_out, two_out, three_out,
    query_s, grad_s, context_s, total_s, stack_s, key_s, value_s, turned_s, rows_s, query_sum,
    keyval_sum,
):
    places = row_places(meta_ref)
    load_keys(places, meta_ref, (own_ref, one_ref, two_ref, three_ref), key_s, value_s, False)
    blocks = key_s.shape[0] // (2 * block)
    for j in range(blocks):
        turned_s[j] = key_s[j * 2 * block : (j + 1) * 2 * block, :].T
    for s, cr, slot, row in places:
        at = at_row(slot * block + row)
        query_s[at, :] = query_ref[cr, s, 0]
        grad_s[at, :] = grad_ref[cr, s, 0]
        context_s[at, :] = context_ref[cr, s, 0]
        total_s[at, :] = total_ref[cr, s, 0]
    first = lane_index((block, lanes)) < head_dim
    none = jnp.zeros((block, lanes), jnp.bfloat16)
    pick = lax.broadcasted_iota(jnp.int32, (8, lanes), 0)
    pick = jnp.where(pick == lane_index((8, lanes)) // head_dim, 1.0, 0.0).astype(jnp.float32)
    for b in range(2):
        at = slice(b * block, (b + 1) * block)
        query = query_s[at, :]
        grads = grad_s[at, :]
        other_query = jnp.concatenate([query[:, head_dim:], query[:, :head_dim]], axis=1)
        other_grads = jnp.concatenate([grads[:, head_dim:], grads[:, :head_dim]], axis=1)
        base = 4 * b * block
        stack_s[base : base + block, :] = jnp.where(first, query, none)
        stack_s[base + block : base + 2 * block, :] = jnp.where(first, other_query, none)
        stack_s[base + 2 * block : base + 3 * block, :] = jnp.where(first, none, other_grads)
        stack_s[base + 3 * block : base + 4 * block, :] = jnp.where(first, none, grads)
        inner = lax.dot_general(
            pick,
            grads.astype(jnp.float32) * context_s[at, :],
            (((1,), (1,)), ((), ())),
            precision=lax.Precision.HIGHEST,
            preferred_element_type=jnp.float32,
        )
        logs = jnp.log2(total_s[at, :]).T
        rows_s[b, 0:1, :] = logs[0:1, :]
        rows_s[b, 1:2, :] = logs[head_dim : head_dim + 1, :]
        rows_s[b, 2:4, :] = inner[0:2, :]
    query_sum[...] = jnp.zeros(query_sum.shape, jnp.float32)
    keyval_sum[...] = jnp.zeros(keyval_sum.shape, jnp.float32)
    key_at = lax.broadcasted_iota(jnp.int32, (block, block), 0)
    query_at = lane_index((block, block))
    for b, j, diagonal in block_steps(meta_ref, blocks):
        rows = pl.ds(pl.multiple_of(b * block, block), block)
        keys = pl.ds(pl.multiple_of(j * (2 * block), 2 * block), 2 * block)
        key_rows = pl.ds(pl.multiple_of(j * block, block), block)
        stack_rows = pl.ds(pl.multiple_of(b * (4 * block), 4 * block), 4 * block)
        scores = dot_nt(key_s[keys, :], query_s[rows, :])
        share_grad = dot_nt(value_s[keys, :], grad_s[rows, :])
        shares_low = []
        score_low = []
        for g in range(2):
            at = slice(g * block, (g + 1) * block)
            shares = jnp.exp2(scores[at, :] * factor - rows_s[b, g : g + 1, :])
            if diagonal:
                shares = jnp.where(query_at >= key_at, shares, 0.0)
            shares_low.append(shares.astype(jnp.bfloat16))
            score_low.append(
                (shares * (share_grad[at, :] - rows_s[b, 2 + g : 3 + g, :])).astype(jnp.bfloat16)
            )
        keyval_sum[key_rows, :] += dot_nn(
            jnp.concatenate(score_low + shares_low, axis=1), stack_s[stack_rows, :]
        )
        query_sum[b] += dot_nn(turned_s[j], jnp.concatenate(score_low, axis=0))
    for b in range(2):
        context_s[b * block : (b + 1) * block, :] = query_sum[b].T * scale
    for s, cr, slot, row in places:
        query_out[cr, s, 0] = context_s[at_row(slot * block + row), :]
    weights = jnp.where(lane_index((piece, lanes)) < head_dim, scale, 1.0)
    for u, out_ref in enumerate((own_out, one_out, two_out, three_out)):
        for s, cr, slot, row in places:
            found = keyval_sum[at_row(meta_ref[2 * u + slot] * block + row), :] * weights
            out_ref[cr, s, 0] = found.astype(out_ref.dtype)


near_x = ((0, 3, 1, 2), (0, 1, 3, 2))
near_z = ((0, 3), (1, 2))
part_rows = 32
chunk = 384


def feed_back_kernel(
    rank_ref, two_ref, cot_ref, gate_ref, upper_ref, hidden_ref, weight_ref, other_ref, mine_ref, part_ref,
    turned_s, left_s, sum_s,
):
    step = pl.program_id(0)
    last = pl.num_programs(0) - 1
    first_down = pl.num_programs(0) * 2 // 3
    half = mine_ref.shape[0]

    @pl.when(step == 0)
    def _():
        for k, ref in enumerate((two_ref, cot_ref)):
            turned_s[...] = ref[...].T
            place = 0
            for c in range(2):
                for h in range(2):
                    for x in near_x[h]:
                        for z in near_z[h]:
                            found = (
                                lax.bitwise_xor(rank_ref[0], x) * 4
                                + lax.bitwise_xor(rank_ref[1], z)
                            ) * 2 + lax.bitwise_xor(rank_ref[2], c)
                            start = pl.multiple_of(found * part_rows, part_rows)
                            left_s[k, place : place + part_rows, :] = turned_s[
                                pl.ds(start, part_rows), :
                            ]
                            place += part_rows
        sum_s[...] = jnp.zeros(sum_s.shape, jnp.float32)

    def product(k, values):
        mine_ref[...] = dot_nn(left_s[k, :half, :], values).astype(jnp.bfloat16)
        other_ref[...] = dot_nn(left_s[k, half:, :], values).astype(jnp.bfloat16)

    @pl.when(step < first_down // 2)
    def _():
        product(0, gate_ref[...])

    @pl.when((step >= first_down // 2) & (step < first_down))
    def _():
        product(0, upper_ref[...])

    @pl.when(step >= first_down)
    def _():
        hidden = hidden_ref[...]
        product(1, hidden)
        sum_s[...] += dot_nt(hidden, weight_ref[...])

    @pl.when(step == last)
    def _():
        rows = part_ref.shape[1]
        for s in range(4):
            part_ref[lax.bitwise_xor(rank_ref[3], s)] = sum_s[
                s * rows : (s + 1) * rows, :
            ].astype(jnp.bfloat16)


def feed_back_step(ranks, two, cotangent, gate, upper, hidden, weights):
    tokens, width = two.shape
    columns = weights.shape[1]
    steps = columns // chunk
    first_down = steps * 2 // 3
    third = first_down // 2
    half = width // 2

    def down_at(j):
        return jnp.maximum(j - first_down, 0)

    return pl.pallas_call(
        feed_back_kernel,
        grid=(steps,),
        in_specs=[
            in_scalars,
            whole((tokens, width)),
            whole((tokens, width)),
            pl.BlockSpec((tokens, chunk), lambda j: (0, jnp.minimum(j, third - 1))),
            pl.BlockSpec((tokens, chunk), lambda j: (0, jnp.clip(j - third, 0, third - 1))),
            pl.BlockSpec((tokens, chunk), lambda j: (0, down_at(j))),
            pl.BlockSpec((width, chunk), lambda j: (0, first_down + down_at(j))),
        ],
        out_specs=[
            pl.BlockSpec((half, chunk), lambda j: (0, j)),
            pl.BlockSpec((half, chunk), lambda j: (0, j)),
            whole((4, tokens // 4, width)),
        ],
        out_shape=[
            jax.ShapeDtypeStruct((half, columns), jnp.bfloat16),
            jax.ShapeDtypeStruct((half, columns), jnp.bfloat16),
            jax.ShapeDtypeStruct((4, tokens // 4, width), jnp.bfloat16),
        ],
        scratch_shapes=[
            pltpu.VMEM((width, tokens), jnp.bfloat16),
            pltpu.VMEM((2, width, tokens), jnp.bfloat16),
            pltpu.VMEM((tokens, width), jnp.float32),
        ],
        compiler_params=pltpu.CompilerParams(vmem_limit_bytes=56 * 2**20),
        cost_estimate=pl.CostEstimate(flops=10**8, bytes_accessed=10**5, transcendentals=0),
        name="feed_back_step",
    )(ranks, two, cotangent, gate, upper, hidden, weights)


def head_weight(refs, s, hr):
    return refs[s][...] if hr == 0 else refs[4][s]


def feature_block(rank, s, width):
    start = lax.bitwise_xor(rank, s) * (width // 4)
    return pl.ds(pl.multiple_of(start, width // 4), width // 4)


def branch_kernel(
    rank_ref, hidden_ref, gain_ref, own_ref, one_ref, two_ref, three_ref, w_own, w_one, w_two,
    w_three, w_swap, middle_ref, normed_ref,
):
    weights = (w_own, w_one, w_two, w_three, w_swap)
    width = hidden_ref.shape[1]
    branch = None
    for s, context_ref in enumerate((own_ref, one_ref, two_ref, three_ref)):
        for hr in range(2):
            context = context_ref[:, hr * lanes : (hr + 1) * lanes]
            part = dot_nt(context, head_weight(weights, s, hr))
            branch = part if branch is None else branch + part
    for s in range(4):
        at = feature_block(rank_ref[0], s, width)
        middle_ref[:, at] = (
            hidden_ref[:, at].astype(jnp.float32)
            + branch[:, s * (width // 4) : (s + 1) * (width // 4)]
        )
    middle = middle_ref[...]
    scale = lax.rsqrt(jnp.mean(middle * middle, axis=-1, keepdims=True) + eps_norm)
    normed_ref[...] = (middle * scale * gain_ref[...]).astype(jnp.bfloat16)


def branch_back_kernel(
    rank_ref, in_own, in_one, in_two, in_three, middle_ref, cot_ref, gain_ref, w_own, w_one, w_two,
    w_three, w_swap, grad_ref, low_ref, terms_ref, own_ref, one_ref, two_ref, three_ref,
):
    weights = (w_own, w_one, w_two, w_three, w_swap)
    parts = [ref[...].astype(jnp.float32) for ref in (in_own, in_one, in_two, in_three)]
    grads = (parts[0] + parts[2]) + (parts[1] + parts[3])
    middle = middle_ref[...]
    scale = lax.rsqrt(jnp.mean(middle * middle, axis=-1, keepdims=True) + eps_norm)
    back, terms = norm_back(middle, scale, gain_ref[...], grads)
    back = cot_ref[...].astype(jnp.float32) + back
    low = back.astype(jnp.bfloat16)
    grad_ref[...] = back
    low_ref[...] = low
    terms_ref[...] = jnp.sum(terms, axis=0, keepdims=True)
    width = low_ref.shape[1]
    low = jnp.concatenate(
        [low_ref[:, feature_block(rank_ref[0], s, width)] for s in range(4)], axis=1
    )
    for s, out_ref in enumerate((own_ref, one_ref, two_ref, three_ref)):
        for hr in range(2):
            out_ref[:, hr * lanes : (hr + 1) * lanes] = dot_nn(
                low, head_weight(weights, s, hr)
            ).astype(jnp.bfloat16)


gain_rows = 32


def send_pieces(rank, rows, pick, gains, out_refs):
    high = gains.astype(jnp.bfloat16)
    rest = (gains - high.astype(jnp.float32)).astype(jnp.bfloat16)
    for s, out_ref in enumerate(out_refs):
        start = pl.multiple_of(lax.bitwise_xor(rank, s) * rows, rows)
        for k in range(3):
            out_ref[k * rows : (k + 1) * rows, :] = pick(k, start).astype(out_ref.dtype)
        out_ref[3 * rows : 3 * rows + gain_rows, :] = high.astype(out_ref.dtype)
        out_ref[3 * rows + gain_rows :, :] = rest.astype(out_ref.dtype)


def sum_refs(refs, rows):
    parts = [ref[rows, :].astype(jnp.float32) for ref in refs]
    return (parts[0] + parts[2]) + (parts[1] + parts[3])


def first_stage_kernel(
    rank_ref, qkv_ref, output_ref, weight_ref, gain_ref, ffn_ref, head_ref,
    own_ref, one_ref, two_ref, three_ref, gain_s,
):
    products = qkv_ref[...] * weight_ref[...].astype(jnp.float32)
    ones = jnp.ones((8, products.shape[1]), jnp.float32)
    attn = lax.dot_general(
        ones,
        products,
        (((1,), (1,)), ((), ())),
        precision=lax.Precision.HIGHEST,
        preferred_element_type=jnp.float32,
    )[0:1, :] / gain_ref[...]
    ffn = ffn_ref[...]
    head = jnp.sum(head_ref[...], axis=0, keepdims=True)
    gain_s[...] = jnp.zeros(gain_s.shape, jnp.float32)
    count = attn.shape[1] // lanes
    for i in range(count):
        gain_s[i : i + 1, :] = attn[:, i * lanes : (i + 1) * lanes]
        gain_s[count + i : count + i + 1, :] = ffn[:, i * lanes : (i + 1) * lanes]
    gain_s[2 * count : 2 * count + 1, :] = head[:, :lanes]
    gain_s[2 * count + 1 : 2 * count + 2, :] = head[:, lanes:]
    rows = qkv_ref.shape[0] // 4

    def pick(k, start):
        if k == 2:
            return output_ref[pl.ds(start, rows), :]
        return qkv_ref[pl.ds(start, rows), k * lanes : (k + 1) * lanes]

    send_pieces(rank_ref[0], rows, pick, gain_s[...], (own_ref, one_ref, two_ref, three_ref))


def second_stage_kernel(
    rank_ref, in_own, in_one, in_two, in_three, own_ref, one_ref, two_ref, three_ref, sum_s,
):
    refs = (in_own, in_one, in_two, in_three)
    count = sum_s.shape[0]
    sum_s[...] = sum_refs(refs, slice(0, count))
    gains = sum_refs(refs, slice(count, count + gain_rows)) + sum_refs(
        refs, slice(count + gain_rows, count + 2 * gain_rows)
    )
    rows = count // 12

    def pick(k, start):
        return sum_s[pl.ds(pl.multiple_of(k * (4 * rows) + start, rows), rows), :]

    send_pieces(rank_ref[0], rows, pick, gains, (own_ref, one_ref, two_ref, three_ref))


def third_stage_kernel(
    in_own, in_one, in_two, in_three, query_ref, keyval_ref, output_ref, gain_ref,
):
    refs = (in_own, in_one, in_two, in_three)
    rows = query_ref.shape[0]
    for k, out_ref in enumerate((query_ref, keyval_ref, output_ref)):
        out_ref[...] = sum_refs(refs, slice(k * rows, (k + 1) * rows))
    gain_ref[...] = sum_refs(refs, slice(3 * rows, 3 * rows + gain_rows)) + sum_refs(
        refs, slice(3 * rows + gain_rows, 3 * rows + 2 * gain_rows)
    )


def blocks_of(arrays):
    return [whole(array.shape) for array in arrays]


def piece_shapes(rows):
    shape = (3 * rows + 2 * gain_rows, lanes)
    return [jax.ShapeDtypeStruct(shape, jnp.float32)] + [
        jax.ShapeDtypeStruct(shape, jnp.bfloat16)
    ] * 3


def branch_step(rank, hidden, gain, contexts, weights):
    rows, width = hidden.shape
    operands = (hidden, gain, *contexts, *weights)
    shapes = [
        jax.ShapeDtypeStruct((rows, width), jnp.float32),
        jax.ShapeDtypeStruct((rows, width), jnp.bfloat16),
    ]
    return pl.pallas_call(
        branch_kernel,
        grid=(1,),
        in_specs=[in_scalars] + blocks_of(operands),
        out_specs=blocks_of(shapes),
        out_shape=shapes,
        compiler_params=pltpu.CompilerParams(vmem_limit_bytes=24 * 2**20),
        cost_estimate=pl.CostEstimate(
            flops=3 * 10**8, bytes_accessed=4 * 10**6, transcendentals=0
        ),
        name="branch_step",
    )(rank[None].astype(jnp.int32), *operands)


def branch_back_step(rank, parts, middle, cotangent, gain, weights):
    rows, width = middle.shape
    operands = (*parts, middle, cotangent, gain, *weights)
    shapes = [
        jax.ShapeDtypeStruct((rows, width), jnp.float32),
        jax.ShapeDtypeStruct((rows, width), jnp.bfloat16),
        jax.ShapeDtypeStruct((1, width), jnp.float32),
    ] + [jax.ShapeDtypeStruct((rows, 2 * lanes), jnp.bfloat16)] * 4
    return pl.pallas_call(
        branch_back_kernel,
        grid=(1,),
        in_specs=[in_scalars] + blocks_of(operands),
        out_specs=blocks_of(shapes),
        out_shape=shapes,
        compiler_params=pltpu.CompilerParams(vmem_limit_bytes=56 * 2**20),
        cost_estimate=pl.CostEstimate(
            flops=3 * 10**8, bytes_accessed=5 * 10**6, transcendentals=0
        ),
        name="branch_back_step",
    )(rank[None].astype(jnp.int32), *operands)


def first_stage(rank, qkv_grad, output_grad, weight, gain, ffn, head):
    operands = (qkv_grad, output_grad, weight, gain, ffn, head)
    shapes = piece_shapes(qkv_grad.shape[0] // 4)
    return pl.pallas_call(
        first_stage_kernel,
        grid=(1,),
        in_specs=[in_scalars] + blocks_of(operands),
        out_specs=blocks_of(shapes),
        out_shape=shapes,
        scratch_shapes=[pltpu.VMEM((gain_rows, lanes), jnp.float32)],
        compiler_params=pltpu.CompilerParams(vmem_limit_bytes=24 * 2**20),
        cost_estimate=pl.CostEstimate(flops=10**7, bytes_accessed=3 * 10**6, transcendentals=0),
        name="first_stage",
    )(rank[None].astype(jnp.int32), *operands)


def second_stage(rank, parts):
    count = parts[0].shape[0] - 2 * gain_rows
    operands = tuple(parts)
    shapes = piece_shapes(count // 12)
    return pl.pallas_call(
        second_stage_kernel,
        grid=(1,),
        in_specs=[in_scalars] + blocks_of(operands),
        out_specs=blocks_of(shapes),
        out_shape=shapes,
        scratch_shapes=[pltpu.VMEM((count, lanes), jnp.float32)],
        compiler_params=pltpu.CompilerParams(vmem_limit_bytes=24 * 2**20),
        cost_estimate=pl.CostEstimate(flops=10**6, bytes_accessed=10**6, transcendentals=0),
        name="second_stage",
    )(rank[None].astype(jnp.int32), *operands)


def third_stage(parts):
    rows = (parts[0].shape[0] - 2 * gain_rows) // 3
    operands = tuple(parts)
    shapes = [jax.ShapeDtypeStruct((rows, lanes), jnp.float32)] * 3 + [
        jax.ShapeDtypeStruct((gain_rows, lanes), jnp.float32)
    ]
    return pl.pallas_call(
        third_stage_kernel,
        grid=(1,),
        in_specs=blocks_of(operands),
        out_specs=blocks_of(shapes),
        out_shape=shapes,
        compiler_params=pltpu.CompilerParams(vmem_limit_bytes=24 * 2**20),
        cost_estimate=pl.CostEstimate(flops=10**6, bytes_accessed=10**6, transcendentals=0),
        name="third_stage",
    )(*operands)


def by_sequence(width):
    return pl.BlockSpec((2, 4, 1, piece, width), lambda s: (0, 0, s, 0, 0))


def whole(shape):
    return pl.BlockSpec(shape, lambda s: (0,) * len(shape))


in_scalars = pl.BlockSpec(memory_space=pltpu.SMEM)


def five(width, dtype, sequences):
    return jax.ShapeDtypeStruct((2, 4, sequences, piece, width), dtype)


def project(rank, own, swapped, weights, gain, cosine, sine):
    sequences, width = own.shape[1], own.shape[3]
    operands = (*weights, gain, cosine, sine)
    rows_spec = pl.BlockSpec((4, 1, piece, width), lambda s: (0, s, 0, 0))
    return pl.pallas_call(
        project_kernel,
        grid=(sequences,),
        in_specs=[in_scalars, rows_spec, rows_spec] + blocks_of(operands),
        out_specs=[by_sequence(2 * lanes), by_sequence(lanes), by_sequence(lanes)],
        out_shape=[five(2 * lanes, jnp.float32, sequences)]
        + [five(lanes, jnp.bfloat16, sequences)] * 2,
        compiler_params=pltpu.CompilerParams(vmem_limit_bytes=56 * 2**20),
        cost_estimate=pl.CostEstimate(flops=10**8, bytes_accessed=2 * 10**6, transcendentals=0),
        name="project",
    )(rank[None].astype(jnp.int32), own, swapped, *operands)


def finish(raw, gain, cosine, sine, query_grad, keyval_parts):
    sequences = raw.shape[2]
    rows = cosine.shape[0]
    return pl.pallas_call(
        finish_kernel,
        grid=(sequences,),
        in_specs=[
            by_sequence(2 * lanes), whole((1, 2 * lanes)), whole((rows, lanes)), whole((rows, lanes)),
        ] + [by_sequence(lanes)] * 5,
        out_specs=[by_sequence(2 * lanes), whole((8, 2 * lanes))],
        out_shape=[
            five(2 * lanes, jnp.bfloat16, sequences),
            jax.ShapeDtypeStruct((8, 2 * lanes), jnp.float32),
        ],
        compiler_params=pltpu.CompilerParams(vmem_limit_bytes=24 * 2**20),
        cost_estimate=pl.CostEstimate(flops=10**8, bytes_accessed=4 * 10**6, transcendentals=0),
        name="finish",
    )(raw, gain, cosine, sine, query_grad, *keyval_parts)


def attend(meta, query, keyval_parts, scale):
    sequences = query.shape[2]
    keys = 4 * 8 * piece
    return pl.pallas_call(
        functools.partial(attend_kernel, scale * log2_e),
        grid=(sequences,),
        in_specs=[in_scalars] + [by_sequence(lanes)] * 5,
        out_specs=[by_sequence(lanes)] * 3
        + [pl.BlockSpec((8, 1, piece, lanes), lambda s: (0, s, 0, 0))],
        out_shape=[
            five(lanes, jnp.float32, sequences),
            five(lanes, jnp.bfloat16, sequences),
            five(lanes, jnp.float32, sequences),
            jax.ShapeDtypeStruct((8, sequences, piece, lanes), jnp.bfloat16),
        ],
        scratch_shapes=[
            pltpu.VMEM((2 * block, lanes), jnp.bfloat16),
            pltpu.VMEM((2 * keys, lanes), jnp.bfloat16),
            pltpu.VMEM((2 * keys, 2 * lanes), jnp.bfloat16),
            pltpu.VMEM((2 * block, 2 * lanes), jnp.float32),
        ],
        compiler_params=pltpu.CompilerParams(vmem_limit_bytes=24 * 2**20),
        cost_estimate=pl.CostEstimate(
            flops=2 * 10**9, bytes_accessed=4 * 10**6, transcendentals=2 * 10**6
        ),
        name="attend",
    )(meta, query, *keyval_parts)


def attend_back(meta, query, keyval_parts, context, total, grads, scale):
    sequences = query.shape[2]
    keys = 4 * 8 * piece
    blocks = keys // block
    return pl.pallas_call(
        functools.partial(attend_back_kernel, scale * log2_e, scale),
        grid=(sequences,),
        in_specs=[in_scalars] + [by_sequence(lanes)] * 8,
        out_specs=[by_sequence(lanes)] * 5,
        out_shape=[five(lanes, jnp.float32, sequences)] * 2
        + [five(lanes, jnp.bfloat16, sequences)] * 3,
        scratch_shapes=[
            pltpu.VMEM((2 * block, lanes), jnp.bfloat16),
            pltpu.VMEM((2 * block, lanes), jnp.bfloat16),
            pltpu.VMEM((2 * block, lanes), jnp.float32),
            pltpu.VMEM((2 * block, lanes), jnp.float32),
            pltpu.VMEM((8 * block, lanes), jnp.bfloat16),
            pltpu.VMEM((2 * keys, lanes), jnp.bfloat16),
            pltpu.VMEM((2 * keys, lanes), jnp.bfloat16),
            pltpu.VMEM((blocks, lanes, 2 * block), jnp.bfloat16),
            pltpu.VMEM((2, 8, block), jnp.float32),
            pltpu.VMEM((2, lanes, block), jnp.float32),
            pltpu.VMEM((keys, lanes), jnp.float32),
        ],
        compiler_params=pltpu.CompilerParams(vmem_limit_bytes=56 * 2**20),
        cost_estimate=pl.CostEstimate(
            flops=5 * 10**9, bytes_accessed=8 * 10**6, transcendentals=2 * 10**6
        ),
        name="attend_back",
    )(meta, query, *keyval_parts, context, total, grads)


def body(
    hidden_in,
    cotangent,
    block_order,
    query_weight,
    keyval_weight,
    output_weight,
    gate_weight,
    up_weight,
    down_weight,
    attn_gain,
    ffn_gain,
    query_gain,
    key_gain,
):
    sequences, _, own_rows, width = hidden_in.shape
    tensor_size = lax.axis_size("tensor")
    heads_size = lax.axis_size("heads")
    chips = heads_size // 2
    shard_rows = own_rows * heads_size
    all_rows = sequences * shard_rows
    units = gate_weight.shape[1]
    query_width = query_weight.shape[2]
    scale = head_dim ** (-0.5)
    rank = lax.axis_index("tensor")
    head_rank = lax.axis_index("heads")
    chip = head_rank // 2
    core = lax.rem(head_rank, 2)
    hidden_own = hidden_in[:, 0]
    cot_own = cotangent[:, 0]
    folded = (2, chips, sequences, own_rows)

    barrier = lax.optimization_barrier
    own_tokens = sequences * own_rows

    attn_own = jnp.concatenate(
        [query_weight[:, 0], keyval_weight[:, 0], output_weight[:, 0]], axis=1
    )
    attn_ring = gather_ring(attn_own, "tensor")
    inputs = hidden_own.astype(jnp.float32)
    scale_one = rms_scale(inputs)
    normed_one = (inputs * scale_one * attn_gain).astype(jnp.bfloat16)
    attn_ring[1], normed_one = barrier((attn_ring[1], normed_one))
    attn_y = place_ring(attn_ring, "tensor")
    attn_y, cot_own, block_order = barrier((attn_y, cot_own, block_order))
    attn_ring = gather_ring(attn_y, "fsdp")

    chip_at = chip ^ jnp.arange(chips, dtype=jnp.int32)
    core_at = lax.rem(core + jnp.arange(2, dtype=jnp.int32), 2)
    head_at = chip_at[None, :] * 2 + core_at[:, None]
    row_at = (head_at[:, :, None] * own_rows + jnp.arange(own_rows, dtype=jnp.int32)).reshape(
        shard_rows
    )
    rank_at = rank ^ jnp.arange(tensor_size, dtype=jnp.int32)
    order_at = block_order[rank_at]
    meta = jnp.concatenate([order_at.reshape(-1), chip[None], core[None]]).astype(jnp.int32)
    positions = (
        jnp.where(row_at >= block, order_at[0, 1], order_at[0, 0]) * block + lax.rem(row_at, block)
    )
    lane = jnp.arange(lanes, dtype=jnp.int32)
    freq = rope_base ** (
        -(lax.rem(lane, head_dim // 2).astype(jnp.float32) * 2.0 / head_dim)
    )
    angles = positions.astype(jnp.float32)[:, None] * freq[None, :]
    cosine = jnp.cos(angles)
    sine = jnp.sin(angles) * jnp.where(lax.rem(lane, head_dim) < head_dim // 2, -1.0, 1.0)[None, :]
    head_gain = jnp.concatenate(
        [query_gain, query_gain, key_gain, jnp.ones((head_dim,), jnp.float32)]
    )[None, :]
    rows_ring, attn_ring, meta, cosine, sine, head_gain = barrier(
        (gather_ring(normed_one, "z"), attn_ring, meta, cosine, sine, head_gain)
    )
    output_all = jnp.stack([part[..., 2 * query_width :] for part in attn_ring])
    output_ring = gather_ring(output_all.reshape(width, query_width), "z")
    rows_own = jnp.stack(rows_ring)
    rows_swap = swap_core(rows_own)
    rows_halves = [rows_own.reshape(-1, width), rows_swap.reshape(-1, width)]

    feed_own = jnp.concatenate([gate_weight, up_weight, down_weight], axis=1)
    feed_all = lax.all_gather(feed_own, ("fsdp", "heads"), axis=0, tiled=True)
    gate_up_all = feed_all[:, : 2 * units]
    down_all = feed_all[:, 2 * units :]

    x_rank = lax.axis_index("fsdp")
    qkv_raw, query_rot, keyval_rot = project(
        x_rank, rows_own, rows_swap, attn_ring, head_gain, cosine, sine
    )
    attn_ring, keyval_rot = barrier((attn_ring, keyval_rot))
    attn_all = place_ring(attn_ring, "fsdp").reshape(width, 3 * query_width)
    qkv_all = attn_all[:, : 2 * query_width]
    cot_one = exchange(cot_own, "tensor", 1)
    keyval_parts = gather_ring(keyval_rot, "tensor")

    cot_two = jnp.stack([cot_own, cot_one])
    keyval_parts, cot_two, output_ring = barrier((keyval_parts, cot_two, output_ring))
    cot_three = exchange(cot_two, "tensor", 3)

    context, context_low, total, context_placed = attend(meta, query_rot, keyval_parts, scale)
    core_rows = (chips, own_tokens, query_width)
    context_swap = swap_core(context_low[1].reshape(core_rows))
    context_pairs = jnp.concatenate([context_low[0].reshape(core_rows), context_swap], axis=2)
    contexts = scatter_ring([context_pairs[s] for s in range(chips)], "z")
    weights = (*output_ring, swap_core(jnp.stack(output_ring)))
    middle, normed_two = branch_step(
        x_rank,
        hidden_own.reshape(own_tokens, width), ffn_gain[None, :], contexts, weights
    )
    normed_two, cot_three = barrier((normed_two, cot_three))
    two_ring = gather_ring(normed_two, "tensor")
    cot_flat = jnp.stack([cot_two[0], cot_two[1], cot_three[1], cot_three[0]]).reshape(-1, width)
    hidden_grad = matmul(cot_flat, down_all)
    two_ring, hidden_grad = barrier((two_ring, hidden_grad))
    two_flat = jnp.stack(two_ring).reshape(-1, width)
    gate_up = matmul(two_flat, gate_up_all)
    gate_value = gate_up[:, :units]
    upper_value = gate_up[:, units:]
    sigmoid_gate = jax.nn.sigmoid(gate_value)
    activated = gate_value * sigmoid_gate
    hidden = (activated * upper_value).astype(jnp.bfloat16)
    gate_low = (
        hidden_grad * upper_value * sigmoid_gate * (1.0 + gate_value * (1.0 - sigmoid_gate))
    ).astype(jnp.bfloat16)
    upper_low = (hidden_grad * activated).astype(jnp.bfloat16)
    both_low = jnp.concatenate([gate_low, upper_low], axis=1)
    two_part = contract_cols(both_low, gate_up_all).astype(jnp.bfloat16)
    two_moved = scatter_ring(
        [two_part[s * own_tokens : (s + 1) * own_tokens] for s in range(tensor_size)], "tensor"
    )

    eighth = width // 8
    ranks = jnp.stack([x_rank, chip, core, rank]).astype(jnp.int32)
    feed_other, feed_mine, feed_part = feed_back_step(
        ranks, two_flat, cot_flat, gate_low, upper_low, hidden, feed_all
    )
    two_moved, feed_other, feed_mine, feed_part = barrier(
        (two_moved, feed_other, feed_mine, feed_part)
    )
    feed_swap = swap_core(feed_other)
    feed_sums = [
        feed_swap[at : at + eighth] + feed_mine[at : at + eighth] for at in range(0, width // 2, eighth)
    ]

    middle_grad, branch_low, ffn_row, *grad_pairs = branch_back_step(
        x_rank,
        two_moved,
        middle,
        cot_own.reshape(own_tokens, width),
        ffn_gain[None, :],
        weights,
    )
    branch_all = lax.all_gather(branch_low.reshape(sequences, own_rows, width), "heads")
    grad_moved = scatter_ring(grad_pairs, "z")
    grad_moved, feed_sums = barrier((grad_moved, feed_sums))
    sent_a = exchange(feed_sums[1], "fsdp", 1)
    sent_b = exchange(feed_sums[3], "fsdp", 3)
    grad_moved = jnp.stack(grad_moved)
    context_grad = jnp.stack(
        [grad_moved[..., :query_width], swap_core(grad_moved[..., query_width:])]
    ).reshape(folded + (query_width,))
    query_grad, own, one, two, three = attend_back(
        meta, query_rot, keyval_parts, context, total, context_grad, scale
    )
    kv_moved = scatter_ring([own, one, two, three], "tensor")
    kv_moved[1], sent_a, sent_b = barrier((kv_moved[1], sent_a, sent_b))
    row_half = eighth // 2
    kept_a, next_a, kept_b, next_b = [
        kept[at].astype(jnp.float32) + sent[at].astype(jnp.float32)
        for kept, sent in ((feed_sums[0], sent_a), (feed_sums[2], sent_b))
        for at in (slice(0, row_half), slice(row_half, eighth))
    ]
    next_a = next_a.astype(jnp.bfloat16)
    next_b = next_b.astype(jnp.bfloat16)
    output_grad = contract_rows(
        branch_all.reshape(all_rows, width), context_placed.reshape(all_rows, query_width)
    )
    kv_moved, kept_a, next_a, kept_b, next_b, feed_part, output_grad = barrier(
        (kv_moved, kept_a, next_a, kept_b, next_b, feed_part, output_grad)
    )
    feed = lax.psum_scatter(feed_part, "tensor", scatter_dimension=0, tiled=True)
    block_out = (middle + feed[0].astype(jnp.float32)).astype(jnp.bfloat16)
    last_a = exchange(next_a, "fsdp", 3)
    last_b = exchange(next_b, "fsdp", 1)

    qkv_low, head_terms = finish(qkv_raw, head_gain, cosine, sine, query_grad, kv_moved)
    qkv_low = qkv_low.reshape(all_rows, 2 * query_width)
    one_part = contract_cols(qkv_low, qkv_all).astype(jnp.bfloat16)
    one_part, qkv_low = barrier((one_part.reshape(folded + (width,)), qkv_low))
    one_swap = swap_core(one_part[1])
    half_rows = all_rows // 2
    qkv_grad = contract_rows(rows_halves[0], qkv_low[:half_rows]) + contract_rows(
        rows_halves[1], qkv_low[half_rows:]
    )
    attn_pieces = first_stage(
        x_rank, qkv_grad, output_grad, qkv_all, attn_gain[None, :], ffn_row, head_terms
    )
    one_sum = one_part[0].astype(jnp.float32) + one_swap.astype(jnp.float32)
    attn_pieces, one_sum = barrier((attn_pieces, one_sum))
    one_sent = exchange(jnp.stack([one_sum[1], one_sum[2]]).astype(jnp.bfloat16), "z", 1)
    attn_moved = scatter_ring(attn_pieces, "fsdp")
    attn_pieces = second_stage(rank, attn_moved)
    attn_moved = scatter_ring(attn_pieces, "tensor")
    attn_moved, one_sent, last_a, last_b, block_out = barrier(
        (attn_moved, one_sent, last_a, last_b, block_out)
    )
    query_out, keyval_out, output_out, gains = third_stage(attn_moved)
    gains = gains + swap_core(gains)
    one_far = (one_sum[3] + one_sent[1].astype(jnp.float32)).astype(jnp.bfloat16)
    one_far = exchange(one_far, "z", 3)
    z_sent = (kept_b + last_b.astype(jnp.float32)).astype(jnp.bfloat16)
    z_sent = exchange(z_sent, "z", 1)
    gains = gains + exchange(gains, "z", 1)
    gains, one_far, z_sent = barrier((gains, one_far, z_sent))
    z_sum = (
        kept_a + last_a.astype(jnp.float32) + z_sent.astype(jnp.float32)
    )
    z_last = exchange(z_sum[part_rows:].astype(jnp.bfloat16), "z", 3)
    gains = gains + exchange(gains, "z", 3)
    feed_grad = z_sum[:part_rows] + z_last.astype(jnp.float32)
    normed_one_grad = one_sum[0] + one_sent[0].astype(jnp.float32) + one_far.astype(jnp.float32)
    input_norm_grad, _ = norm_back(inputs, scale_one, attn_gain, normed_one_grad)
    input_grad = middle_grad.reshape(inputs.shape) + input_norm_grad
    gain_at = width // lanes
    return (
        block_out.reshape(hidden_in.shape),
        input_grad[:, None],
        query_out[:, None],
        keyval_out[:, None],
        output_out[:, None],
        feed_grad[:, :units],
        feed_grad[:, units : 2 * units],
        feed_grad[:, 2 * units :],
        gains[:gain_at].reshape(width),
        gains[gain_at : 2 * gain_at].reshape(width),
        gains[2 * gain_at, :head_dim] + gains[2 * gain_at, head_dim:],
        gains[2 * gain_at + 1, :head_dim],
    )


def solution(mesh):
    placed = (
        P("fsdp", "tensor", "heads", None),
        P("fsdp", "tensor", "heads", None),
        P(),
        P(("fsdp", "tensor"), "heads", None),
        P(("fsdp", "tensor"), "heads", None),
        P(("fsdp", "tensor"), "heads", None),
        P(("fsdp", "heads"), "tensor"),
        P(("fsdp", "heads"), "tensor"),
        P(("fsdp", "heads"), "tensor"),
        P(),
        P(),
        P(),
        P(),
    )
    return jax.shard_map(
        body,
        mesh=mesh,
        in_specs=placed,
        out_specs=(
            P("fsdp", "tensor", "heads", None),
            P("fsdp", "tensor", "heads", None),
            P(("fsdp", "tensor"), "heads", None),
            P(("fsdp", "tensor"), "heads", None),
            P(("fsdp", "tensor"), "heads", None),
            P(("fsdp", "heads"), "tensor"),
            P(("fsdp", "heads"), "tensor"),
            P(("fsdp", "heads"), "tensor"),
            P(),
            P(),
            P(),
            P(),
        ),
        check_vma=False,
    )
```
